256 devices in a mesh: ctx: 32 (over y, x, core), head: 8 (over z).
Axes of the slice: x: 4, y: 4, z: 8, core: 2. Of those that a mesh axis runs over, the one named last changes fastest.
Arguments:
- queries: bfloat16 [16384, 64, 128], P('ctx', 'head'), may hold values from -6 to 6
- key_rows: bfloat16 [16384, 64, 128], P('ctx', 'head'), may hold values from -2 to 2
- value_rows: bfloat16 [16384, 64, 128], P('ctx', 'head'), may hold values from -21 to 21
- upstream: bfloat16 [16384, 64, 128], P('ctx', 'head'), may hold values from -6 to 6
- norm_gain: float32 [64, 128], P('head'), may hold values from 0.1 to 1.9
- slope_index: int32 [64], P('head'), may hold values from 0 to 63
Outputs:
- grad_query: bfloat16 [16384, 64, 128], P('ctx', 'head')
- grad_key: bfloat16 [16384, 64, 128], P('ctx', 'head')
- grad_value: bfloat16 [16384, 64, 128], P('ctx', 'head')
The draws below stay inside these ranges and needn't reach their ends.
All inputs are finite; a program needn't handle non-finite values.
Results may differ from the reference program's by a relative error of at most 0.0064.
Values sent between devices are 32-bit elements; how exact they have to be, the bound alone decides.
No kernel may reach another device: no remote copies, remote signals or barrier semaphores. Data moves between devices by JAX's collectives and lax.ppermute only.
A program may use at most 128 MiB of HBM per device.

```python
import jax
import jax.numpy as jnp
from jax import lax

HD = 128
L_DEV = 512
HEADS = 64
SEQ = 16384
N_CTX = 32


def block_level(key):
    blocks = SEQ // L_DEV
    lift = jax.random.uniform(jax.random.fold_in(key, 101), (blocks,), jnp.float32, -3.0, 0.0)
    return jnp.repeat(jnp.exp(lift), L_DEV)[:, None, None]


def draw_key_rows(key, part):
    level = block_level(key)
    key = jax.random.fold_in(key, 13)
    base = jnp.clip(jax.random.normal(key, (SEQ, HEADS, HD), jnp.float32), -6.0, 6.0)
    return (base * HD ** (-0.5) * level).astype(jnp.bfloat16)


def draw_value_rows(key, part):
    level = block_level(key)
    key = jax.random.fold_in(key, 11)
    head_scale = 3.0 ** (jnp.arange(HEADS).astype(jnp.float32) / (HEADS - 1))
    base = jnp.clip(jax.random.normal(key, (SEQ, HEADS, HD), jnp.float32), -6.0, 6.0)
    return (base * 0.6 * head_scale[None, :, None] * level).astype(jnp.bfloat16)


def draw_upstream(key, part):
    key = jax.random.fold_in(key, 17)
    level = block_level(jax.random.fold_in(key, 3))
    base = jnp.clip(jax.random.normal(key, (SEQ, HEADS, HD), jnp.float32), -6.0, 6.0)
    return (base * level).astype(jnp.bfloat16)


def draw_slope_index(key, part):
    key = jax.random.fold_in(key, 5)
    broad = jax.random.randint(key, (HEADS,), 0, 64)
    slow = 63 - jax.random.randint(jax.random.fold_in(key, 2), (HEADS,), 0, 12)
    order = jax.random.permutation(jax.random.fold_in(key, 1), HEADS)
    rank = jnp.zeros((HEADS,), jnp.int32).at[order].set(jnp.arange(HEADS).astype(jnp.int32))
    chosen = jnp.where(rank % 2 == 0, slow, broad)
    chosen = chosen.at[order[0]].set(63)
    chosen = chosen.at[order[1]].set(0)
    return chosen.astype(jnp.int32)


def levels(key, shape, shards, smallest, high):
    def one(dim, blocks):
        steps = jax.random.uniform(jax.random.fold_in(jax.random.fold_in(key, 6), dim), (blocks,), jnp.float32, smallest / len(shards), high / len(shards))
        return jnp.repeat(jnp.exp(steps), shape[dim] // blocks).reshape((-1,) + (1,) * (len(shape) - dim - 1))

    loudness = one(*shards[0])
    for cut in shards[1:]:
        loudness = loudness * one(*cut)
    return loudness


def centred(rng, dims, width, reach, pieces=(), kind=jnp.bfloat16):
    loudness = levels(rng, dims, pieces, -0.22, 0.18) if pieces else 1.0
    result = jax.random.normal(rng, dims, jnp.float32) * width * loudness
    return jnp.minimum(jnp.maximum(result, -reach), reach).astype(kind)


def setup_inputs(seed: int = 0) -> dict:
    key_list = jax.random.split(jax.random.key(seed), 7)
    queries = centred(key_list[0], (SEQ, HEADS, HD), 1.0, 6.0, ((0, 32), (1, 8)))
    key_rows = draw_key_rows(jax.random.fold_in(key_list[6], 71), 0)
    value_rows = draw_value_rows(jax.random.fold_in(key_list[6], 71), 0)
    upstream = draw_upstream(jax.random.fold_in(key_list[6], 71), 0)
    norm_gain = jnp.clip(1.0 + 0.18 * jax.random.normal(key_list[4], (HEADS, HD), jnp.float32), 0.1, 1.9)
    slope_index = draw_slope_index(jax.random.fold_in(key_list[6], 71), 0)
    return dict(queries=queries, key_rows=key_rows, value_rows=value_rows, upstream=upstream, norm_gain=norm_gain, slope_index=slope_index)


def decay_tables(slope_index):
    layer_factor = 1.0 - 78.0 / 79.0 + 1e-05
    decay_rate = 2.0 ** (-8.0 * (slope_index.astype(jnp.float32) + 1.0) / 64.0) * layer_factor
    position = jnp.arange(L_DEV).astype(jnp.float32)
    row_pos = position[:, None]
    col_pos = position[None, :]
    distance = jnp.maximum(row_pos - col_pos, 0.0)
    decay_mask = jnp.where(row_pos >= col_pos, jnp.exp(-decay_rate[:, None, None] * distance), 0.0)
    decay_in = jnp.exp(-decay_rate[None, :] * (position[:, None] + 1.0))
    decay_first = jnp.exp(-decay_rate[None, :] * position[:, None])
    decay_last = jnp.exp(-decay_rate[None, :] * (L_DEV - 1.0 - position[:, None]))
    decay_back = jnp.exp(-decay_rate[None, :] * (L_DEV - position[:, None]))
    block_decay = jnp.exp(-decay_rate * L_DEV)
    return (decay_mask, decay_in, decay_first, decay_last, decay_back, block_decay)

def reference(queries, key_rows, value_rows, upstream, norm_gain, slope_index):
    decay_mask, decay_in, decay_first, decay_last, decay_back, block_decay = decay_tables(slope_index)
    shaped = (N_CTX, L_DEV, HEADS, HD)
    q_blocks = queries.reshape(shaped)
    k_blocks = key_rows.reshape(shaped)
    v_blocks = value_rows.reshape(shaped)
    u_blocks = upstream.reshape(shaped)
    features = HEADS * HD

    def key_state_of(pair):
        keys_here, values_here = pair
        weighted = (keys_here.astype(jnp.float32) * decay_last[:, :, None]).astype(jnp.bfloat16)
        return jnp.einsum('jhd,jhe->hde', weighted.astype(jnp.float32), values_here.astype(jnp.float32))
    key_states = lax.map(key_state_of, (k_blocks, v_blocks))

    def advance(state, incoming):
        return (block_decay[:, None, None] * state + incoming, state)
    empty = jnp.zeros((HEADS, HD, HD), jnp.float32)
    _, entering = lax.scan(advance, empty, key_states)

    def attention(queries_here, keys_here):
        scores = jnp.einsum('ihd,jhd->hij', queries_here.astype(jnp.float32), keys_here.astype(jnp.float32))
        return (scores * decay_mask).astype(jnp.bfloat16)

    def first_pass(group):
        queries_here, keys_here, values_here, upstream_here, enter_here = group
        enter_b = enter_here.astype(jnp.bfloat16).astype(jnp.float32)
        attn_b = attention(queries_here, keys_here).astype(jnp.float32)
        local_part = jnp.einsum('hij,jhd->ihd', attn_b, values_here.astype(jnp.float32))
        carried = jnp.einsum('ihd,hde->ihe', queries_here.astype(jnp.float32), enter_b)
        output = local_part + decay_in[:, :, None] * carried
        scaled_up = norm_gain[None] * upstream_here.astype(jnp.float32)
        total_sq = lax.optimization_barrier(jnp.sum(output * output, axis=(1, 2)))
        total_dot = lax.optimization_barrier(jnp.sum(output * scaled_up, axis=(1, 2)))
        inv_rms = lax.rsqrt(total_sq / features + 1e-06)
        grad_out = inv_rms[:, None, None] * scaled_up - output * (inv_rms ** 3 * total_dot / features)[:, None, None]
        grad_out = grad_out.astype(jnp.bfloat16)
        weighted_q = (queries_here.astype(jnp.float32) * decay_first[:, :, None]).astype(jnp.bfloat16)
        query_state = jnp.einsum('ihd,ihe->hde', weighted_q.astype(jnp.float32), grad_out.astype(jnp.float32))
        return (grad_out, query_state)
    grad_outs, query_states = lax.map(first_pass, (q_blocks, k_blocks, v_blocks, u_blocks, entering))
    _, leaving = lax.scan(advance, empty, query_states, reverse=True)

    def second_pass(group):
        queries_here, keys_here, values_here, grad_here, enter_here, leave_here = group
        enter_b = enter_here.astype(jnp.bfloat16).astype(jnp.float32)
        leave_b = leave_here.astype(jnp.bfloat16).astype(jnp.float32)
        q_full = queries_here.astype(jnp.float32)
        k_full = keys_here.astype(jnp.float32)
        v_full = values_here.astype(jnp.float32)
        g_full = grad_here.astype(jnp.float32)
        attn_b = attention(queries_here, keys_here).astype(jnp.float32)
        back_scores = jnp.einsum('ihe,jhe->hij', g_full, v_full)
        back_b = (back_scores * decay_mask).astype(jnp.bfloat16).astype(jnp.float32)
        grad_q = jnp.einsum('hij,jhd->ihd', back_b, k_full) + decay_in[:, :, None] * jnp.einsum('ihe,hde->ihd', g_full, enter_b)
        grad_k = jnp.einsum('hij,ihd->jhd', back_b, q_full) + decay_back[:, :, None] * jnp.einsum('jhe,hde->jhd', v_full, leave_b)
        grad_v = jnp.einsum('hij,ihe->jhe', attn_b, g_full) + decay_back[:, :, None] * jnp.einsum('jhd,hde->jhe', k_full, leave_b)
        return (grad_q.astype(jnp.bfloat16), grad_k.astype(jnp.bfloat16), grad_v.astype(jnp.bfloat16))
    grad_q, grad_k, grad_v = lax.map(second_pass, (q_blocks, k_blocks, v_blocks, grad_outs, entering, leaving))
    whole = (SEQ, HEADS, HD)
    return (grad_q.reshape(whole), grad_k.reshape(whole), grad_v.reshape(whole))
```

```python
import functools
import math

import jax
import jax.numpy as jnp
from jax import lax
from jax.experimental import pallas as pl
from jax.experimental.pallas import tpu as pltpu
from jax.sharding import PartitionSpec as P

F32 = jnp.float32
BF16 = jnp.bfloat16
LAYER_FACTOR = 1.0 - 78.0 / 79.0 + 1e-05
HEADS = 8
HALF = 4
LENGTH = 512
SIZE = 128
CHIPS = 16
VMEM_LIMIT = 40 * 1024 * 1024


def rate_of(slope_ref, head):
    slope = jnp.full((1, 1), slope_ref[head].astype(F32), F32)
    return jnp.exp((slope + 1.0) * (-8.0 / 64.0 * math.log(2.0))) * LAYER_FACTOR


def rows_of(shape, start=0):
    return lax.broadcasted_iota(jnp.int32, shape, 0).astype(F32) + jnp.float32(start)


def dot(a, b, dims):
    return lax.dot_general(a, b, (dims, ((), ())), preferred_element_type=F32)


NN = ((1,), (0,))
NT = ((1,), (1,))
TN = ((0,), (0,))


def masks(rate):
    shape = (256, 256)
    gap = (
        lax.broadcasted_iota(jnp.int32, shape, 0) - lax.broadcasted_iota(jnp.int32, shape, 1)
    ).astype(F32)
    base = jnp.exp(-rate * gap)
    return jnp.where(gap >= 0.0, base, 0.0), base * jnp.exp(-256.0 * rate)


def masks_t(rate):
    shape = (256, 256)
    gap = (
        lax.broadcasted_iota(jnp.int32, shape, 1) - lax.broadcasted_iota(jnp.int32, shape, 0)
    ).astype(F32)
    base = jnp.exp(-rate * gap)
    return jnp.where(gap >= 0.0, base, 0.0), base * jnp.exp(-256.0 * rate)


def key_kernel(chunk, slope_ref, core_ref, k_ref, v_ref, keep_ref, send_ref, kh_ref, vh_ref, kf, vf, acc):
    step = pl.program_id(0)
    kf[...] = k_ref[...].astype(F32).reshape(chunk * HEADS, SIZE)
    vf[...] = v_ref[...].astype(F32).reshape(chunk * HEADS, SIZE)
    core = core_ref[0]
    for h in range(HEADS):
        k = kf[pl.ds(h, chunk, stride=HEADS), :]
        v = vf[pl.ds(h, chunk, stride=HEADS), :].astype(BF16)
        pos = lax.broadcasted_iota(jnp.int32, (chunk, SIZE), 0) + step * chunk
        weight = jnp.exp(-rate_of(slope_ref, h) * (LENGTH - 1.0 - pos.astype(F32)))
        kh_ref[h] = k.astype(BF16)
        vh_ref[h] = v
        part = dot((k * weight).astype(BF16), v, TN)

        @pl.when(step == 0)
        def _():
            acc[h] = part

        @pl.when(step > 0)
        def _():
            acc[h] += part

    @pl.when(step == pl.num_programs(0) - 1)
    def _():
        @pl.when(core == 0)
        def _():
            keep_ref[...] = acc[:HALF]
            send_ref[...] = acc[HALF:]

        @pl.when(core == 1)
        def _():
            keep_ref[...] = acc[HALF:]
            send_ref[...] = acc[:HALF]


def smem():
    return pl.BlockSpec(memory_space=pltpu.SMEM)


def params():
    return pltpu.CompilerParams(vmem_limit_bytes=VMEM_LIMIT)


def cost(flops, bytes_accessed):
    return pl.CostEstimate(flops=flops, bytes_accessed=bytes_accessed, transcendentals=0)


def head_block(rows=LENGTH, width=SIZE):
    return pl.BlockSpec((1, rows, width), lambda h: (h, 0, 0))


def whole(shape):
    return pl.BlockSpec(shape, lambda *_: (0,) * len(shape))


def sds(shape, dtype):
    return jax.ShapeDtypeStruct(shape, dtype)


def key_states(slope, core, k, v, chunk=128):
    half = (HALF, SIZE, SIZE)
    return pl.pallas_call(
        functools.partial(key_kernel, chunk),
        grid=(LENGTH // chunk,),
        in_specs=[
            smem(),
            smem(),
            pl.BlockSpec((chunk, HEADS, SIZE), lambda i: (i, 0, 0)),
            pl.BlockSpec((chunk, HEADS, SIZE), lambda i: (i, 0, 0)),
        ],
        out_specs=[
            whole(half),
            whole(half),
            pl.BlockSpec((HEADS, chunk, SIZE), lambda i: (0, i, 0)),
            pl.BlockSpec((HEADS, chunk, SIZE), lambda i: (0, i, 0)),
        ],
        out_shape=[
            sds(half, F32),
            sds(half, F32),
            sds((HEADS, LENGTH, SIZE), BF16),
            sds((HEADS, LENGTH, SIZE), BF16),
        ],
        scratch_shapes=[
            pltpu.VMEM((chunk * HEADS, SIZE), F32),
            pltpu.VMEM((chunk * HEADS, SIZE), F32),
            pltpu.VMEM((HEADS, SIZE, SIZE), F32),
        ],
        compiler_params=params(),
        name="key_states",
    )(slope, core, k, v)


def turn_kernel(chunk, q_ref, u_ref, qh_ref, uh_ref, qf, uf):
    qf[...] = q_ref[...].astype(F32).reshape(chunk * HEADS, SIZE)
    uf[...] = u_ref[...].astype(F32).reshape(chunk * HEADS, SIZE)
    for h in range(HEADS):
        qh_ref[h] = qf[pl.ds(h, chunk, stride=HEADS), :].astype(BF16)
        uh_ref[h] = uf[pl.ds(h, chunk, stride=HEADS), :].astype(BF16)


def turn(q, u, chunk=128):
    block = pl.BlockSpec((chunk, HEADS, SIZE), lambda i: (i, 0, 0))
    out = pl.BlockSpec((HEADS, chunk, SIZE), lambda i: (0, i, 0))
    return pl.pallas_call(
        functools.partial(turn_kernel, chunk),
        grid=(LENGTH // chunk,),
        in_specs=[block, block],
        out_specs=[out, out],
        out_shape=[sds((HEADS, LENGTH, SIZE), BF16)] * 2,
        scratch_shapes=[pltpu.VMEM((chunk * HEADS, SIZE), F32)] * 2,
        compiler_params=params(),
        cost_estimate=cost(0, 4 * 2**20),
        name="turn",
    )(q, u)


def local_kernel(slope_ref, q_ref, k_ref, v_ref, loc_ref):
    rate = rate_of(slope_ref, pl.program_id(0))
    diag, off = masks(rate)
    q0, q1 = q_ref[0, :256], q_ref[0, 256:]
    k0, k1 = k_ref[0, :256], k_ref[0, 256:]
    v0, v1 = v_ref[0, :256], v_ref[0, 256:]
    a00 = (dot(q0, k0, NT) * diag).astype(BF16)
    a10 = (dot(q1, k0, NT) * off).astype(BF16)
    a11 = (dot(q1, k1, NT) * diag).astype(BF16)
    loc_ref[0, :256] = dot(a00, v0, NN)
    loc_ref[0, 256:] = dot(a10, v0, NN) + dot(a11, v1, NN)


def local_part(slope, q, k, v):
    return pl.pallas_call(
        local_kernel,
        grid=(HEADS,),
        in_specs=[smem(), head_block(), head_block(), head_block()],
        out_specs=head_block(),
        out_shape=sds((HEADS, LENGTH, SIZE), F32),
        compiler_params=params(),
        cost_estimate=cost(2 * 10**9, 5 * 2**20),
        name="local_part",
    )(slope, q, k, v)


def prefix_kernel(reverse, slope_ref, place_ref, z_ref, out_ref):
    rate = rate_of(slope_ref, place_ref[0])
    decay = jnp.exp(-2.0 * LENGTH * rate)
    state = jnp.zeros((32, SIZE), F32)
    order = list(range(CHIPS))
    if reverse:
        order = order[::-1]
    for p in order:
        out_ref[p] = state
        state = decay * state + z_ref[p]


def prefix(slope, place, z, reverse):
    shape = (CHIPS, 32, SIZE)
    return pl.pallas_call(
        functools.partial(prefix_kernel, reverse),
        in_specs=[smem(), smem(), pl.BlockSpec(memory_space=pltpu.VMEM)],
        out_specs=pl.BlockSpec(memory_space=pltpu.VMEM),
        out_shape=sds(shape, F32),
        compiler_params=params(),
        name="prefix",
    )(slope, place, z)


def state_of(core_ref, head, own_ref, other_ref):
    mine = (head // HALF) == core_ref[0]
    return jnp.where(mine, own_ref[0], other_ref[0]).astype(BF16)


def half_block():
    return pl.BlockSpec((1, SIZE, SIZE), lambda h: (lax.rem(h, HALF), 0, 0))


def output_kernel(slope_ref, core_ref, q_ref, u_ref, gain_ref, own_ref, other_ref, loc_ref, o_ref, sums_ref, sq, dt):
    h = pl.program_id(0)
    rate = rate_of(slope_ref, h)
    state = state_of(core_ref, h, own_ref, other_ref)
    decay_in = jnp.exp(-rate * (rows_of((LENGTH, SIZE)) + 1.0))
    out = loc_ref[0] + decay_in * dot(q_ref[0], state, NN)
    o_ref[0] = out
    scaled = gain_ref[0] * u_ref[0].astype(F32)

    @pl.when(h == 0)
    def _():
        sq[...] = out * out
        dt[...] = out * scaled

    @pl.when(h > 0)
    def _():
        sq[...] += out * out
        dt[...] += out * scaled

    @pl.when(h == HEADS - 1)
    def _():
        for b in range(4):
            sums_ref[pl.ds(b, 1), :] = jnp.sum(sq[b * 128 : (b + 1) * 128, :].T, axis=0, keepdims=True)
            sums_ref[pl.ds(4 + b, 1), :] = jnp.sum(dt[b * 128 : (b + 1) * 128, :].T, axis=0, keepdims=True)


def outputs(slope, core, q, u, gain, own, other, loc):
    return pl.pallas_call(
        output_kernel,
        grid=(HEADS,),
        in_specs=[
            smem(),
            smem(),
            head_block(),
            head_block(),
            pl.BlockSpec((1, 1, SIZE), lambda h: (h, 0, 0)),
            half_block(),
            half_block(),
            head_block(),
        ],
        out_specs=[head_block(), whole((8, SIZE))],
        out_shape=[sds((HEADS, LENGTH, SIZE), F32), sds((8, SIZE), F32)],
        scratch_shapes=[pltpu.VMEM((LENGTH, SIZE), F32)] * 2,
        compiler_params=params(),
        name="outputs",
    )(slope, core, q, u, gain, own, other, loc)


def grad_kernel(features, slope_ref, core_ref, sums_ref, q_ref, u_ref, gain_ref, o_ref, g_ref, keep_ref, send_ref, inv, coef):
    h = pl.program_id(0)

    @pl.when(h == 0)
    def _():
        sq = sums_ref[0:4, :]
        dt = sums_ref[4:8, :]
        root = lax.rsqrt(sq * (1.0 / features) + 1e-06)
        factor = root * root * root * dt * (1.0 / features)
        for b in range(4):
            inv[b * 128 : (b + 1) * 128, :] = jnp.broadcast_to(root[b : b + 1, :], (128, 128)).T
            coef[b * 128 : (b + 1) * 128, :] = jnp.broadcast_to(factor[b : b + 1, :], (128, 128)).T

    rate = rate_of(slope_ref, h)
    scaled = gain_ref[0] * u_ref[0].astype(F32)
    g = (inv[...] * scaled - o_ref[0] * coef[...]).astype(BF16)
    g_ref[0] = g
    first = jnp.exp(-rate * rows_of((LENGTH, SIZE)))
    weighted = (q_ref[0].astype(F32) * first).astype(BF16)
    state = dot(weighted, g, TN)
    slot = lax.rem(h, HALF)

    @pl.when(h // HALF == core_ref[0])
    def _():
        keep_ref[slot] = state

    @pl.when(h // HALF != core_ref[0])
    def _():
        send_ref[slot] = state


def grads(slope, core, sums, q, u, gain, o, features):
    half = (HALF, SIZE, SIZE)
    return pl.pallas_call(
        functools.partial(grad_kernel, features),
        grid=(HEADS,),
        in_specs=[
            smem(),
            smem(),
            whole((8, SIZE)),
            head_block(),
            head_block(),
            pl.BlockSpec((1, 1, SIZE), lambda h: (h, 0, 0)),
            head_block(),
        ],
        out_specs=[head_block(), whole(half), whole(half)],
        out_shape=[sds((HEADS, LENGTH, SIZE), BF16), sds(half, F32), sds(half, F32)],
        scratch_shapes=[pltpu.VMEM((LENGTH, SIZE), F32)] * 2,
        compiler_params=params(),
        name="grads",
    )(slope, core, sums, q, u, gain, o)


def grad_query_kernel(slope_ref, core_ref, g_ref, k_ref, v_ref, own_ref, other_ref, out_ref, wide):
    h = pl.program_id(0)
    rate = rate_of(slope_ref, h)
    diag, off = masks(rate)
    g0, g1 = g_ref[0, :256], g_ref[0, 256:]
    k0, k1 = k_ref[0, :256], k_ref[0, 256:]
    v0, v1 = v_ref[0, :256], v_ref[0, 256:]
    state = state_of(core_ref, h, own_ref, other_ref)
    b00 = (dot(g0, v0, NT) * diag).astype(BF16)
    b10 = (dot(g1, v0, NT) * off).astype(BF16)
    b11 = (dot(g1, v1, NT) * diag).astype(BF16)
    decay_in = jnp.exp(-rate * (rows_of((LENGTH, SIZE)) + 1.0))
    carried = decay_in * dot(g_ref[0], state, NT)
    wide[pl.ds(h, 256, stride=HEADS), :] = dot(b00, k0, NN) + carried[:256]
    wide[pl.ds(h + 256 * HEADS, 256, stride=HEADS), :] = (
        dot(b10, k0, NN) + dot(b11, k1, NN) + carried[256:]
    )

    @pl.when(h == HEADS - 1)
    def _():
        out_ref[...] = wide[...].reshape(LENGTH, HEADS, SIZE).astype(BF16)


def grad_query(slope, core, g, k, v, own, other):
    return pl.pallas_call(
        grad_query_kernel,
        grid=(HEADS,),
        in_specs=[smem(), smem(), head_block(), head_block(), head_block(), half_block(), half_block()],
        out_specs=whole((LENGTH, HEADS, SIZE)),
        out_shape=sds((LENGTH, HEADS, SIZE), BF16),
        scratch_shapes=[pltpu.VMEM((LENGTH * HEADS, SIZE), F32)],
        compiler_params=params(),
        cost_estimate=cost(3 * 10**9, 5 * 2**20),
        name="grad_query",
    )(slope, core, g, k, v, own, other)


def back_kernel(slope_ref, a_ref, b_ref, c_ref, out_ref):
    rate = rate_of(slope_ref, pl.program_id(0))
    diag, off = masks_t(rate)
    a0, a1 = a_ref[0, :256], a_ref[0, 256:]
    b0, b1 = b_ref[0, :256], b_ref[0, 256:]
    c0, c1 = c_ref[0, :256], c_ref[0, 256:]
    t00 = (dot(a0, b0, NT) * diag).astype(BF16)
    t01 = (dot(a0, b1, NT) * off).astype(BF16)
    t11 = (dot(a1, b1, NT) * diag).astype(BF16)
    out_ref[0, :256] = dot(t00, c0, NN) + dot(t01, c1, NN)
    out_ref[0, 256:] = dot(t11, c1, NN)


def back(slope, a, b, c, name):
    return pl.pallas_call(
        back_kernel,
        grid=(HEADS,),
        in_specs=[smem(), head_block(), head_block(), head_block()],
        out_specs=head_block(),
        out_shape=sds((HEADS, LENGTH, SIZE), F32),
        compiler_params=params(),
        cost_estimate=cost(2 * 10**9, 5 * 2**20),
        name=name,
    )(slope, a, b, c)


def finish_kernel(chunk, slope_ref, core_ref, k_ref, v_ref, kl_ref, vl_ref, own_ref, other_ref, gk_ref, gv_ref, wk, wv):
    step = pl.program_id(0)
    core = core_ref[0]
    for h in range(HEADS):
        rate = rate_of(slope_ref, h)
        pos = (lax.broadcasted_iota(jnp.int32, (chunk, SIZE), 0) + step * chunk).astype(F32)
        decay = jnp.exp(-rate * (LENGTH - pos))
        mine = core == h // HALF
        state = jnp.where(mine, own_ref[h % HALF], other_ref[h % HALF]).astype(BF16)
        wk[pl.ds(h, chunk, stride=HEADS), :] = kl_ref[h] + decay * dot(v_ref[h], state, NT)
        wv[pl.ds(h, chunk, stride=HEADS), :] = vl_ref[h] + decay * dot(k_ref[h], state, NN)
    gk_ref[...] = wk[...].reshape(chunk, HEADS, SIZE).astype(BF16)
    gv_ref[...] = wv[...].reshape(chunk, HEADS, SIZE).astype(BF16)


def finish(slope, core, k, v, kl, vl, own, other, chunk=128):
    half = (HALF, SIZE, SIZE)
    rows = pl.BlockSpec((HEADS, chunk, SIZE), lambda i: (0, i, 0))
    out = pl.BlockSpec((chunk, HEADS, SIZE), lambda i: (i, 0, 0))
    return pl.pallas_call(
        functools.partial(finish_kernel, chunk),
        grid=(LENGTH // chunk,),
        in_specs=[smem(), smem(), rows, rows, rows, rows, whole(half), whole(half)],
        out_specs=[out, out],
        out_shape=[sds((LENGTH, HEADS, SIZE), BF16)] * 2,
        scratch_shapes=[pltpu.VMEM((chunk * HEADS, SIZE), F32)] * 2,
        compiler_params=params(),
        name="finish",
    )(slope, core, k, v, kl, vl, own, other)


def exchange(a):
    return lax.ppermute(a, "ctx", [(i, i ^ 1) for i in range(2 * CHIPS)])


def all_to_all(a):
    groups = [[2 * p + c for p in range(CHIPS)] for c in range(2)]
    return lax.all_to_all(a, "ctx", 0, 0, axis_index_groups=groups, tiled=True)


def scan_states(slope, place, core, decay, keep, send, reverse):
    recv = exchange(send)
    first = core == 0
    low = jnp.where(first, keep, recv)
    high = jnp.where(first, recv, keep)
    if reverse:
        total = low + decay * high
    else:
        total = decay * low + high
    moved = all_to_all(total.reshape(CHIPS, 32, SIZE))
    state = all_to_all(prefix(slope, place, moved, reverse)).reshape(HALF, SIZE, SIZE)
    if reverse:
        beyond = high + decay * state
        mine = jnp.where(first, beyond, state)
        give = jnp.where(first, state, beyond)
    else:
        beyond = decay * state + low
        mine = jnp.where(first, state, beyond)
        give = jnp.where(first, beyond, state)
    return mine, exchange(give)


def on_device(queries, key_rows, value_rows, upstream, norm_gain, slope_index):
    place = lax.axis_index("ctx")
    core = lax.rem(place, 2)
    chip = place // 2
    core_ref = core.reshape(1).astype(jnp.int32)
    own_head = (core * HALF + chip // (CHIPS // HALF)).reshape(1).astype(jnp.int32)
    rate = 2.0 ** (-8.0 * (slope_index.astype(F32) + 1.0) / 64.0) * LAYER_FACTOR
    block_decay = jnp.exp(-rate * LENGTH)
    decay = jnp.where(core == 0, block_decay[:HALF], block_decay[HALF:])[:, None, None]
    gain = norm_gain.reshape(HEADS, 1, SIZE)

    keep, send, kh, vh = key_states(slope_index, core_ref, key_rows, value_rows)
    qh, uh = turn(queries, upstream)
    loc = local_part(slope_index, qh, kh, vh)
    e_own, e_other = scan_states(slope_index, own_head, core, decay, keep, send, False)
    out, sums = outputs(slope_index, core_ref, qh, uh, gain, e_own, e_other, loc)
    sums = lax.psum(sums, "head")
    features = float(lax.axis_size("head") * HEADS * SIZE)
    g, keep, send = grads(slope_index, core_ref, sums, qh, uh, gain, out, features)
    gv_local = back(slope_index, kh, qh, g, "gv_local")
    gk_local = back(slope_index, vh, g, qh, "gk_local")
    gq = grad_query(slope_index, core_ref, g, kh, vh, e_own, e_other)
    l_own, l_other = scan_states(slope_index, own_head, core, decay, keep, send, True)
    gk, gv = finish(slope_index, core_ref, kh, vh, gk_local, gv_local, l_own, l_other)
    return gq, gk, gv


def solution(mesh):
    rows = P("ctx", "head", None)
    return jax.shard_map(
        on_device,
        mesh=mesh,
        in_specs=(rows, rows, rows, rows, P("head", None), P("head")),
        out_specs=(rows, rows, rows),
        check_vma=False,
    )
```

```python
import functools
import math

import jax
import jax.numpy as jnp
from jax import lax
from jax.experimental import pallas as pl
from jax.experimental.pallas import tpu as pltpu
from jax.sharding import PartitionSpec as P

F32 = jnp.float32
BF16 = jnp.bfloat16
LAYER_FACTOR = 1.0 - 78.0 / 79.0 + 1e-05
HEADS = 8
LENGTH = 512
SIZE = 128
BLOCKS = 32
SLICE = HEADS * SIZE // BLOCKS
CHUNK = 128
PARTS = LENGTH // CHUNK
VMEM_LIMIT = 24 * 1024 * 1024

NN = ((1,), (0,))
NT = ((1,), (1,))
TN = ((0,), (0,))


def rate_of(slope_ref, head):
    slope = jnp.full((1, 1), slope_ref[head].astype(F32), F32)
    return jnp.exp((slope + 1.0) * (-8.0 / 64.0 * math.log(2.0))) * LAYER_FACTOR


def rows_of(shape, start=0):
    return (lax.broadcasted_iota(jnp.int32, shape, 0) + start).astype(F32)


def dot(a, b, dims):
    return lax.dot_general(a, b, (dims, ((), ())), preferred_element_type=F32)


def masks(rate, transposed=False):
    shape = (256, 256)
    gap = lax.broadcasted_iota(jnp.int32, shape, 0) - lax.broadcasted_iota(jnp.int32, shape, 1)
    if transposed:
        gap = -gap
    base = jnp.exp(-rate * gap.astype(F32))
    return jnp.where(gap >= 0, base, 0.0), base * jnp.exp(-256.0 * rate)


def hbm(x):
    return pltpu.with_memory_space_constraint(x, pltpu.HBM)


def near(x):
    return pltpu.with_memory_space_constraint(x, pltpu.VMEM)


def call(body, name, ins, outs, scratch=(), flops=0, moved=0):
    kinds = {"smem": pltpu.SMEM, "vmem": pltpu.VMEM, "hbm": pl.ANY, "any": pl.ANY}
    args, in_specs = [], []
    for kind, x in ins:
        in_specs.append(pl.BlockSpec(memory_space=kinds[kind]))
        args.append({"vmem": near, "hbm": hbm}.get(kind, lambda a: a)(x))
    out_shape, out_specs = [], []
    for kind, shape, dtype in outs:
        out_specs.append(pl.BlockSpec(memory_space=kinds[kind]))
        out_shape.append((pltpu.VMEM if kind == "vmem" else pltpu.HBM)(shape, dtype))
    return pl.pallas_call(
        body,
        in_specs=in_specs,
        out_specs=out_specs,
        out_shape=out_shape,
        scratch_shapes=list(scratch),
        compiler_params=pltpu.CompilerParams(vmem_limit_bytes=VMEM_LIMIT),
        cost_estimate=pl.CostEstimate(flops=flops, bytes_accessed=moved, transcendentals=0),
        name=name,
    )(*args)


STATE = (HEADS, SIZE, SIZE)
ROWS = (HEADS, LENGTH, SIZE)
WHOLE = (LENGTH, HEADS, SIZE)


def by_head(wide, part):
    return [wide[pl.ds(h + part * CHUNK * HEADS, CHUNK, stride=HEADS), :] for h in range(HEADS)]


def spread(wide, block, part):
    wide[pl.ds(part * CHUNK * HEADS, CHUNK * HEADS), :] = block.astype(F32).reshape(CHUNK * HEADS, SIZE)


SPLIT = ((0, 2), (2, 6))


def fetch(pairs, sems):
    groups = []
    for n, (start, count) in enumerate(SPLIT):
        groups.append([])
        for i, (src, dst) in enumerate(pairs):
            part = pl.ds(start, count)
            c = pltpu.make_async_copy(src.at[part], dst.at[part], sems.at[n * len(pairs) + i])
            c.start()
            groups[-1].append(c)
    return groups


def await_head(groups, h):
    for n, (start, _) in enumerate(SPLIT):
        if h == start:
            wait_all(groups[n])


def put(src, dst, part, sem):
    c = pltpu.make_async_copy(src.at[part], dst.at[part], sem)
    c.start()
    return c


def fetch_rows(src, dst, sems, base=0):
    return [put(src, dst, pl.ds(p * CHUNK, CHUNK), sems.at[base + p]) for p in range(PARTS)]


def wait_all(copies):
    for c in copies:
        c.wait()


def dma(count):
    return pltpu.SemaphoreType.DMA((count,))


def key_kernel(slope_hbm, k_hbm, v_hbm, s_ref, kh_hbm, vh_hbm, slope_ref, kin, vin, kw, vw, kh, vh, sems, out_sems):
    first = pltpu.make_async_copy(slope_hbm, slope_ref, sems.at[2 * PARTS])
    first.start()
    k_copies = fetch_rows(k_hbm, kin, sems)
    v_copies = fetch_rows(v_hbm, vin, sems, PARTS)
    first.wait()
    rates = [rate_of(slope_ref, h) for h in range(HEADS)]
    writes = []
    for p in range(PARTS):
        rows = pl.ds(p * CHUNK, CHUNK)
        k_copies[p].wait()
        v_copies[p].wait()
        spread(kw, kin[rows], p)
        spread(vw, vin[rows], p)
        ks, vs = by_head(kw, p), by_head(vw, p)
        left = LENGTH - 1.0 - rows_of((CHUNK, SIZE), p * CHUNK)
        for h in range(HEADS):
            v = vs[h].astype(BF16)
            kh[h, rows, :] = ks[h].astype(BF16)
            vh[h, rows, :] = v
            part = dot((ks[h] * jnp.exp(-rates[h] * left)).astype(BF16), v, TN)
            s_ref[h] = part if p == 0 else s_ref[h] + part
        for i, (a, b) in enumerate(((kh, kh_hbm), (vh, vh_hbm))):
            writes.append(pltpu.make_async_copy(a.at[:, rows], b.at[:, rows], out_sems.at[2 * p + i]))
            writes[-1].start()
    wait_all(writes)


def key_states(slope, k, v):
    wide = pltpu.VMEM((LENGTH * HEADS, SIZE), F32)
    return call(
        key_kernel,
        "key_states",
        [("hbm", slope), ("hbm", k), ("hbm", v)],
        [("vmem", STATE, F32), ("hbm", ROWS, BF16), ("hbm", ROWS, BF16)],
        [
            pltpu.SMEM((HEADS,), jnp.int32),
            pltpu.VMEM(WHOLE, BF16),
            pltpu.VMEM(WHOLE, BF16),
            wide,
            wide,
            pltpu.VMEM(ROWS, BF16),
            pltpu.VMEM(ROWS, BF16),
            dma(2 * PARTS + 1),
            dma(2 * PARTS),
        ],
    )


def local_kernel(slope_ref, q_hbm, k_hbm, v_hbm, u_hbm, loc_hbm, qh_hbm, uh_hbm, wq_hbm, qin, uin, qw, uw, q, k, v, u, loc, wq, sems, in_sems, out_sems):
    q_copies = fetch_rows(q_hbm, qin, in_sems)
    copies = fetch(((k_hbm, k), (v_hbm, v)), sems)
    u_copies = fetch_rows(u_hbm, uin, in_sems, PARTS)
    wait_all(q_copies)
    writes = []
    for p in range(PARTS):
        rows = pl.ds(p * CHUNK, CHUNK)
        spread(qw, qin[rows], p)
        for h, block in enumerate(by_head(qw, p)):
            q[h, rows, :] = block.astype(BF16)
    writes.append(pltpu.make_async_copy(q, qh_hbm, out_sems.at[0]))
    writes[-1].start()
    done = rows_of((LENGTH, SIZE))
    for h in range(HEADS):
        await_head(copies, h)
        rate = rate_of(slope_ref, h)
        diag, off = masks(rate)
        q0, q1 = q[h, :256], q[h, 256:]
        k0, k1 = k[h, :256], k[h, 256:]
        v0, v1 = v[h, :256], v[h, 256:]
        a00 = (dot(q0, k0, NT) * diag).astype(BF16)
        a10 = (dot(q1, k0, NT) * off).astype(BF16)
        a11 = (dot(q1, k1, NT) * diag).astype(BF16)
        loc[h, :256] = dot(a00, v0, NN)
        loc[h, 256:] = dot(a10, v0, NN) + dot(a11, v1, NN)
        wq[h] = (q[h].astype(F32) * jnp.exp(-rate * done)).T.astype(BF16)
    writes.append(pltpu.make_async_copy(loc, loc_hbm, out_sems.at[1]))
    writes.append(pltpu.make_async_copy(wq, wq_hbm, out_sems.at[2]))
    writes[-1].start()
    writes[-2].start()
    wait_all(u_copies)
    for p in range(PARTS):
        rows = pl.ds(p * CHUNK, CHUNK)
        spread(uw, uin[rows], p)
        for h, block in enumerate(by_head(uw, p)):
            u[h, rows, :] = block.astype(BF16)
    writes.append(pltpu.make_async_copy(u, uh_hbm, out_sems.at[3]))
    writes[-1].start()
    wait_all(writes)


def local_part(slope, q, k, v, u):
    rows, wide = pltpu.VMEM(ROWS, BF16), pltpu.VMEM((LENGTH * HEADS, SIZE), F32)
    whole = pltpu.VMEM(WHOLE, BF16)
    turned = (HEADS, SIZE, LENGTH)
    return call(
        local_kernel,
        "local_part",
        [("smem", slope), ("hbm", q), ("hbm", k), ("hbm", v), ("hbm", u)],
        [("hbm", ROWS, F32), ("hbm", ROWS, BF16), ("hbm", ROWS, BF16), ("hbm", turned, BF16)],
        [
            whole,
            whole,
            wide,
            wide,
            rows,
            rows,
            rows,
            rows,
            pltpu.VMEM(ROWS, F32),
            pltpu.VMEM(turned, BF16),
            dma(4),
            dma(2 * PARTS),
            dma(4),
        ],
        flops=2 * 10**9,
        moved=8 * 2**20,
    )


def prefix_kernel(reverse, slope_ref, z_ref, out_ref):
    head = lax.axis_index("ctx") // (BLOCKS // HEADS)
    decay = jnp.exp(-float(LENGTH) * rate_of(slope_ref, head))
    state = jnp.zeros((SLICE, SIZE), F32)
    for p in range(BLOCKS - 1, -1, -1) if reverse else range(BLOCKS):
        out_ref[p] = state
        state = decay * state + z_ref[p]


def prefix(slope, z, reverse):
    (out,) = call(
        functools.partial(prefix_kernel, reverse),
        "prefix",
        [("smem", slope), ("vmem", z)],
        [("vmem", (BLOCKS, SLICE, SIZE), F32)],
    )
    return out


def output_kernel(slope_ref, q_ref, u_ref, gain_ref, e_ref, loc_ref, o_ref, sums_ref, sq, dt, sums):
    done = rows_of((LENGTH, SIZE), 1)
    for h in range(HEADS):
        decay_in = jnp.exp(-rate_of(slope_ref, h) * done)
        out = loc_ref[h] + decay_in * dot(q_ref[h], e_ref[h].astype(BF16), NN)
        o_ref[h] = out
        scaled = gain_ref[h : h + 1, :] * u_ref[h].astype(F32)
        sq[...] = out * out if h == 0 else sq[...] + out * out
        dt[...] = out * scaled if h == 0 else dt[...] + out * scaled
    for b in range(4):
        rows = slice(b * 128, (b + 1) * 128)
        sums[b : b + 1, :] = jnp.sum(sq[rows, :].T, axis=0, keepdims=True)
        sums[4 + b : 5 + b, :] = jnp.sum(dt[rows, :].T, axis=0, keepdims=True)
    for i in range(sums_ref.shape[0]):
        sums_ref[i] = sums[...]


def outputs(slope, q, u, gain, e, loc, peers):
    return call(
        output_kernel,
        "outputs",
        [("smem", slope), ("vmem", q), ("vmem", u), ("vmem", gain), ("vmem", e), ("vmem", loc)],
        [("vmem", ROWS, F32), ("vmem", (peers, 8, SIZE), F32)],
        [pltpu.VMEM((LENGTH, SIZE), F32), pltpu.VMEM((LENGTH, SIZE), F32), pltpu.VMEM((8, SIZE), F32)],
    )


def grad_kernel(sums_ref, wq_ref, u_ref, gain_ref, o_ref, g_hbm, s_ref, g, sems):
    peers = sums_ref.shape[0]
    features = float(peers * HEADS * SIZE)
    sums = sums_ref[0]
    for i in range(1, peers):
        sums = sums + sums_ref[i]
    root = lax.rsqrt(sums[0:4, :] * (1.0 / features) + 1e-06)
    factor = root * root * root * sums[4:8, :] * (1.0 / features)
    writes = []
    for b in range(4):
        rows = pl.ds(b * 128, 128)
        inv = jnp.broadcast_to(root[b : b + 1, :], (128, 128)).T
        coef = jnp.broadcast_to(factor[b : b + 1, :], (128, 128)).T
        for h in range(HEADS):
            scaled = gain_ref[h : h + 1, :] * u_ref[h, rows, :].astype(F32)
            g[h, rows, :] = (inv * scaled - o_ref[h, rows, :] * coef).astype(BF16)
        writes.append(pltpu.make_async_copy(g.at[:, rows], g_hbm.at[:, rows], sems.at[b]))
        writes[-1].start()
    for h in range(HEADS):
        s_ref[h] = dot(wq_ref[h], g[h], NN)
    wait_all(writes)


def grads(sums, wq, u, gain, o):
    return call(
        grad_kernel,
        "grads",
        [("vmem", sums), ("vmem", wq), ("vmem", u), ("vmem", gain), ("vmem", o)],
        [("hbm", ROWS, BF16), ("vmem", STATE, F32)],
        [pltpu.VMEM(ROWS, BF16), dma(4)],
    )


def query_kernel(slope_ref, g_hbm, k_hbm, v_hbm, e_hbm, out_hbm, g, k, v, e, wide, block, sems, e_sems, out_sems):
    e_copy = pltpu.make_async_copy(e_hbm, e, e_sems.at[0])
    e_copy.start()
    copies = fetch(((g_hbm, g), (k_hbm, k), (v_hbm, v)), sems)
    e_copy.wait()
    done = rows_of((LENGTH, SIZE), 1)
    for h in range(HEADS):
        await_head(copies, h)
        rate = rate_of(slope_ref, h)
        diag, off = masks(rate)
        g0, g1 = g[h, :256], g[h, 256:]
        k0, k1 = k[h, :256], k[h, 256:]
        v0, v1 = v[h, :256], v[h, 256:]
        b00 = (dot(g0, v0, NT) * diag).astype(BF16)
        b10 = (dot(g1, v0, NT) * off).astype(BF16)
        b11 = (dot(g1, v1, NT) * diag).astype(BF16)
        carried = jnp.exp(-rate * done) * dot(g[h], e[h].astype(BF16), NT)
        wide[pl.ds(h, 256, stride=HEADS), :] = dot(b00, k0, NN) + carried[:256]
        wide[pl.ds(h + 256 * HEADS, 256, stride=HEADS), :] = (
            dot(b10, k0, NN) + dot(b11, k1, NN) + carried[256:]
        )
    writes = []
    for p in range(PARTS):
        rows = pl.ds(p * CHUNK, CHUNK)
        block[rows] = wide[pl.ds(p * CHUNK * HEADS, CHUNK * HEADS), :].reshape(CHUNK, HEADS, SIZE).astype(BF16)
        writes.append(pltpu.make_async_copy(block.at[rows], out_hbm.at[rows], out_sems.at[p]))
        writes[-1].start()
    wait_all(writes)


def grad_query(slope, g, k, v, e):
    rows = pltpu.VMEM(ROWS, BF16)
    (out,) = call(
        query_kernel,
        "grad_query",
        [("smem", slope), ("hbm", g), ("hbm", k), ("hbm", v), ("any", e)],
        [("hbm", WHOLE, BF16)],
        [
            rows,
            rows,
            rows,
            pltpu.VMEM(STATE, F32),
            pltpu.VMEM((LENGTH * HEADS, SIZE), F32),
            pltpu.VMEM(WHOLE, BF16),
            dma(6),
            dma(1),
            dma(PARTS),
        ],
        flops=3 * 10**9,
        moved=5 * 2**20,
    )
    return out


def back_kernel(slope_ref, k_hbm, v_hbm, q_hbm, g_hbm, kl_hbm, vl_hbm, k, v, q, g, kl, vl, sems, out_sems):
    copies = fetch(((k_hbm, k), (q_hbm, q), (g_hbm, g), (v_hbm, v)), sems)
    writes = []
    for h in range(HEADS):
        await_head(copies, h)
        diag, off = masks(rate_of(slope_ref, h), True)
        k0, k1 = k[h, :256], k[h, 256:]
        v0, v1 = v[h, :256], v[h, 256:]
        q0, q1 = q[h, :256], q[h, 256:]
        g0, g1 = g[h, :256], g[h, 256:]
        for a0, a1, b0, b1, c0, c1, to in (
            (k0, k1, q0, q1, g0, g1, vl),
            (v0, v1, g0, g1, q0, q1, kl),
        ):
            t00 = (dot(a0, b0, NT) * diag).astype(BF16)
            t01 = (dot(a0, b1, NT) * off).astype(BF16)
            t11 = (dot(a1, b1, NT) * diag).astype(BF16)
            to[h, :256] = (dot(t00, c0, NN) + dot(t01, c1, NN)).astype(BF16)
            to[h, 256:] = dot(t11, c1, NN).astype(BF16)
        if h % 4 == 3:
            part = pl.ds(h - 3, 4)
            writes.append(put(vl, vl_hbm, part, out_sems.at[h // 4]))
            writes.append(put(kl, kl_hbm, part, out_sems.at[2 + h // 4]))
    wait_all(writes)


def back(slope, k, v, q, g):
    rows = pltpu.VMEM(ROWS, BF16)
    return call(
        back_kernel,
        "back",
        [("smem", slope), ("hbm", k), ("hbm", v), ("hbm", q), ("hbm", g)],
        [("hbm", ROWS, BF16), ("hbm", ROWS, BF16)],
        [rows, rows, rows, rows, rows, rows, dma(8), dma(4)],
        flops=4 * 10**9,
        moved=8 * 2**20,
    )


def finish_kernel(slope_ref, k_hbm, v_hbm, kl_hbm, vl_hbm, l_ref, gk_hbm, gv_hbm, k, v, kl, vl, wk, wv, gk, gv, sems, out_sems):
    copies = []
    for p in range(2):
        rows = pl.ds(p * 256, 256)
        group = []
        for i, (a, b) in enumerate(((k_hbm, k), (v_hbm, v), (kl_hbm, kl), (vl_hbm, vl))):
            group.append(pltpu.make_async_copy(a.at[:, rows], b.at[:, rows], sems.at[4 * p + i]))
            group[-1].start()
        copies.append(group)
    rates = [rate_of(slope_ref, h) for h in range(HEADS)]
    writes = []
    for p in range(2):
        rows = pl.ds(p * 256, 256)
        wait_all(copies[p])
        left = LENGTH - rows_of((256, SIZE), p * 256)
        flat = pl.ds(p * 256 * HEADS, 256 * HEADS)
        for h in range(HEADS):
            strided = pl.ds(h + p * 256 * HEADS, 256, stride=HEADS)
            decay = jnp.exp(-rates[h] * left)
            state = l_ref[h].astype(BF16)
            wk[strided, :] = kl[h, rows, :].astype(F32) + decay * dot(v[h, rows, :], state, NT)
            wv[strided, :] = vl[h, rows, :].astype(F32) + decay * dot(k[h, rows, :], state, NN)
        gk[rows] = wk[flat, :].reshape(256, HEADS, SIZE).astype(BF16)
        gv[rows] = wv[flat, :].reshape(256, HEADS, SIZE).astype(BF16)
        for i, (a, b) in enumerate(((gk, gk_hbm), (gv, gv_hbm))):
            writes.append(pltpu.make_async_copy(a.at[rows], b.at[rows], out_sems.at[2 * p + i]))
            writes[-1].start()
    wait_all(writes)


def finish(slope, k, v, kl, vl, l):
    wide = pltpu.VMEM((LENGTH * HEADS, SIZE), F32)
    rows, block = pltpu.VMEM(ROWS, BF16), pltpu.VMEM(WHOLE, BF16)
    return call(
        finish_kernel,
        "finish",
        [("smem", slope), ("hbm", k), ("hbm", v), ("hbm", kl), ("hbm", vl), ("vmem", l)],
        [("hbm", WHOLE, BF16), ("hbm", WHOLE, BF16)],
        [rows, rows, rows, rows, wide, wide, block, block, dma(8), dma(4)],
    )


def all_to_all(a):
    return lax.all_to_all(a.reshape(BLOCKS, SLICE, SIZE), "ctx", 0, 0, tiled=True)


def on_device(queries, key_rows, value_rows, upstream, norm_gain, slope_index):
    slope = slope_index

    states, kh, vh = key_states(slope, key_rows, value_rows)
    moved = all_to_all(states)
    loc, qh, uh, wq = local_part(slope, queries, kh, vh, upstream)
    moved, loc, qh, uh, wq = lax.optimization_barrier((moved, loc, qh, uh, wq))
    entering = all_to_all(prefix(slope, moved, False)).reshape(STATE)

    peers = lax.axis_size("head")
    out, sums = outputs(slope, qh, uh, norm_gain, entering, loc, peers)
    sums = lax.all_to_all(sums, "head", 0, 0, tiled=True)
    g, states = grads(sums, wq, uh, norm_gain, out)

    moved = all_to_all(states)
    gk_local, gv_local = back(slope, kh, vh, qh, g)
    moved, gk_local, gv_local = lax.optimization_barrier((moved, gk_local, gv_local))
    leaving = all_to_all(prefix(slope, moved, True)).reshape(STATE)
    gq = grad_query(slope, g, kh, vh, entering)
    leaving, gq = lax.optimization_barrier((leaving, gq))
    gk, gv = finish(slope, kh, vh, gk_local, gv_local, leaving)
    return gq, gk, gv


def solution(mesh):
    rows = P("ctx", "head", None)
    return jax.shard_map(
        on_device,
        mesh=mesh,
        in_specs=(rows, rows, rows, rows, P("head", None), P("head")),
        out_specs=(rows, rows, rows),
        check_vma=False,
    )
```

```python
import functools
import math

import jax
import jax.numpy as jnp
from jax import lax
from jax.experimental import pallas as pl
from jax.experimental.pallas import tpu as pltpu
from jax.sharding import PartitionSpec as P

F32 = jnp.float32
BF16 = jnp.bfloat16
LAYER_FACTOR = 1.0 - 78.0 / 79.0 + 1e-05
HEADS = 8
LENGTH = 512
SIZE = 128
BLOCKS = 32
SLICE = HEADS * SIZE // BLOCKS
CHUNK = 128
PARTS = LENGTH // CHUNK
VMEM_LIMIT = 32 * 1024 * 1024

NN = ((1,), (0,))
NT = ((1,), (1,))
TN = ((0,), (0,))


def rate_of(slope_ref, head):
    slope = jnp.full((1, 1), slope_ref[head].astype(F32), F32)
    return jnp.exp((slope + 1.0) * (-8.0 / 64.0 * math.log(2.0))) * LAYER_FACTOR


def rows_of(shape, start=0):
    return (lax.broadcasted_iota(jnp.int32, shape, 0) + start).astype(F32)


def dot(a, b, dims):
    return lax.dot_general(a, b, (dims, ((), ())), preferred_element_type=F32)


def masks(rate, transposed=False):
    shape = (256, 256)
    gap = lax.broadcasted_iota(jnp.int32, shape, 0) - lax.broadcasted_iota(jnp.int32, shape, 1)
    if transposed:
        gap = -gap
    base = jnp.exp(-rate * gap.astype(F32))
    return jnp.where(gap >= 0, base, 0.0), base * jnp.exp(-256.0 * rate)


def hbm(x):
    return pltpu.with_memory_space_constraint(x, pltpu.HBM)


def near(x):
    return pltpu.with_memory_space_constraint(x, pltpu.VMEM)


def call(body, name, ins, outs, scratch=(), flops=0, moved=0):
    kinds = {"smem": pltpu.SMEM, "vmem": pltpu.VMEM, "hbm": pl.ANY, "any": pl.ANY}
    args, in_specs = [], []
    for kind, x in ins:
        in_specs.append(pl.BlockSpec(memory_space=kinds[kind]))
        args.append({"vmem": near, "hbm": hbm}.get(kind, lambda a: a)(x))
    out_shape, out_specs = [], []
    for kind, shape, dtype in outs:
        out_specs.append(pl.BlockSpec(memory_space=kinds[kind]))
        out_shape.append((pltpu.VMEM if kind == "vmem" else pltpu.HBM)(shape, dtype))
    return pl.pallas_call(
        body,
        in_specs=in_specs,
        out_specs=out_specs,
        out_shape=out_shape,
        scratch_shapes=list(scratch),
        compiler_params=pltpu.CompilerParams(vmem_limit_bytes=VMEM_LIMIT),
        cost_estimate=pl.CostEstimate(flops=flops, bytes_accessed=moved, transcendentals=0),
        name=name,
    )(*args)


STATE = (HEADS, SIZE, SIZE)
ROWS = (HEADS, LENGTH, SIZE)
WHOLE = (LENGTH, HEADS, SIZE)


def by_head(wide, part):
    return [wide[pl.ds(h + part * CHUNK * HEADS, CHUNK, stride=HEADS), :] for h in range(HEADS)]


def spread(wide, block, part):
    wide[pl.ds(part * CHUNK * HEADS, CHUNK * HEADS), :] = block.astype(F32).reshape(CHUNK * HEADS, SIZE)


SPLIT = ((0, 2), (2, 6))


def fetch(pairs, sems):
    groups = []
    for n, (start, count) in enumerate(SPLIT):
        groups.append([])
        for i, (src, dst) in enumerate(pairs):
            part = pl.ds(start, count)
            c = pltpu.make_async_copy(src.at[part], dst.at[part], sems.at[n * len(pairs) + i])
            c.start()
            groups[-1].append(c)
    return groups


def await_head(groups, h):
    for n, (start, _) in enumerate(SPLIT):
        if h == start:
            wait_all(groups[n])


def put(src, dst, part, sem):
    c = pltpu.make_async_copy(src.at[part], dst.at[part], sem)
    c.start()
    return c


def fetch_rows(src, dst, sems, base=0):
    return [put(src, dst, pl.ds(p * CHUNK, CHUNK), sems.at[base + p]) for p in range(PARTS)]


def wait_all(copies):
    for c in copies:
        c.wait()


def dma(count):
    return pltpu.SemaphoreType.DMA((count,))


def key_kernel(slope_hbm, k_hbm, v_hbm, s_hbm, slope_ref, kin, vin, kw, vw, s, sems, out_sems):
    first = pltpu.make_async_copy(slope_hbm, slope_ref, sems.at[2 * PARTS])
    first.start()
    k_copies = fetch_rows(k_hbm, kin, sems)
    v_copies = fetch_rows(v_hbm, vin, sems, PARTS)
    first.wait()
    rates = [rate_of(slope_ref, h) for h in range(HEADS)]
    writes = []
    for p in range(PARTS):
        rows = pl.ds(p * CHUNK, CHUNK)
        k_copies[p].wait()
        v_copies[p].wait()
        spread(kw, kin[rows], p)
        spread(vw, vin[rows], p)
        ks, vs = by_head(kw, p), by_head(vw, p)
        left = LENGTH - 1.0 - rows_of((CHUNK, SIZE), p * CHUNK)
        for h in range(HEADS):
            weighted = (ks[h] * jnp.exp(-rates[h] * left)).astype(BF16)
            part = dot(weighted, vs[h].astype(BF16), TN)
            s[h] = part if p == 0 else s[h] + part
            if p == PARTS - 1 and h % 4 == 3:
                writes.append(put(s, s_hbm, pl.ds(h - 3, 4), out_sems.at[h // 4]))
    wait_all(writes)


def key_states(slope, k, v):
    whole, wide = pltpu.VMEM(WHOLE, BF16), pltpu.VMEM((LENGTH * HEADS, SIZE), F32)
    (out,) = call(
        key_kernel,
        "key_states",
        [("hbm", slope), ("hbm", k), ("hbm", v)],
        [("hbm", STATE, F32)],
        [pltpu.SMEM((HEADS,), jnp.int32), whole, whole, wide, wide, pltpu.VMEM(STATE, F32), dma(2 * PARTS + 1), dma(2)],
    )
    return out


def local_kernel(slope_ref, q_hbm, k_hbm, v_hbm, u_hbm, loc, qh_hbm, kh_hbm, vh_hbm, uh_hbm, wq_hbm, qin, kin, vin, uin, wide, q, k, v, u, wq, in_sems, out_sems):
    sources = ((q_hbm, qin, q, qh_hbm), (k_hbm, kin, k, kh_hbm), (v_hbm, vin, v, vh_hbm), (u_hbm, uin, u, uh_hbm))
    copies = [pltpu.make_async_copy(s[0], s[1], in_sems.at[i]) for i, s in enumerate(sources)]
    for c in copies:
        c.start()
    writes = []

    def turn(i):
        _, near_by, turned, to = sources[i]
        copies[i].wait()
        for p in range(PARTS):
            rows = pl.ds(p * CHUNK, CHUNK)
            spread(wide.at[i], near_by[rows], p)
            for h, block in enumerate(by_head(wide.at[i], p)):
                turned[h, rows, :] = block.astype(BF16)
        writes.append(pltpu.make_async_copy(turned, to, out_sems.at[i]))
        writes[-1].start()

    turn(0)
    turn(1)
    turn(2)
    done = rows_of((LENGTH, SIZE))
    for h in range(HEADS):
        rate = rate_of(slope_ref, h)
        diag, off = masks(rate)
        q0, q1 = q[h, :256], q[h, 256:]
        k0, k1 = k[h, :256], k[h, 256:]
        v0, v1 = v[h, :256], v[h, 256:]
        a00 = (dot(q0, k0, NT) * diag).astype(BF16)
        a10 = (dot(q1, k0, NT) * off).astype(BF16)
        a11 = (dot(q1, k1, NT) * diag).astype(BF16)
        loc[h, :256] = dot(a00, v0, NN)
        loc[h, 256:] = dot(a10, v0, NN) + dot(a11, v1, NN)
        wq[h] = (q[h].astype(F32) * jnp.exp(-rate * done)).T.astype(BF16)
    writes.append(pltpu.make_async_copy(wq, wq_hbm, out_sems.at[4]))
    writes[-1].start()
    turn(3)
    wait_all(writes)


def local_part(slope, q, k, v, u):
    rows, whole = pltpu.VMEM(ROWS, BF16), pltpu.VMEM(WHOLE, BF16)
    turned = (HEADS, SIZE, LENGTH)
    return call(
        local_kernel,
        "local_part",
        [("smem", slope), ("hbm", q), ("hbm", k), ("hbm", v), ("hbm", u)],
        [("vmem", ROWS, F32)] + [("hbm", ROWS, BF16)] * 4 + [("hbm", turned, BF16)],
        [whole] * 4
        + [pltpu.VMEM((4, LENGTH * HEADS, SIZE), F32)]
        + [rows] * 4
        + [pltpu.VMEM(turned, BF16), dma(4), dma(5)],
        flops=2 * 10**9,
        moved=8 * 2**20,
    )


def prefix_kernel(reverse, slope_ref, z_ref, out_hbm, out, sems):
    head = lax.axis_index("ctx") // (BLOCKS // HEADS)
    decay = jnp.exp(-float(LENGTH) * rate_of(slope_ref, head))
    state = jnp.zeros((SLICE, SIZE), F32)
    writes = []
    for n in range(BLOCKS):
        p = BLOCKS - 1 - n if reverse else n
        out[p] = state
        state = decay * state + z_ref[p]
        if n % 8 == 7:
            writes.append(put(out, out_hbm, pl.ds(p if reverse else p - 7, 8), sems.at[n // 8]))
    wait_all(writes)


def prefix_near_kernel(slope_ref, z_ref, out_ref):
    head = lax.axis_index("ctx") // (BLOCKS // HEADS)
    decay = jnp.exp(-float(LENGTH) * rate_of(slope_ref, head))
    state = jnp.zeros((SLICE, SIZE), F32)
    for p in range(BLOCKS):
        out_ref[p] = state
        state = decay * state + z_ref[p]


def prefix(slope, z, reverse):
    shape = (BLOCKS, SLICE, SIZE)
    if not reverse:
        return call(prefix_near_kernel, "prefix", [("smem", slope), ("vmem", z)], [("vmem", shape, F32)])[0]
    (out,) = call(
        functools.partial(prefix_kernel, reverse),
        "prefix",
        [("smem", slope), ("vmem", z)],
        [("hbm", shape, F32)],
        [pltpu.VMEM(shape, F32), dma(4)],
    )
    return out


def output_kernel(slope_ref, q_ref, u_ref, gain_ref, e_ref, loc, o_ref, sums_ref, sq, dt, sums):
    done = rows_of((LENGTH, SIZE), 1)
    for h in range(HEADS):
        decay_in = jnp.exp(-rate_of(slope_ref, h) * done)
        o_ref[h] = decay_in * dot(q_ref[h], e_ref[h].astype(BF16), NN)
    for r in range(0, LENGTH, 32):
        rows = pl.ds(r, 32)
        square = product = None
        for h in range(HEADS):
            out = o_ref[h, rows, :] + loc[h, rows, :]
            o_ref[h, rows, :] = out
            scaled = gain_ref[h : h + 1, :] * u_ref[h, rows, :].astype(F32)
            square = out * out if h == 0 else square + out * out
            product = out * scaled if h == 0 else product + out * scaled
        sq[rows, :] = square
        dt[rows, :] = product
    for b in range(4):
        rows = slice(b * 128, (b + 1) * 128)
        sums[b : b + 1, :] = jnp.sum(sq[rows, :].T, axis=0, keepdims=True)
        sums[4 + b : 5 + b, :] = jnp.sum(dt[rows, :].T, axis=0, keepdims=True)
    for i in range(sums_ref.shape[0]):
        sums_ref[i] = sums[...]


def outputs(slope, q, u, gain, e, loc, peers):
    return call(
        output_kernel,
        "outputs",
        [("smem", slope), ("vmem", q), ("vmem", u), ("vmem", gain), ("vmem", e), ("vmem", loc)],
        [("vmem", ROWS, F32), ("vmem", (peers, 8, SIZE), F32)],
        [
            pltpu.VMEM((LENGTH, SIZE), F32),
            pltpu.VMEM((LENGTH, SIZE), F32),
            pltpu.VMEM((8, SIZE), F32),
        ],
    )


def grad_kernel(sums_ref, wq_ref, u_ref, gain_ref, o_ref, g_hbm, s_hbm, g, s, sems):
    peers = sums_ref.shape[0]
    features = float(peers * HEADS * SIZE)
    sums = sums_ref[0]
    for i in range(1, peers):
        sums = sums + sums_ref[i]
    root = lax.rsqrt(sums[0:4, :] * (1.0 / features) + 1e-06)
    factor = root * root * root * sums[4:8, :] * (1.0 / features)
    writes = []
    for b in range(4):
        rows = pl.ds(b * 128, 128)
        inv = jnp.broadcast_to(root[b : b + 1, :], (128, 128)).T
        coef = jnp.broadcast_to(factor[b : b + 1, :], (128, 128)).T
        for h in range(HEADS):
            scaled = gain_ref[h : h + 1, :] * u_ref[h, rows, :].astype(F32)
            g[h, rows, :] = (inv * scaled - o_ref[h, rows, :] * coef).astype(BF16)
        writes.append(pltpu.make_async_copy(g.at[:, rows], g_hbm.at[:, rows], sems.at[b]))
        writes[-1].start()
    for h in range(HEADS):
        s[h] = dot(wq_ref[h], g[h], NN)
        if h % 4 == 3:
            writes.append(put(s, s_hbm, pl.ds(h - 3, 4), sems.at[4 + h // 4]))
    wait_all(writes)


def grads(sums, wq, u, gain, o):
    return call(
        grad_kernel,
        "grads",
        [("vmem", sums), ("vmem", wq), ("vmem", u), ("vmem", gain), ("vmem", o)],
        [("hbm", ROWS, BF16), ("hbm", STATE, F32)],
        [pltpu.VMEM(ROWS, BF16), pltpu.VMEM(STATE, F32), dma(6)],
    )


def query_kernel(slope_ref, g_hbm, k_hbm, v_hbm, e_hbm, out_hbm, g, k, v, e, wide, block, sems, e_sems, out_sems):
    e_copy = pltpu.make_async_copy(e_hbm, e, e_sems.at[0])
    e_copy.start()
    copies = fetch(((g_hbm, g), (k_hbm, k), (v_hbm, v)), sems)
    e_copy.wait()
    done = rows_of((LENGTH, SIZE), 1)
    for h in range(HEADS):
        await_head(copies, h)
        rate = rate_of(slope_ref, h)
        diag, off = masks(rate)
        g0, g1 = g[h, :256], g[h, 256:]
        k0, k1 = k[h, :256], k[h, 256:]
        v0, v1 = v[h, :256], v[h, 256:]
        b00 = (dot(g0, v0, NT) * diag).astype(BF16)
        b10 = (dot(g1, v0, NT) * off).astype(BF16)
        b11 = (dot(g1, v1, NT) * diag).astype(BF16)
        carried = jnp.exp(-rate * done) * dot(g[h], e[h].astype(BF16), NT)
        wide[pl.ds(h, 256, stride=HEADS), :] = dot(b00, k0, NN) + carried[:256]
        wide[pl.ds(h + 256 * HEADS, 256, stride=HEADS), :] = (
            dot(b10, k0, NN) + dot(b11, k1, NN) + carried[256:]
        )
    writes = []
    for p in range(PARTS):
        rows = pl.ds(p * CHUNK, CHUNK)
        block[rows] = wide[pl.ds(p * CHUNK * HEADS, CHUNK * HEADS), :].reshape(CHUNK, HEADS, SIZE).astype(BF16)
        writes.append(pltpu.make_async_copy(block.at[rows], out_hbm.at[rows], out_sems.at[p]))
        writes[-1].start()
    wait_all(writes)


def grad_query(slope, g, k, v, e):
    rows = pltpu.VMEM(ROWS, BF16)
    (out,) = call(
        query_kernel,
        "grad_query",
        [("smem", slope), ("hbm", g), ("hbm", k), ("hbm", v), ("any", e)],
        [("hbm", WHOLE, BF16)],
        [
            rows,
            rows,
            rows,
            pltpu.VMEM(STATE, F32),
            pltpu.VMEM((LENGTH * HEADS, SIZE), F32),
            pltpu.VMEM(WHOLE, BF16),
            dma(6),
            dma(1),
            dma(PARTS),
        ],
        flops=3 * 10**9,
        moved=5 * 2**20,
    )
    return out


def back_kernel(slope_ref, k_hbm, v_hbm, q_hbm, g_hbm, kl, vl, k, v, q, g, sems):
    copies = fetch(((k_hbm, k), (q_hbm, q), (g_hbm, g), (v_hbm, v)), sems)
    for h in range(HEADS):
        await_head(copies, h)
        diag, off = masks(rate_of(slope_ref, h), True)
        k0, k1 = k[h, :256], k[h, 256:]
        v0, v1 = v[h, :256], v[h, 256:]
        q0, q1 = q[h, :256], q[h, 256:]
        g0, g1 = g[h, :256], g[h, 256:]
        for a0, a1, b0, b1, c0, c1, to in (
            (k0, k1, q0, q1, g0, g1, vl),
            (v0, v1, g0, g1, q0, q1, kl),
        ):
            t00 = (dot(a0, b0, NT) * diag).astype(BF16)
            t01 = (dot(a0, b1, NT) * off).astype(BF16)
            t11 = (dot(a1, b1, NT) * diag).astype(BF16)
            to[h, :256] = (dot(t00, c0, NN) + dot(t01, c1, NN)).astype(BF16)
            to[h, 256:] = dot(t11, c1, NN).astype(BF16)


def back(slope, k, v, q, g):
    rows = pltpu.VMEM(ROWS, BF16)
    return call(
        back_kernel,
        "back",
        [("smem", slope), ("hbm", k), ("hbm", v), ("hbm", q), ("hbm", g)],
        [("vmem", ROWS, BF16), ("vmem", ROWS, BF16)],
        [rows, rows, rows, rows, dma(8)],
        flops=4 * 10**9,
        moved=8 * 2**20,
    )


def finish_kernel(slope_ref, k_hbm, v_hbm, kl_ref, vl_ref, l_ref, gk_hbm, gv_hbm, k, v, wk, wv, gk, gv, sems, out_sems):
    copies = [pltpu.make_async_copy(v_hbm, v, sems.at[0]), pltpu.make_async_copy(k_hbm, k, sems.at[1])]
    for c in copies:
        c.start()
    rates = [rate_of(slope_ref, h) for h in range(HEADS)]
    left = LENGTH - rows_of((LENGTH, SIZE))
    writes = []
    for n, (x, add, wide, out, to, dims) in enumerate(
        ((v, kl_ref, wk, gk, gk_hbm, NT), (k, vl_ref, wv, gv, gv_hbm, NN))
    ):
        copies[n].wait()
        for h in range(HEADS):
            moved = jnp.exp(-rates[h] * left) * dot(x[h], l_ref[h].astype(BF16), dims)
            wide[pl.ds(h, LENGTH, stride=HEADS), :] = add[h].astype(F32) + moved
        for p in range(2):
            rows = pl.ds(p * 256, 256)
            flat = pl.ds(p * 256 * HEADS, 256 * HEADS)
            out[rows] = wide[flat, :].reshape(256, HEADS, SIZE).astype(BF16)
            writes.append(put(out, to, rows, out_sems.at[2 * n + p]))
    wait_all(writes)


def finish(slope, k, v, kl, vl, l):
    wide = pltpu.VMEM((LENGTH * HEADS, SIZE), F32)
    rows, block = pltpu.VMEM(ROWS, BF16), pltpu.VMEM(WHOLE, BF16)
    return call(
        finish_kernel,
        "finish",
        [("smem", slope), ("hbm", k), ("hbm", v), ("vmem", kl), ("vmem", vl), ("vmem", l)],
        [("hbm", WHOLE, BF16), ("hbm", WHOLE, BF16)],
        [rows, rows, wide, wide, block, block, dma(2), dma(4)],
    )


def all_to_all(a):
    return lax.all_to_all(a.reshape(BLOCKS, SLICE, SIZE), "ctx", 0, 0, tiled=True)


def on_device(queries, key_rows, value_rows, upstream, norm_gain, slope_index):
    slope = slope_index

    states = key_states(slope, key_rows, value_rows)
    moved = all_to_all(states)
    loc, qh, kh, vh, uh, wq = local_part(slope, queries, key_rows, value_rows, upstream)
    moved, loc, qh, kh, vh, uh, wq = lax.optimization_barrier((moved, loc, qh, kh, vh, uh, wq))
    entering = all_to_all(prefix(slope, moved, False)).reshape(STATE)

    peers = lax.axis_size("head")
    out, sums = outputs(slope, qh, uh, norm_gain, entering, loc, peers)
    sums = lax.all_to_all(sums, "head", 0, 0, tiled=True)
    g, states = grads(sums, wq, uh, norm_gain, out)

    moved = all_to_all(states)
    gk_local, gv_local = back(slope, kh, vh, qh, g)
    moved, gk_local, gv_local = lax.optimization_barrier((moved, gk_local, gv_local))
    leaving = all_to_all(prefix(slope, moved, True)).reshape(STATE)
    gq = grad_query(slope, g, kh, vh, entering)
    leaving, gq = lax.optimization_barrier((leaving, gq))
    gk, gv = finish(slope, kh, vh, gk_local, gv_local, leaving)
    return gq, gk, gv


def solution(mesh):
    rows = P("ctx", "head", None)
    return jax.shard_map(
        on_device,
        mesh=mesh,
        in_specs=(rows, rows, rows, rows, P("head", None), P("head")),
        out_specs=(rows, rows, rows),
        check_vma=False,
    )
```

```python
import functools
import math

import jax
import jax.numpy as jnp
from jax import lax
from jax.experimental import pallas as pl
from jax.experimental.pallas import tpu as pltpu
from jax.sharding import PartitionSpec as P

F32 = jnp.float32
BF16 = jnp.bfloat16
LAYER_FACTOR = 1.0 - 78.0 / 79.0 + 1e-05
HEADS = 8
LENGTH = 512
SIZE = 128
HALF = 4
RING = 4
CHUNK = 128
PARTS = LENGTH // CHUNK
VMEM_LIMIT = 24 * 1024 * 1024

NN = ((1,), (0,))
NT = ((1,), (1,))
TN = ((0,), (0,))


def rate_of(slope_ref, head):
    slope = jnp.full((1, 1), slope_ref[head].astype(F32), F32)
    return jnp.exp((slope + 1.0) * (-8.0 / 64.0 * math.log(2.0))) * LAYER_FACTOR


def rows_of(shape, start=0):
    return (lax.broadcasted_iota(jnp.int32, shape, 0) + start).astype(F32)


def dot(a, b, dims):
    return lax.dot_general(a, b, (dims, ((), ())), preferred_element_type=F32)


def masks(rate, transposed=False):
    shape = (256, 256)
    gap = lax.broadcasted_iota(jnp.int32, shape, 0) - lax.broadcasted_iota(jnp.int32, shape, 1)
    if transposed:
        gap = -gap
    base = jnp.exp(-rate * gap.astype(F32))
    return jnp.where(gap >= 0, base, 0.0), base * jnp.exp(-256.0 * rate)


def hbm(x):
    return pltpu.with_memory_space_constraint(x, pltpu.HBM)


def near(x):
    return pltpu.with_memory_space_constraint(x, pltpu.VMEM)


def call(body, name, ins, outs, scratch=(), flops=0, moved=0):
    kinds = {"smem": pltpu.SMEM, "vmem": pltpu.VMEM, "hbm": pl.ANY, "any": pl.ANY}
    args, in_specs = [], []
    for kind, x in ins:
        in_specs.append(pl.BlockSpec(memory_space=kinds[kind]))
        args.append({"vmem": near, "hbm": hbm}.get(kind, lambda a: a)(x))
    out_shape, out_specs = [], []
    for kind, shape, dtype in outs:
        out_specs.append(pl.BlockSpec(memory_space=kinds[kind]))
        out_shape.append((pltpu.VMEM if kind == "vmem" else pltpu.HBM)(shape, dtype))
    return pl.pallas_call(
        body,
        in_specs=in_specs,
        out_specs=out_specs,
        out_shape=out_shape,
        scratch_shapes=list(scratch),
        compiler_params=pltpu.CompilerParams(vmem_limit_bytes=VMEM_LIMIT),
        cost_estimate=pl.CostEstimate(flops=flops, bytes_accessed=moved, transcendentals=0),
        name=name,
    )(*args)


STATE = (HEADS, SIZE, SIZE)
HALF_STATE = (HALF, SIZE, SIZE)
ONE = (SIZE, SIZE)
ROWS = (HEADS, LENGTH, SIZE)
WHOLE = (LENGTH, HEADS, SIZE)


def by_head(wide, part):
    return [wide[pl.ds(h + part * CHUNK * HEADS, CHUNK, stride=HEADS), :] for h in range(HEADS)]


def spread(wide, block, part):
    wide[pl.ds(part * CHUNK * HEADS, CHUNK * HEADS), :] = block.astype(F32).reshape(CHUNK * HEADS, SIZE)


def core_of():
    return lax.rem(lax.axis_index("ctx"), 2)


def x_of():
    return lax.rem(lax.axis_index("ctx") // 2, RING)


def y_of():
    return lax.axis_index("ctx") // (2 * RING)


def put(src, dst, part, sem):
    c = pltpu.make_async_copy(src.at[part], dst.at[part], sem)
    c.start()
    return c


def fetch_rows(src, dst, sems, base=0):
    return [put(src, dst, pl.ds(p * CHUNK, CHUNK), sems.at[base + p]) for p in range(PARTS)]


def wait_all(copies):
    for c in copies:
        c.wait()


def dma(count):
    return pltpu.SemaphoreType.DMA((count,))


def key_kernel(slope_hbm, k_hbm, v_hbm, keep_ref, send_ref, slope_ref, kin, vin, kw, vw, s, sems):
    first = pltpu.make_async_copy(slope_hbm, slope_ref, sems.at[2 * PARTS])
    first.start()
    k_copies = fetch_rows(k_hbm, kin, sems)
    v_copies = fetch_rows(v_hbm, vin, sems, PARTS)
    first.wait()
    rates = [rate_of(slope_ref, h) for h in range(HEADS)]
    for p in range(PARTS):
        rows = pl.ds(p * CHUNK, CHUNK)
        k_copies[p].wait()
        v_copies[p].wait()
        spread(kw, kin[rows], p)
        spread(vw, vin[rows], p)
        ks, vs = by_head(kw, p), by_head(vw, p)
        left = LENGTH - 1.0 - rows_of((CHUNK, SIZE), p * CHUNK)
        for h in range(HEADS):
            weighted = (ks[h] * jnp.exp(-rates[h] * left)).astype(BF16)
            part = dot(weighted, vs[h].astype(BF16), TN)
            s[h] = part if p == 0 else s[h] + part
    core = core_of()
    send_ref[...] = s[pl.ds((1 - core) * HALF, HALF)]
    keep_ref[...] = s[pl.ds(core * HALF, HALF)]


def key_states(slope, k, v):
    whole, wide = pltpu.VMEM(WHOLE, BF16), pltpu.VMEM((LENGTH * HEADS, SIZE), F32)
    return call(
        key_kernel,
        "key_states",
        [("hbm", slope), ("hbm", k), ("hbm", v)],
        [("vmem", HALF_STATE, F32), ("vmem", HALF_STATE, F32)],
        [pltpu.SMEM((HEADS,), jnp.int32), whole, whole, wide, wide, pltpu.VMEM(STATE, F32), dma(2 * PARTS + 1)],
    )


def turn_kernel(weigh, slope_ref, a_hbm, b_hbm, *refs):
    if weigh:
        q_ref, a_ref, b_ref, wq_ref, a_in, b_in, wide, sems = refs
    else:
        a_ref, b_ref, a_in, b_in, wide, sems = refs
    pairs = ((a_hbm, a_in, a_ref), (b_hbm, b_in, b_ref))
    copies = [fetch_rows(s, d, sems, i * PARTS) for i, (s, d, _) in enumerate(pairs)]
    if weigh:
        done = rows_of((LENGTH, SIZE))
        for h in range(HEADS):
            wq_ref[h] = (q_ref[h].astype(F32) * jnp.exp(-rate_of(slope_ref, h) * done)).T.astype(BF16)
    for i, (_, near_by, turned) in enumerate(pairs):
        for p in range(PARTS):
            rows = pl.ds(p * CHUNK, CHUNK)
            copies[i][p].wait()
            spread(wide.at[i], near_by[rows], p)
            for h, block in enumerate(by_head(wide.at[i], p)):
                turned[h, rows, :] = block.astype(BF16)


def turn(slope, a, b, q=None):
    whole = pltpu.VMEM(WHOLE, BF16)
    weigh = q is not None
    return call(
        functools.partial(turn_kernel, weigh),
        "turn",
        [("smem", slope), ("hbm", a), ("hbm", b)] + ([("vmem", q)] if weigh else []),
        [("vmem", ROWS, BF16)] * 2 + ([("vmem", (HEADS, SIZE, LENGTH), BF16)] if weigh else []),
        [whole, whole, pltpu.VMEM((2, LENGTH * HEADS, SIZE), F32), dma(2 * PARTS)],
        moved=8 * 2**20,
    )


def local_kernel(slope_ref, q_ref, k_ref, v_ref, loc_ref):
    for h in range(HEADS):
        diag, off = masks(rate_of(slope_ref, h))
        q0, q1 = q_ref[h, :256], q_ref[h, 256:]
        k0, k1 = k_ref[h, :256], k_ref[h, 256:]
        v0, v1 = v_ref[h, :256], v_ref[h, 256:]
        a00 = (dot(q0, k0, NT) * diag).astype(BF16)
        a10 = (dot(q1, k0, NT) * off).astype(BF16)
        a11 = (dot(q1, k1, NT) * diag).astype(BF16)
        loc_ref[h, :256] = dot(a00, v0, NN)
        loc_ref[h, 256:] = dot(a10, v0, NN) + dot(a11, v1, NN)


def local_part(slope, q, k, v):
    (out,) = call(
        local_kernel,
        "local_part",
        [("smem", slope), ("vmem", q), ("vmem", k), ("vmem", v)],
        [("vmem", ROWS, F32)],
        flops=2 * 10**9,
        moved=5 * 2**20,
    )
    return out


def decay_of(slope_ref, head, length):
    return jnp.exp(-float(length) * rate_of(slope_ref, head))


def around(place, d):
    return lax.rem(place + d + RING, RING)


def total_kernel(reverse, slope_ref, keep_ref, recv_ref, own_ref, to1, to2, to3, total):
    core, x = core_of(), x_of()
    flag = (core == 0) != reverse
    for h in range(HALF):
        decay = decay_of(slope_ref, core * HALF + h, LENGTH)
        total[h] = jnp.where(flag, decay, 1.0) * keep_ref[h] + jnp.where(flag, 1.0, decay) * recv_ref[h]
    own_ref[...] = total[x]
    for d, ref in ((1, to1), (2, to2), (3, to3)):
        ref[...] = total[around(x, d)]


def row_kernel(reverse, slope_ref, own_ref, from1, from2, from3, sum_ref, part_ref, held):
    x = x_of()
    decay = decay_of(slope_ref, core_of() * HALF + x, 2 * LENGTH)
    held[x] = own_ref[...]
    for d, ref in ((1, from1), (2, from2), (3, from3)):
        held[around(x, -d)] = ref[...]
    state = jnp.zeros(ONE, F32)
    for n in range(RING):
        place = RING - 1 - n if reverse else n
        part_ref[place] = state
        state = decay * state + held[place]
    sum_ref[...] = state


def column_kernel(reverse, slope_ref, own_ref, from1, from2, from3, part_ref, mine_ref, to1, to2, to3, held, done):
    x, y = x_of(), y_of()
    head = core_of() * HALF + x
    decay = decay_of(slope_ref, head, 2 * RING * LENGTH)
    held[y] = own_ref[...]
    for d, ref in ((1, from1), (2, from2), (3, from3)):
        held[around(y, -d)] = ref[...]
    state = jnp.zeros(ONE, F32)
    for n in range(RING - 1):
        place = RING - 1 - n if reverse else n
        before = place > y if reverse else place < y
        state = jnp.where(before, decay * state + held[place], state)
    for place in range(RING):
        steps = RING - 1 - place if reverse else place
        done[place] = decay_of(slope_ref, head, 2 * LENGTH * steps) * state + part_ref[place]
    mine_ref[...] = done[x]
    for d, ref in ((1, to1), (2, to2), (3, to3)):
        ref[...] = done[around(x, d)]


def after_kernel(reverse, slope_ref, own_ref, from1, from2, from3, keep_ref, recv_ref, out_ref, give_ref, held):
    core, x = core_of(), x_of()
    flag = (core == 0) != reverse
    held[x] = own_ref[...]
    for d, ref in ((1, from1), (2, from2), (3, from3)):
        held[around(x, -d)] = ref[...]
    for h in range(HALF):
        decay = decay_of(slope_ref, core * HALF + h, LENGTH)
        state = held[h]
        beyond = decay * state + jnp.where(flag, keep_ref[h], recv_ref[h])
        out_ref[h] = jnp.where(flag, state, beyond)
        give_ref[h] = jnp.where(flag, beyond, state)


def small(kernel, name, reverse, slope, ins, outs, scratch):
    return call(
        functools.partial(kernel, reverse),
        name,
        [("smem", slope)] + [("vmem", a) for a in ins],
        [("vmem", shape, F32) for shape in outs],
        [pltpu.VMEM(shape, F32) for shape in scratch],
    )


def states_of(own_ref, other_ref, state):
    core = core_of()
    state[pl.ds(core * HALF, HALF)] = own_ref[...].astype(BF16)
    state[pl.ds((1 - core) * HALF, HALF)] = other_ref[...].astype(BF16)


def output_kernel(slope_ref, q_ref, u_ref, gain_ref, own_ref, other_ref, loc, o_ref, sums_ref, state, sq, dt, sums):
    states_of(own_ref, other_ref, state)
    done = rows_of((LENGTH, SIZE), 1)
    for h in range(HEADS):
        decay_in = jnp.exp(-rate_of(slope_ref, h) * done)
        o_ref[h] = decay_in * dot(q_ref[h], state[h], NN)
    for r in range(0, LENGTH, 32):
        rows = pl.ds(r, 32)
        square = product = None
        for h in range(HEADS):
            out = o_ref[h, rows, :] + loc[h, rows, :]
            o_ref[h, rows, :] = out
            scaled = gain_ref[h : h + 1, :] * u_ref[h, rows, :].astype(F32)
            square = out * out if h == 0 else square + out * out
            product = out * scaled if h == 0 else product + out * scaled
        sq[rows, :] = square
        dt[rows, :] = product
    for b in range(4):
        rows = slice(b * 128, (b + 1) * 128)
        sums[b : b + 1, :] = jnp.sum(sq[rows, :].T, axis=0, keepdims=True)
        sums[4 + b : 5 + b, :] = jnp.sum(dt[rows, :].T, axis=0, keepdims=True)
    for i in range(sums_ref.shape[0]):
        sums_ref[i] = sums[...]


def outputs(slope, q, u, gain, own, other, loc, peers):
    return call(
        output_kernel,
        "outputs",
        [("smem", slope), ("vmem", q), ("vmem", u), ("vmem", gain), ("vmem", own), ("vmem", other), ("vmem", loc)],
        [("vmem", ROWS, F32), ("vmem", (peers, 8, SIZE), F32)],
        [
            pltpu.VMEM(STATE, BF16),
            pltpu.VMEM((LENGTH, SIZE), F32),
            pltpu.VMEM((LENGTH, SIZE), F32),
            pltpu.VMEM((8, SIZE), F32),
        ],
    )


def grad_kernel(sums_ref, wq_ref, u_ref, gain_ref, o_ref, g, keep_ref, send_ref, acc):
    peers = sums_ref.shape[0]
    features = float(peers * HEADS * SIZE)
    sums = sums_ref[0]
    for i in range(1, peers):
        sums = sums + sums_ref[i]
    root = lax.rsqrt(sums[0:4, :] * (1.0 / features) + 1e-06)
    factor = root * root * root * sums[4:8, :] * (1.0 / features)
    for b in range(4):
        rows = pl.ds(b * 128, 128)
        inv = jnp.broadcast_to(root[b : b + 1, :], (128, 128)).T
        coef = jnp.broadcast_to(factor[b : b + 1, :], (128, 128)).T
        for h in range(HEADS):
            scaled = gain_ref[h : h + 1, :] * u_ref[h, rows, :].astype(F32)
            g[h, rows, :] = (inv * scaled - o_ref[h, rows, :] * coef).astype(BF16)
    for h in range(HEADS):
        acc[h] = dot(wq_ref[h], g[h], NN)
    core = core_of()
    keep_ref[...] = acc[pl.ds(core * HALF, HALF)]
    send_ref[...] = acc[pl.ds((1 - core) * HALF, HALF)]


def grads(sums, wq, u, gain, o):
    return call(
        grad_kernel,
        "grads",
        [("vmem", sums), ("vmem", wq), ("vmem", u), ("vmem", gain), ("vmem", o)],
        [("vmem", ROWS, BF16), ("vmem", HALF_STATE, F32), ("vmem", HALF_STATE, F32)],
        [pltpu.VMEM(STATE, F32)],
    )


def query_kernel(slope_ref, g_ref, k_ref, v_ref, own_ref, other_ref, out_hbm, state, wide, block, sems):
    states_of(own_ref, other_ref, state)
    done = rows_of((LENGTH, SIZE), 1)
    for h in range(HEADS):
        rate = rate_of(slope_ref, h)
        diag, off = masks(rate)
        g0, g1 = g_ref[h, :256], g_ref[h, 256:]
        k0, k1 = k_ref[h, :256], k_ref[h, 256:]
        v0, v1 = v_ref[h, :256], v_ref[h, 256:]
        b00 = (dot(g0, v0, NT) * diag).astype(BF16)
        b10 = (dot(g1, v0, NT) * off).astype(BF16)
        b11 = (dot(g1, v1, NT) * diag).astype(BF16)
        carried = jnp.exp(-rate * done) * dot(g_ref[h], state[h], NT)
        wide[pl.ds(h, 256, stride=HEADS), :] = dot(b00, k0, NN) + carried[:256]
        wide[pl.ds(h + 256 * HEADS, 256, stride=HEADS), :] = (
            dot(b10, k0, NN) + dot(b11, k1, NN) + carried[256:]
        )
    copies = []
    for p in range(PARTS):
        rows = pl.ds(p * CHUNK, CHUNK)
        block[rows] = wide[pl.ds(p * CHUNK * HEADS, CHUNK * HEADS), :].reshape(CHUNK, HEADS, SIZE).astype(BF16)
        copies.append(put(block, out_hbm, rows, sems.at[p]))
    wait_all(copies)


def grad_query(slope, g, k, v, own, other):
    (out,) = call(
        query_kernel,
        "grad_query",
        [("smem", slope), ("vmem", g), ("vmem", k), ("vmem", v), ("vmem", own), ("vmem", other)],
        [("hbm", WHOLE, BF16)],
        [
            pltpu.VMEM((HEADS, SIZE, SIZE), BF16),
            pltpu.VMEM((LENGTH * HEADS, SIZE), F32),
            pltpu.VMEM(WHOLE, BF16),
            dma(PARTS),
        ],
        flops=3 * 10**9,
        moved=5 * 2**20,
    )
    return out


def back_kernel(slope_ref, a_ref, b_ref, c_ref, out_ref):
    for h in range(HEADS):
        diag, off = masks(rate_of(slope_ref, h), True)
        a0, a1 = a_ref[h, :256], a_ref[h, 256:]
        b0, b1 = b_ref[h, :256], b_ref[h, 256:]
        c0, c1 = c_ref[h, :256], c_ref[h, 256:]
        t00 = (dot(a0, b0, NT) * diag).astype(BF16)
        t01 = (dot(a0, b1, NT) * off).astype(BF16)
        t11 = (dot(a1, b1, NT) * diag).astype(BF16)
        out_ref[h, :256] = (dot(t00, c0, NN) + dot(t01, c1, NN)).astype(BF16)
        out_ref[h, 256:] = dot(t11, c1, NN).astype(BF16)


def back(slope, a, b, c, name):
    (out,) = call(
        back_kernel,
        name,
        [("smem", slope), ("vmem", a), ("vmem", b), ("vmem", c)],
        [("vmem", ROWS, BF16)],
        flops=2 * 10**9,
        moved=5 * 2**20,
    )
    return out


def finish_kernel(slope_ref, k, v, kl_ref, vl_ref, own_ref, other_ref, gk_hbm, gv_hbm, state, wk, wv, gk, gv, out_sems):
    states_of(own_ref, other_ref, state)
    rates = [rate_of(slope_ref, h) for h in range(HEADS)]
    left = LENGTH - rows_of((LENGTH, SIZE))
    writes = []
    for n, (x, add, wide, out, to, dims) in enumerate(
        ((v, kl_ref, wk, gk, gk_hbm, NT), (k, vl_ref, wv, gv, gv_hbm, NN))
    ):
        for h in range(HEADS):
            moved = jnp.exp(-rates[h] * left) * dot(x[h], state[h], dims)
            wide[pl.ds(h, LENGTH, stride=HEADS), :] = add[h].astype(F32) + moved
        for p in range(2):
            rows = pl.ds(p * 256, 256)
            flat = pl.ds(p * 256 * HEADS, 256 * HEADS)
            out[rows] = wide[flat, :].reshape(256, HEADS, SIZE).astype(BF16)
            writes.append(put(out, to, rows, out_sems.at[2 * n + p]))
    wait_all(writes)


def finish(slope, k, v, kl, vl, own, other):
    wide = pltpu.VMEM((LENGTH * HEADS, SIZE), F32)
    block = pltpu.VMEM(WHOLE, BF16)
    return call(
        finish_kernel,
        "finish",
        [("smem", slope), ("vmem", k), ("vmem", v), ("vmem", kl), ("vmem", vl), ("vmem", own), ("vmem", other)],
        [("hbm", WHOLE, BF16), ("hbm", WHOLE, BF16)],
        [pltpu.VMEM(STATE, BF16), wide, wide, block, block, dma(4)],
    )


def permute(a, dy, dx, dc):
    pairs = []
    for y in range(RING):
        for x in range(RING):
            for c in range(2):
                to = ((y + dy) % RING * RING + (x + dx) % RING) * 2 + (c ^ dc)
                pairs.append(((y * RING + x) * 2 + c, to))
    return lax.ppermute(a, "ctx", pairs)


def exchange(a):
    return permute(a, 0, 0, 1)


def along_x(parts):
    return [permute(a, 0, d + 1, 0) for d, a in enumerate(parts)]


def along_y(a):
    return [permute(a, d, 0, 0) for d in (1, 2, 3)]


def beside(moved, work):
    out = lax.optimization_barrier((tuple(moved), tuple(work)))
    return list(out[0]), list(out[1])


def scan(slope, keep, send, reverse, first, second, third):
    recv = exchange(send)
    one = [ONE] * 4
    own, *parts = small(total_kernel, "chip_total", reverse, slope, [keep, recv], one, [HALF_STATE])
    moved = along_x(parts)
    moved, done1 = beside(moved, first())
    row, part = small(row_kernel, "row_sum", reverse, slope, [own, *moved], [ONE, HALF_STATE], [HALF_STATE])
    moved = along_y(row)
    moved, done2 = beside(moved, second(done1))
    own, *parts = small(
        column_kernel, "column_sum", reverse, slope, [row, *moved, part], one, [HALF_STATE, HALF_STATE]
    )
    moved = along_x(parts)
    moved, done3 = beside(moved, third(done1, done2))
    mine, give = small(
        after_kernel, "after", reverse, slope, [own, *moved, keep, recv], [HALF_STATE] * 2, [HALF_STATE]
    )
    return mine, exchange(give), done1, done2, done3


def on_device(queries, key_rows, value_rows, upstream, norm_gain, slope_index):
    slope = slope_index

    keep, send = key_states(slope, key_rows, value_rows)
    e_own, e_other, (qh, kh), (vh, uh, wq), (loc,) = scan(
        slope,
        keep,
        send,
        False,
        lambda: turn(slope, queries, key_rows),
        lambda a: turn(slope, value_rows, upstream, a[0]),
        lambda a, b: [local_part(slope, a[0], a[1], b[0])],
    )

    peers = lax.axis_size("head")
    out, sums = outputs(slope, qh, uh, norm_gain, e_own, e_other, loc, peers)
    sums = lax.all_to_all(sums, "head", 0, 0, tiled=True)
    g, keep, send = grads(sums, wq, uh, norm_gain, out)

    l_own, l_other, (gv_local,), (gk_local,), (gq,) = scan(
        slope,
        keep,
        send,
        True,
        lambda: [back(slope, kh, qh, g, "gv_local")],
        lambda a: [back(slope, vh, g, qh, "gk_local")],
        lambda a, b: [grad_query(slope, g, kh, vh, e_own, e_other)],
    )
    gk, gv = finish(slope, kh, vh, gk_local, gv_local, l_own, l_other)
    return gq, gk, gv


def solution(mesh):
    rows = P("ctx", "head", None)
    return jax.shard_map(
        on_device,
        mesh=mesh,
        in_specs=(rows, rows, rows, rows, P("head", None), P("head")),
        out_specs=(rows, rows, rows),
        check_vma=False,
    )
```

```python
import functools
import math

import jax
import jax.numpy as jnp
from jax import lax
from jax.experimental import pallas as pl
from jax.experimental.pallas import tpu as pltpu
from jax.sharding import PartitionSpec as P

F32 = jnp.float32
BF16 = jnp.bfloat16
LAYER_FACTOR = 1.0 - 78.0 / 79.0 + 1e-05
HEADS = 8
LENGTH = 512
SIZE = 128
HALF = 4
RING = 4
CHUNK = 128
PARTS = LENGTH // CHUNK
VMEM_LIMIT = 24 * 1024 * 1024

NN = ((1,), (0,))
NT = ((1,), (1,))
TN = ((0,), (0,))


def rate_of(rates_ref, head):
    return rates_ref[head][:1, :1]


def rows_of(shape, start=0):
    return (lax.broadcasted_iota(jnp.int32, shape, 0) + start).astype(F32)


def dot(a, b, dims):
    return lax.dot_general(a, b, (dims, ((), ())), preferred_element_type=F32)


def masks(rate, transposed=False):
    shape = (256, 256)
    gap = lax.broadcasted_iota(jnp.int32, shape, 0) - lax.broadcasted_iota(jnp.int32, shape, 1)
    if transposed:
        gap = -gap
    base = jnp.exp(-rate * gap.astype(F32))
    return jnp.where(gap >= 0, base, 0.0), base * jnp.exp(-256.0 * rate)


def hbm(x):
    return pltpu.with_memory_space_constraint(x, pltpu.HBM)


def near(x):
    return pltpu.with_memory_space_constraint(x, pltpu.VMEM)


def call(body, name, ins, outs, scratch=(), flops=0, moved=0, aliases=None):
    kinds = {"vmem": pltpu.VMEM, "hbm": pl.ANY}
    args, in_specs = [], []
    for kind, x in ins:
        in_specs.append(pl.BlockSpec(memory_space=kinds[kind]))
        args.append({"vmem": near, "hbm": hbm}[kind](x))
    out_shape, out_specs = [], []
    for kind, shape, dtype in outs:
        out_specs.append(pl.BlockSpec(memory_space=kinds[kind]))
        out_shape.append((pltpu.VMEM if kind == "vmem" else pltpu.HBM)(shape, dtype))
    return pl.pallas_call(
        body,
        in_specs=in_specs,
        out_specs=out_specs,
        out_shape=out_shape,
        scratch_shapes=list(scratch),
        input_output_aliases=aliases or {},
        compiler_params=pltpu.CompilerParams(vmem_limit_bytes=VMEM_LIMIT),
        cost_estimate=pl.CostEstimate(flops=flops, bytes_accessed=moved, transcendentals=0),
        name=name,
    )(*args)


STATE = (HEADS, SIZE, SIZE)
HALF_STATE = (HALF, SIZE, SIZE)
RATES = (HEADS, 8, SIZE)
WIDE = (LENGTH * HEADS, SIZE)
ONE = (SIZE, SIZE)
ROWS = (HEADS, LENGTH, SIZE)
WHOLE = (LENGTH, HEADS, SIZE)


def by_head(wide, part):
    return [wide[pl.ds(h + part * CHUNK * HEADS, CHUNK, stride=HEADS), :] for h in range(HEADS)]


def spread(wide, block, part):
    wide[pl.ds(part * CHUNK * HEADS, CHUNK * HEADS), :] = block.astype(F32).reshape(CHUNK * HEADS, SIZE)


def core_of():
    return lax.rem(lax.axis_index("ctx"), 2)


def x_of():
    return lax.rem(lax.axis_index("ctx") // 2, RING)


def y_of():
    return lax.axis_index("ctx") // (2 * RING)


def put(src, dst, part, sem):
    c = pltpu.make_async_copy(src.at[part], dst.at[part], sem)
    c.start()
    return c


def fetch_rows(src, dst, sems, base=0):
    return [put(src, dst, pl.ds(p * CHUNK, CHUNK), sems.at[base + p]) for p in range(PARTS)]


def wait_all(copies):
    for c in copies:
        c.wait()


def dma(count):
    return pltpu.SemaphoreType.DMA((count,))


def half_states(kw, vw, rates_ref, first_head, rows, left, s):
    start, count = rows
    for j in range(HALF):
        strided = pl.ds(first_head + j + start * HEADS, count, stride=HEADS)
        weight = jnp.exp(-rate_of(rates_ref, first_head + j) * left)
        part = dot((kw[strided, :] * weight).astype(BF16), vw[strided, :].astype(BF16), TN)
        s[j] = part if start == 0 else s[j] + part


def send_kernel(slope_hbm, k_hbm, v_hbm, send_ref, kw, vw, rates_ref, slope_ref, kin, vin, sems):
    first = pltpu.make_async_copy(slope_hbm, slope_ref, sems.at[2 * PARTS])
    first.start()
    k_copies = fetch_rows(k_hbm, kin, sems)
    v_copies = fetch_rows(v_hbm, vin, sems, PARTS)
    first.wait()
    for h in range(HEADS):
        slope = jnp.full((8, SIZE), slope_ref[h].astype(F32), F32)
        rates_ref[h] = jnp.exp((slope + 1.0) * (-8.0 / 64.0 * math.log(2.0))) * LAYER_FACTOR
    other = (1 - core_of()) * HALF
    for p in range(PARTS):
        rows = pl.ds(p * CHUNK, CHUNK)
        k_copies[p].wait()
        v_copies[p].wait()
        spread(kw, kin[rows], p)
        spread(vw, vin[rows], p)
        left = LENGTH - 1.0 - rows_of((CHUNK, SIZE), p * CHUNK)
        half_states(kw, vw, rates_ref, other, (p * CHUNK, CHUNK), left, send_ref)


def send_states(slope, k, v):
    whole = pltpu.VMEM(WHOLE, BF16)
    return call(
        send_kernel,
        "send_states",
        [("hbm", slope), ("hbm", k), ("hbm", v)],
        [("vmem", HALF_STATE, F32), ("vmem", WIDE, F32), ("vmem", WIDE, F32), ("vmem", RATES, F32)],
        [pltpu.SMEM((HEADS,), jnp.int32), whole, whole, dma(2 * PARTS + 1)],
    )


def keep_kernel(rates_ref, kw, vw, keep_ref):
    left = LENGTH - 1.0 - rows_of((LENGTH, SIZE))
    half_states(kw, vw, rates_ref, core_of() * HALF, (0, LENGTH), left, keep_ref)


def keep_states(rates, kw, vw):
    (out,) = call(
        keep_kernel,
        "keep_states",
        [("vmem", rates), ("vmem", kw), ("vmem", vw)],
        [("vmem", HALF_STATE, F32)],
        flops=2 * 10**9,
        moved=4 * 2**20,
    )
    return out


def turn_kernel(weigh, rates_ref, a_wide, b_hbm, *refs):
    if weigh:
        q_ref, a_ref, b_ref, wq_ref, b_in, wide, sems = refs
    else:
        a_ref, b_ref, b_in, wide, sems = refs
    copies = fetch_rows(b_hbm, b_in, sems)
    if weigh:
        done = rows_of((LENGTH, SIZE))
        for h in range(HEADS):
            wq_ref[h] = (q_ref[h].astype(F32) * jnp.exp(-rate_of(rates_ref, h) * done)).T.astype(BF16)
    for p in range(PARTS):
        rows = pl.ds(p * CHUNK, CHUNK)
        for h, block in enumerate(by_head(a_wide, p)):
            a_ref[h, rows, :] = block.astype(BF16)
    for p in range(PARTS):
        rows = pl.ds(p * CHUNK, CHUNK)
        copies[p].wait()
        spread(wide, b_in[rows], p)
        for h, block in enumerate(by_head(wide, p)):
            b_ref[h, rows, :] = block.astype(BF16)


def turn(rates, a_wide, b, q=None):
    weigh = q is not None
    return call(
        functools.partial(turn_kernel, weigh),
        "turn",
        [("vmem", rates), ("vmem", a_wide), ("hbm", b)] + ([("vmem", q)] if weigh else []),
        [("vmem", ROWS, BF16)] * 2 + ([("vmem", (HEADS, SIZE, LENGTH), BF16)] if weigh else []),
        [pltpu.VMEM(WHOLE, BF16), pltpu.VMEM(WIDE, F32), dma(PARTS)],
        moved=8 * 2**20,
    )


def local_kernel(rates_ref, q_ref, k_ref, v_ref, loc_ref):
    for h in range(HEADS):
        diag, off = masks(rate_of(rates_ref, h))
        q0, q1 = q_ref[h, :256], q_ref[h, 256:]
        k0, k1 = k_ref[h, :256], k_ref[h, 256:]
        v0, v1 = v_ref[h, :256], v_ref[h, 256:]
        a00 = (dot(q0, k0, NT) * diag).astype(BF16)
        a10 = (dot(q1, k0, NT) * off).astype(BF16)
        a11 = (dot(q1, k1, NT) * diag).astype(BF16)
        loc_ref[h, :256] = dot(a00, v0, NN)
        loc_ref[h, 256:] = dot(a10, v0, NN) + dot(a11, v1, NN)


def local_part(rates, q, k, v):
    (out,) = call(
        local_kernel,
        "local_part",
        [("vmem", rates), ("vmem", q), ("vmem", k), ("vmem", v)],
        [("vmem", ROWS, F32)],
        flops=2 * 10**9,
        moved=5 * 2**20,
    )
    return out


def decay_of(rates_ref, head, length):
    return jnp.exp(-float(length) * rate_of(rates_ref, head))


def around(place, d):
    return lax.rem(place + d + RING, RING)


def total_kernel(reverse, rates_ref, keep_ref, recv_ref, own_ref, to1, to2, to3, total):
    core, x = core_of(), x_of()
    flag = (core == 0) != reverse
    for h in range(HALF):
        decay = decay_of(rates_ref, core * HALF + h, LENGTH)
        total[h] = jnp.where(flag, decay, 1.0) * keep_ref[h] + jnp.where(flag, 1.0, decay) * recv_ref[h]
    own_ref[...] = total[x]
    for d, ref in ((1, to1), (2, to2), (3, to3)):
        ref[...] = total[around(x, d)]


def row_kernel(reverse, rates_ref, own_ref, from1, from2, from3, sum_ref, part_ref, held):
    x = x_of()
    decay = decay_of(rates_ref, core_of() * HALF + x, 2 * LENGTH)
    held[x] = own_ref[...]
    for d, ref in ((1, from1), (2, from2), (3, from3)):
        held[around(x, -d)] = ref[...]
    state = jnp.zeros(ONE, F32)
    for n in range(RING):
        place = RING - 1 - n if reverse else n
        part_ref[place] = state
        state = decay * state + held[place]
    sum_ref[...] = state


def column_kernel(reverse, rates_ref, own_ref, from1, from2, from3, part_ref, mine_ref, to1, to2, to3, held, done):
    x, y = x_of(), y_of()
    head = core_of() * HALF + x
    decay = decay_of(rates_ref, head, 2 * RING * LENGTH)
    held[y] = own_ref[...]
    for d, ref in ((1, from1), (2, from2), (3, from3)):
        held[around(y, -d)] = ref[...]
    state = jnp.zeros(ONE, F32)
    for n in range(RING - 1):
        place = RING - 1 - n if reverse else n
        before = place > y if reverse else place < y
        state = jnp.where(before, decay * state + held[place], state)
    for place in range(RING):
        steps = RING - 1 - place if reverse else place
        done[place] = decay_of(rates_ref, head, 2 * LENGTH * steps) * state + part_ref[place]
    mine_ref[...] = done[x]
    for d, ref in ((1, to1), (2, to2), (3, to3)):
        ref[...] = done[around(x, d)]


def after_kernel(reverse, rates_ref, own_ref, from1, from2, from3, keep_ref, recv_ref, out_ref, give_ref, held):
    core, x = core_of(), x_of()
    flag = (core == 0) != reverse
    held[x] = own_ref[...]
    for d, ref in ((1, from1), (2, from2), (3, from3)):
        held[around(x, -d)] = ref[...]
    for h in range(HALF):
        decay = decay_of(rates_ref, core * HALF + h, LENGTH)
        state = held[h]
        beyond = decay * state + jnp.where(flag, keep_ref[h], recv_ref[h])
        out_ref[h] = jnp.where(flag, state, beyond)
        give_ref[h] = jnp.where(flag, beyond, state)


def small(kernel, name, reverse, rates, ins, outs, scratch):
    return call(
        functools.partial(kernel, reverse),
        name,
        [("vmem", rates)] + [("vmem", a) for a in ins],
        [("vmem", shape, F32) for shape in outs],
        [pltpu.VMEM(shape, F32) for shape in scratch],
    )


def states_of(own_ref, other_ref, state):
    core = core_of()
    state[pl.ds(core * HALF, HALF)] = own_ref[...].astype(BF16)
    state[pl.ds((1 - core) * HALF, HALF)] = other_ref[...].astype(BF16)


def half_outputs(rates_ref, q_ref, u_ref, gain_ref, state_ref, loc, first_head, o_ref, sq, dt, fresh):
    done = rows_of((LENGTH, SIZE), 1)
    for j in range(HALF):
        h = first_head + j
        decay_in = jnp.exp(-rate_of(rates_ref, h) * done)
        o_ref[j] = loc[h] + decay_in * dot(q_ref[h], state_ref[j].astype(BF16), NN)
    for r in range(0, LENGTH, 32):
        rows = pl.ds(r, 32)
        square, product = (None, None) if fresh else (sq[rows, :], dt[rows, :])
        for j in range(HALF):
            h = first_head + j
            out = o_ref[j, rows, :]
            scaled = gain_ref[pl.ds(h, 1), :] * u_ref[h, rows, :].astype(F32)
            square = out * out if square is None else square + out * out
            product = out * scaled if product is None else product + out * scaled
        sq[rows, :] = square
        dt[rows, :] = product


def own_output_kernel(rates_ref, q_ref, u_ref, gain_ref, state_ref, loc, o_ref, sq, dt):
    half_outputs(rates_ref, q_ref, u_ref, gain_ref, state_ref, loc, core_of() * HALF, o_ref, sq, dt, True)


def other_output_kernel(rates_ref, q_ref, u_ref, gain_ref, state_ref, loc, sq_ref, dt_ref, o_ref, sums_ref, sq, dt, sums):
    sq[...] = sq_ref[...]
    dt[...] = dt_ref[...]
    first_head = (1 - core_of()) * HALF
    half_outputs(rates_ref, q_ref, u_ref, gain_ref, state_ref, loc, first_head, o_ref, sq, dt, False)
    for b in range(4):
        rows = slice(b * 128, (b + 1) * 128)
        sums[b : b + 1, :] = jnp.sum(sq[rows, :].T, axis=0, keepdims=True)
        sums[4 + b : 5 + b, :] = jnp.sum(dt[rows, :].T, axis=0, keepdims=True)
    for i in range(sums_ref.shape[0]):
        sums_ref[i] = sums[...]


HALF_ROWS = (HALF, LENGTH, SIZE)


def own_outputs(rates, q, u, gain, state, loc):
    return call(
        own_output_kernel,
        "own_outputs",
        [("vmem", a) for a in (rates, q, u, gain, state, loc)],
        [("vmem", HALF_ROWS, F32), ("vmem", (LENGTH, SIZE), F32), ("vmem", (LENGTH, SIZE), F32)],
        flops=10**9,
        moved=4 * 2**20,
    )


def other_outputs(rates, q, u, gain, state, loc, sq, dt, peers):
    total = pltpu.VMEM((LENGTH, SIZE), F32)
    return call(
        other_output_kernel,
        "other_outputs",
        [("vmem", a) for a in (rates, q, u, gain, state, loc, sq, dt)],
        [("vmem", HALF_ROWS, F32), ("vmem", (peers, 8, SIZE), F32)],
        [total, total, pltpu.VMEM((8, SIZE), F32)],
    )


def grad_kernel(sums_ref, wq_ref, u_ref, gain_ref, own_ref, other_ref, g, keep_ref, send_ref, acc):
    core = core_of()
    peers = sums_ref.shape[0]
    features = float(peers * HEADS * SIZE)
    sums = sums_ref[0]
    for i in range(1, peers):
        sums = sums + sums_ref[i]
    root = lax.rsqrt(sums[0:4, :] * (1.0 / features) + 1e-06)
    factor = root * root * root * sums[4:8, :] * (1.0 / features)
    for b in range(4):
        rows = pl.ds(b * 128, 128)
        inv = jnp.broadcast_to(root[b : b + 1, :], (128, 128)).T
        coef = jnp.broadcast_to(factor[b : b + 1, :], (128, 128)).T
        for side, o_ref in ((core, own_ref), (1 - core, other_ref)):
            for j in range(HALF):
                h = side * HALF + j
                scaled = gain_ref[pl.ds(h, 1), :] * u_ref[h, rows, :].astype(F32)
                g[h, rows, :] = (inv * scaled - o_ref[j, rows, :] * coef).astype(BF16)
    for h in range(HEADS):
        acc[h] = dot(wq_ref[h], g[h], NN)
    keep_ref[...] = acc[pl.ds(core * HALF, HALF)]
    send_ref[...] = acc[pl.ds((1 - core) * HALF, HALF)]


def grads(sums, wq, u, gain, own, other):
    return call(
        grad_kernel,
        "grads",
        [("vmem", sums), ("vmem", wq), ("vmem", u), ("vmem", gain), ("vmem", own), ("vmem", other)],
        [("vmem", ROWS, BF16), ("vmem", HALF_STATE, F32), ("vmem", HALF_STATE, F32)],
        [pltpu.VMEM(STATE, F32)],
    )


def query_kernel(rates_ref, g_ref, k_ref, v_ref, own_ref, other_ref, out_hbm, state, wide, block, sems):
    states_of(own_ref, other_ref, state)
    done = rows_of((LENGTH, SIZE), 1)
    for h in range(HEADS):
        rate = rate_of(rates_ref, h)
        diag, off = masks(rate)
        g0, g1 = g_ref[h, :256], g_ref[h, 256:]
        k0, k1 = k_ref[h, :256], k_ref[h, 256:]
        v0, v1 = v_ref[h, :256], v_ref[h, 256:]
        b00 = (dot(g0, v0, NT) * diag).astype(BF16)
        b10 = (dot(g1, v0, NT) * off).astype(BF16)
        b11 = (dot(g1, v1, NT) * diag).astype(BF16)
        carried = jnp.exp(-rate * done) * dot(g_ref[h], state[h], NT)
        wide[pl.ds(h, 256, stride=HEADS), :] = dot(b00, k0, NN) + carried[:256]
        wide[pl.ds(h + 256 * HEADS, 256, stride=HEADS), :] = (
            dot(b10, k0, NN) + dot(b11, k1, NN) + carried[256:]
        )
    copies = []
    for p in range(PARTS):
        rows = pl.ds(p * CHUNK, CHUNK)
        block[rows] = wide[pl.ds(p * CHUNK * HEADS, CHUNK * HEADS), :].reshape(CHUNK, HEADS, SIZE).astype(BF16)
        copies.append(put(block, out_hbm, rows, sems.at[p]))
    wait_all(copies)


def grad_query(rates, g, k, v, own, other):
    (out,) = call(
        query_kernel,
        "grad_query",
        [("vmem", rates), ("vmem", g), ("vmem", k), ("vmem", v), ("vmem", own), ("vmem", other)],
        [("hbm", WHOLE, BF16)],
        [
            pltpu.VMEM((HEADS, SIZE, SIZE), BF16),
            pltpu.VMEM((LENGTH * HEADS, SIZE), F32),
            pltpu.VMEM(WHOLE, BF16),
            dma(PARTS),
        ],
        flops=3 * 10**9,
        moved=5 * 2**20,
    )
    return out


def back_kernel(rates_ref, a_ref, b_ref, c_ref, out_ref):
    for h in range(HEADS):
        diag, off = masks(rate_of(rates_ref, h), True)
        a0, a1 = a_ref[h, :256], a_ref[h, 256:]
        b0, b1 = b_ref[h, :256], b_ref[h, 256:]
        c0, c1 = c_ref[h, :256], c_ref[h, 256:]
        t00 = (dot(a0, b0, NT) * diag).astype(BF16)
        t01 = (dot(a0, b1, NT) * off).astype(BF16)
        t11 = (dot(a1, b1, NT) * diag).astype(BF16)
        out_ref[h, :256] = (dot(t00, c0, NN) + dot(t01, c1, NN)).astype(BF16)
        out_ref[h, 256:] = dot(t11, c1, NN).astype(BF16)


def back(rates, a, b, c, name):
    (out,) = call(
        back_kernel,
        name,
        [("vmem", rates), ("vmem", a), ("vmem", b), ("vmem", c)],
        [("vmem", ROWS, BF16)],
        flops=2 * 10**9,
        moved=5 * 2**20,
    )
    return out


def half_finish(rates_ref, k, v, kl_ref, vl_ref, state_ref, first_head, wk, wv):
    left = LENGTH - rows_of((LENGTH, SIZE))
    for x, add, wide, dims in ((v, kl_ref, wk, NT), (k, vl_ref, wv, NN)):
        for j in range(HALF):
            h = first_head + j
            moved = jnp.exp(-rate_of(rates_ref, h) * left) * dot(x[h], state_ref[j].astype(BF16), dims)
            wide[pl.ds(h, LENGTH, stride=HEADS), :] = add[h].astype(F32) + moved
        yield


def own_finish_kernel(rates_ref, k, v, kl_ref, vl_ref, state_ref, wk, wv):
    for _ in half_finish(rates_ref, k, v, kl_ref, vl_ref, state_ref, core_of() * HALF, wk, wv):
        pass


def other_finish_kernel(rates_ref, k, v, kl_ref, vl_ref, state_ref, wk_in, wv_in, gk_hbm, gv_hbm, wk, wv, gk, gv, sems):
    writes = []
    sides = ((wk, gk, gk_hbm), (wv, gv, gv_hbm))
    halves = half_finish(rates_ref, k, v, kl_ref, vl_ref, state_ref, (1 - core_of()) * HALF, wk, wv)
    for n, _ in enumerate(halves):
        wide, out, to = sides[n]
        for p in range(PARTS):
            rows = pl.ds(p * CHUNK, CHUNK)
            flat = pl.ds(p * CHUNK * HEADS, CHUNK * HEADS)
            out[rows] = wide[flat, :].reshape(CHUNK, HEADS, SIZE).astype(BF16)
            writes.append(put(out, to, rows, sems.at[PARTS * n + p]))
    wait_all(writes)


def own_finish(rates, k, v, kl, vl, state):
    return call(
        own_finish_kernel,
        "own_finish",
        [("vmem", a) for a in (rates, k, v, kl, vl, state)],
        [("vmem", WIDE, F32), ("vmem", WIDE, F32)],
        flops=10**9,
        moved=8 * 2**20,
    )


def other_finish(rates, k, v, kl, vl, state, wk, wv):
    block = pltpu.VMEM(WHOLE, BF16)
    return call(
        other_finish_kernel,
        "other_finish",
        [("vmem", a) for a in (rates, k, v, kl, vl, state, wk, wv)],
        [("hbm", WHOLE, BF16), ("hbm", WHOLE, BF16), ("vmem", WIDE, F32), ("vmem", WIDE, F32)],
        [block, block, dma(2 * PARTS)],
        aliases={6: 2, 7: 3},
    )[:2]


def permute(a, dy, dx, dc):
    pairs = []
    for y in range(RING):
        for x in range(RING):
            for c in range(2):
                to = ((y + dy) % RING * RING + (x + dx) % RING) * 2 + (c ^ dc)
                pairs.append(((y * RING + x) * 2 + c, to))
    return lax.ppermute(a, "ctx", pairs)


def exchange(a):
    return permute(a, 0, 0, 1)


def along_x(parts):
    return [permute(a, 0, d + 1, 0) for d, a in enumerate(parts)]


def along_y(a):
    return [permute(a, d, 0, 0) for d in (1, 2, 3)]


def beside(moved, work):
    out = lax.optimization_barrier((tuple(moved), tuple(work)))
    return list(out[0]), list(out[1])


def scan(rates, keep, send, reverse, first, second, third, last):
    recv = exchange(send)
    recv, keep = lax.optimization_barrier((recv, keep()))
    one = [ONE] * 4
    own, *parts = small(total_kernel, "chip_total", reverse, rates, [keep, recv], one, [HALF_STATE])
    moved = along_x(parts)
    moved, done1 = beside(moved, first())
    row, part = small(row_kernel, "row_sum", reverse, rates, [own, *moved], [ONE, HALF_STATE], [HALF_STATE])
    moved = along_y(row)
    moved, done2 = beside(moved, second(done1))
    own, *parts = small(
        column_kernel, "column_sum", reverse, rates, [row, *moved, part], one, [HALF_STATE, HALF_STATE]
    )
    moved = along_x(parts)
    moved, done3 = beside(moved, third(done1, done2))
    mine, give = small(
        after_kernel, "after", reverse, rates, [own, *moved, keep, recv], [HALF_STATE] * 2, [HALF_STATE]
    )
    (other,), done4 = beside([exchange(give)], last(mine, done1, done2, done3))
    return mine, other, done1, done2, done3, done4


def on_device(queries, key_rows, value_rows, upstream, norm_gain, slope_index):
    send, kw, vw, rates = send_states(slope_index, key_rows, value_rows)
    e_own, e_other, (kh, qh), (vh, uh, wq), (loc,), (out_own, sq, dt) = scan(
        rates,
        lambda: keep_states(rates, kw, vw),
        send,
        False,
        lambda: turn(rates, kw, queries),
        lambda a: turn(rates, vw, upstream, a[1]),
        lambda a, b: [local_part(rates, a[1], a[0], b[0])],
        lambda e, a, b, c: own_outputs(rates, a[1], b[1], norm_gain, e, c[0]),
    )

    peers = lax.axis_size("head")
    out_other, sums = other_outputs(rates, qh, uh, norm_gain, e_other, loc, sq, dt, peers)
    sums = lax.all_to_all(sums, "head", 0, 0, tiled=True)
    g, keep, send = grads(sums, wq, uh, norm_gain, out_own, out_other)

    l_own, l_other, (gv_local,), (gk_local,), (gq,), (wk, wv) = scan(
        rates,
        lambda: keep,
        send,
        True,
        lambda: [back(rates, kh, qh, g, "gv_local")],
        lambda a: [back(rates, vh, g, qh, "gk_local")],
        lambda a, b: [grad_query(rates, g, kh, vh, e_own, e_other)],
        lambda l, a, b, c: own_finish(rates, kh, vh, b[0], a[0], l),
    )
    gk, gv = other_finish(rates, kh, vh, gk_local, gv_local, l_other, wk, wv)
    return gq, gk, gv


def solution(mesh):
    rows = P("ctx", "head", None)
    return jax.shard_map(
        on_device,
        mesh=mesh,
        in_specs=(rows, rows, rows, rows, P("head", None), P("head")),
        out_specs=(rows, rows, rows),
        check_vma=False,
    )
```

```python
import functools
import math

import jax
import jax.numpy as jnp
from jax import lax
from jax.experimental import pallas as pl
from jax.experimental.pallas import tpu as pltpu
from jax.sharding import PartitionSpec as P

F32 = jnp.float32
BF16 = jnp.bfloat16
LAYER_FACTOR = 1.0 - 78.0 / 79.0 + 1e-05
HEADS = 8
LENGTH = 512
SIZE = 128
HALF = 4
RING = 4
CHUNK = 128
PARTS = LENGTH // CHUNK
VMEM_LIMIT = 24 * 1024 * 1024

NN = ((1,), (0,))
NT = ((1,), (1,))
TN = ((0,), (0,))


def rate_of(rates_ref, head):
    return rates_ref[head][:1, :1]


def rows_of(shape, start=0):
    return (lax.broadcasted_iota(jnp.int32, shape, 0) + start).astype(F32)


def dot(a, b, dims):
    return lax.dot_general(a, b, (dims, ((), ())), preferred_element_type=F32)


def masks(rate, transposed=False):
    shape = (256, 256)
    gap = lax.broadcasted_iota(jnp.int32, shape, 0) - lax.broadcasted_iota(jnp.int32, shape, 1)
    if transposed:
        gap = -gap
    base = jnp.exp(-rate * gap.astype(F32))
    return jnp.where(gap >= 0, base, 0.0), base * jnp.exp(-256.0 * rate)


def hbm(x):
    return pltpu.with_memory_space_constraint(x, pltpu.HBM)


def near(x):
    return pltpu.with_memory_space_constraint(x, pltpu.VMEM)


def call(body, name, ins, outs, scratch=(), flops=0, moved=0, aliases=None):
    kinds = {"vmem": pltpu.VMEM, "hbm": pl.ANY}
    args, in_specs = [], []
    for kind, x in ins:
        in_specs.append(pl.BlockSpec(memory_space=kinds[kind]))
        args.append({"vmem": near, "hbm": hbm}[kind](x))
    out_shape, out_specs = [], []
    for kind, shape, dtype in outs:
        out_specs.append(pl.BlockSpec(memory_space=kinds[kind]))
        out_shape.append((pltpu.VMEM if kind == "vmem" else pltpu.HBM)(shape, dtype))
    return pl.pallas_call(
        body,
        in_specs=in_specs,
        out_specs=out_specs,
        out_shape=out_shape,
        scratch_shapes=list(scratch),
        input_output_aliases=aliases or {},
        compiler_params=pltpu.CompilerParams(vmem_limit_bytes=VMEM_LIMIT),
        cost_estimate=pl.CostEstimate(flops=flops, bytes_accessed=moved, transcendentals=0),
        name=name,
    )(*args)


STATE = (HEADS, SIZE, SIZE)
HALF_STATE = (HALF, SIZE, SIZE)
RATES = (HEADS, 8, SIZE)
WIDE = (LENGTH * HEADS, SIZE)
ONE = (SIZE, SIZE)
ROWS = (HEADS, LENGTH, SIZE)
WHOLE = (LENGTH, HEADS, SIZE)


def by_head(wide, part):
    return [wide[pl.ds(h + part * CHUNK * HEADS, CHUNK, stride=HEADS), :] for h in range(HEADS)]


def spread(wide, block, part):
    wide[pl.ds(part * CHUNK * HEADS, CHUNK * HEADS), :] = block.astype(F32).reshape(CHUNK * HEADS, SIZE)


def core_of():
    return lax.rem(lax.axis_index("ctx"), 2)


def x_of():
    return lax.rem(lax.axis_index("ctx") // 2, RING)


def y_of():
    return lax.axis_index("ctx") // (2 * RING)


def put(src, dst, part, sem):
    c = pltpu.make_async_copy(src.at[part], dst.at[part], sem)
    c.start()
    return c


def fetch_rows(src, dst, sems, base=0):
    return [put(src, dst, pl.ds(p * CHUNK, CHUNK), sems.at[base + p]) for p in range(PARTS)]


def wait_all(copies):
    for c in copies:
        c.wait()


def dma(count):
    return pltpu.SemaphoreType.DMA((count,))


def half_states(kw, vw, rates_ref, first_head, rows, left, s):
    start, count = rows
    for j in range(HALF):
        strided = pl.ds(first_head + j + start * HEADS, count, stride=HEADS)
        weight = jnp.exp(-rate_of(rates_ref, first_head + j) * left)
        part = dot((kw[strided, :] * weight).astype(BF16), vw[strided, :].astype(BF16), TN)
        s[j] = part if start == 0 else s[j] + part


def send_kernel(slope_hbm, k_hbm, v_hbm, send_ref, kw, vw, rates_ref, slope_ref, kin, vin, sems):
    first = pltpu.make_async_copy(slope_hbm, slope_ref, sems.at[2 * PARTS])
    first.start()
    copies = []
    for p in range(PARTS):
        rows = pl.ds(p * CHUNK, CHUNK)
        copies.append((put(k_hbm, kin, rows, sems.at[p]), put(v_hbm, vin, rows, sems.at[PARTS + p])))
    first.wait()
    for h in range(HEADS):
        slope = jnp.full((8, SIZE), slope_ref[h].astype(F32), F32)
        rates_ref[h] = jnp.exp((slope + 1.0) * (-8.0 / 64.0 * math.log(2.0))) * LAYER_FACTOR
    other = (1 - core_of()) * HALF
    for p in range(PARTS):
        rows = pl.ds(p * CHUNK, CHUNK)
        wait_all(copies[p])
        spread(kw, kin[rows], p)
        spread(vw, vin[rows], p)
        left = LENGTH - 1.0 - rows_of((CHUNK, SIZE), p * CHUNK)
        half_states(kw, vw, rates_ref, other, (p * CHUNK, CHUNK), left, send_ref)


def send_states(slope, k, v):
    whole = pltpu.VMEM(WHOLE, BF16)
    return call(
        send_kernel,
        "send_states",
        [("hbm", slope), ("hbm", k), ("hbm", v)],
        [("vmem", HALF_STATE, F32), ("vmem", WIDE, F32), ("vmem", WIDE, F32), ("vmem", RATES, F32)],
        [pltpu.SMEM((HEADS,), jnp.int32), whole, whole, dma(2 * PARTS + 1)],
    )


def keep_kernel(rates_ref, kw, vw, keep_ref):
    left = LENGTH - 1.0 - rows_of((LENGTH, SIZE))
    half_states(kw, vw, rates_ref, core_of() * HALF, (0, LENGTH), left, keep_ref)


def keep_states(rates, kw, vw):
    (out,) = call(
        keep_kernel,
        "keep_states",
        [("vmem", rates), ("vmem", kw), ("vmem", vw)],
        [("vmem", HALF_STATE, F32)],
        flops=2 * 10**9,
        moved=4 * 2**20,
    )
    return out


def turn_kernel(weigh, rates_ref, a_wide, b_hbm, *refs):
    if weigh:
        q_ref, a_ref, b_ref, wq_ref, b_in, wide, sems = refs
    else:
        a_ref, b_ref, b_in, wide, sems = refs
    copies = fetch_rows(b_hbm, b_in, sems)
    if weigh:
        done = rows_of((LENGTH, SIZE))
        for h in range(HEADS):
            wq_ref[h] = (q_ref[h].astype(F32) * jnp.exp(-rate_of(rates_ref, h) * done)).T.astype(BF16)
    for p in range(PARTS):
        rows = pl.ds(p * CHUNK, CHUNK)
        for h, block in enumerate(by_head(a_wide, p)):
            a_ref[h, rows, :] = block.astype(BF16)
    for p in range(PARTS):
        rows = pl.ds(p * CHUNK, CHUNK)
        copies[p].wait()
        spread(wide, b_in[rows], p)
        for h, block in enumerate(by_head(wide, p)):
            b_ref[h, rows, :] = block.astype(BF16)


def turn(rates, a_wide, b, q=None):
    weigh = q is not None
    return call(
        functools.partial(turn_kernel, weigh),
        "turn",
        [("vmem", rates), ("vmem", a_wide), ("hbm", b)] + ([("vmem", q)] if weigh else []),
        [("vmem", ROWS, BF16)] * 2 + ([("vmem", (HEADS, SIZE, LENGTH), BF16)] if weigh else []),
        [pltpu.VMEM(WHOLE, BF16), pltpu.VMEM(WIDE, F32), dma(PARTS)],
        moved=8 * 2**20,
    )


def local_kernel(rates_ref, q_ref, k_ref, v_ref, loc_ref):
    for h in range(HEADS):
        diag, off = masks(rate_of(rates_ref, h))
        q0, q1 = q_ref[h, :256], q_ref[h, 256:]
        k0, k1 = k_ref[h, :256], k_ref[h, 256:]
        v0, v1 = v_ref[h, :256], v_ref[h, 256:]
        a00 = (dot(q0, k0, NT) * diag).astype(BF16)
        a10 = (dot(q1, k0, NT) * off).astype(BF16)
        a11 = (dot(q1, k1, NT) * diag).astype(BF16)
        loc_ref[h, :256] = dot(a00, v0, NN)
        loc_ref[h, 256:] = dot(a10, v0, NN) + dot(a11, v1, NN)


def local_part(rates, q, k, v):
    (out,) = call(
        local_kernel,
        "local_part",
        [("vmem", rates), ("vmem", q), ("vmem", k), ("vmem", v)],
        [("vmem", ROWS, F32)],
        flops=2 * 10**9,
        moved=5 * 2**20,
    )
    return out


def decay_of(rates_ref, head, length):
    return jnp.exp(-float(length) * rate_of(rates_ref, head))


def around(place, d):
    return lax.rem(place + d + RING, RING)


def total_kernel(reverse, rates_ref, keep_ref, recv_ref, own_ref, to1, to2, to3, total):
    core, x = core_of(), x_of()
    flag = (core == 0) != reverse
    for h in range(HALF):
        decay = decay_of(rates_ref, core * HALF + h, LENGTH)
        total[h] = jnp.where(flag, decay, 1.0) * keep_ref[h] + jnp.where(flag, 1.0, decay) * recv_ref[h]
    own_ref[...] = total[x]
    for d, ref in ((1, to1), (2, to2), (3, to3)):
        ref[...] = total[around(x, d)]


def row_kernel(reverse, rates_ref, own_ref, from1, from2, from3, sum_ref, part_ref, held):
    x = x_of()
    decay = decay_of(rates_ref, core_of() * HALF + x, 2 * LENGTH)
    held[x] = own_ref[...]
    for d, ref in ((1, from1), (2, from2), (3, from3)):
        held[around(x, -d)] = ref[...]
    state = jnp.zeros(ONE, F32)
    for n in range(RING):
        place = RING - 1 - n if reverse else n
        part_ref[place] = state
        state = decay * state + held[place]
    sum_ref[...] = state


def column_kernel(reverse, rates_ref, own_ref, from1, from2, from3, part_ref, mine_ref, to1, to2, to3, held, done):
    x, y = x_of(), y_of()
    head = core_of() * HALF + x
    decay = decay_of(rates_ref, head, 2 * RING * LENGTH)
    held[y] = own_ref[...]
    for d, ref in ((1, from1), (2, from2), (3, from3)):
        held[around(y, -d)] = ref[...]
    state = jnp.zeros(ONE, F32)
    for n in range(RING - 1):
        place = RING - 1 - n if reverse else n
        before = place > y if reverse else place < y
        state = jnp.where(before, decay * state + held[place], state)
    for place in range(RING):
        steps = RING - 1 - place if reverse else place
        done[place] = decay_of(rates_ref, head, 2 * LENGTH * steps) * state + part_ref[place]
    mine_ref[...] = done[x]
    for d, ref in ((1, to1), (2, to2), (3, to3)):
        ref[...] = done[around(x, d)]


def after_kernel(reverse, rates_ref, own_ref, from1, from2, from3, keep_ref, recv_ref, out_ref, give_ref, held):
    core, x = core_of(), x_of()
    flag = (core == 0) != reverse
    held[x] = own_ref[...]
    for d, ref in ((1, from1), (2, from2), (3, from3)):
        held[around(x, -d)] = ref[...]
    for h in range(HALF):
        decay = decay_of(rates_ref, core * HALF + h, LENGTH)
        state = held[h]
        beyond = decay * state + jnp.where(flag, keep_ref[h], recv_ref[h])
        out_ref[h] = jnp.where(flag, state, beyond)
        give_ref[h] = jnp.where(flag, beyond, state)


def small(kernel, name, reverse, rates, ins, outs, scratch):
    return call(
        functools.partial(kernel, reverse),
        name,
        [("vmem", rates)] + [("vmem", a) for a in ins],
        [("vmem", shape, F32) for shape in outs],
        [pltpu.VMEM(shape, F32) for shape in scratch],
    )


def states_of(own_ref, other_ref, state):
    core = core_of()
    state[pl.ds(core * HALF, HALF)] = own_ref[...].astype(BF16)
    state[pl.ds((1 - core) * HALF, HALF)] = other_ref[...].astype(BF16)


def half_outputs(rates_ref, q_ref, u_ref, gain_ref, state_ref, loc, first_head, o_ref, sq, dt, fresh):
    done = rows_of((LENGTH, SIZE), 1)
    for j in range(HALF):
        h = first_head + j
        decay_in = jnp.exp(-rate_of(rates_ref, h) * done)
        o_ref[j] = loc[h] + decay_in * dot(q_ref[h], state_ref[j].astype(BF16), NN)
    for r in range(0, LENGTH, 32):
        rows = pl.ds(r, 32)
        square, product = (None, None) if fresh else (sq[rows, :], dt[rows, :])
        for j in range(HALF):
            h = first_head + j
            out = o_ref[j, rows, :]
            scaled = gain_ref[pl.ds(h, 1), :] * u_ref[h, rows, :].astype(F32)
            square = out * out if square is None else square + out * out
            product = out * scaled if product is None else product + out * scaled
        sq[rows, :] = square
        dt[rows, :] = product


def own_output_kernel(rates_ref, q_ref, u_ref, gain_ref, state_ref, loc, o_ref, sq, dt):
    half_outputs(rates_ref, q_ref, u_ref, gain_ref, state_ref, loc, core_of() * HALF, o_ref, sq, dt, True)


def other_output_kernel(rates_ref, q_ref, u_ref, gain_ref, state_ref, loc, sq_ref, dt_ref, o_ref, sums_ref, sq, dt, sums):
    sq[...] = sq_ref[...]
    dt[...] = dt_ref[...]
    first_head = (1 - core_of()) * HALF
    half_outputs(rates_ref, q_ref, u_ref, gain_ref, state_ref, loc, first_head, o_ref, sq, dt, False)
    for b in range(4):
        rows = slice(b * 128, (b + 1) * 128)
        sums[b : b + 1, :] = jnp.sum(sq[rows, :].T, axis=0, keepdims=True)
        sums[4 + b : 5 + b, :] = jnp.sum(dt[rows, :].T, axis=0, keepdims=True)
    for i in range(sums_ref.shape[0]):
        sums_ref[i] = sums[...]


HALF_ROWS = (HALF, LENGTH, SIZE)


def own_outputs(rates, q, u, gain, state, loc):
    return call(
        own_output_kernel,
        "own_outputs",
        [("vmem", a) for a in (rates, q, u, gain, state, loc)],
        [("vmem", HALF_ROWS, F32), ("vmem", (LENGTH, SIZE), F32), ("vmem", (LENGTH, SIZE), F32)],
        flops=10**9,
        moved=4 * 2**20,
    )


def other_outputs(rates, q, u, gain, state, loc, sq, dt, peers):
    total = pltpu.VMEM((LENGTH, SIZE), F32)
    return call(
        other_output_kernel,
        "other_outputs",
        [("vmem", a) for a in (rates, q, u, gain, state, loc, sq, dt)],
        [("vmem", HALF_ROWS, F32), ("vmem", (peers, 8, SIZE), F32)],
        [total, total, pltpu.VMEM((8, SIZE), F32)],
    )


def half_grads(sums_ref, wq_ref, u_ref, gain_ref, o_ref, side, g, s):
    peers = sums_ref.shape[0]
    features = float(peers * HEADS * SIZE)
    sums = sums_ref[0]
    for i in range(1, peers):
        sums = sums + sums_ref[i]
    root = lax.rsqrt(sums[0:4, :] * (1.0 / features) + 1e-06)
    factor = root * root * root * sums[4:8, :] * (1.0 / features)
    for b in range(4):
        rows = pl.ds(b * 128, 128)
        inv = jnp.broadcast_to(root[b : b + 1, :], (128, 128)).T
        coef = jnp.broadcast_to(factor[b : b + 1, :], (128, 128)).T
        for j in range(HALF):
            h = side * HALF + j
            scaled = gain_ref[pl.ds(h, 1), :] * u_ref[h, rows, :].astype(F32)
            g[h, rows, :] = (inv * scaled - o_ref[j, rows, :] * coef).astype(BF16)
    for j in range(HALF):
        h = side * HALF + j
        s[j] = dot(wq_ref[h], g[h], NN)


def send_grad_kernel(sums_ref, wq_ref, u_ref, gain_ref, o_ref, g, s):
    half_grads(sums_ref, wq_ref, u_ref, gain_ref, o_ref, 1 - core_of(), g, s)


def keep_grad_kernel(sums_ref, wq_ref, u_ref, gain_ref, o_ref, g_in, g, s):
    half_grads(sums_ref, wq_ref, u_ref, gain_ref, o_ref, core_of(), g, s)


def send_grads(sums, wq, u, gain, other):
    return call(
        send_grad_kernel,
        "send_grads",
        [("vmem", a) for a in (sums, wq, u, gain, other)],
        [("vmem", ROWS, BF16), ("vmem", HALF_STATE, F32)],
    )


def keep_grads(sums, wq, u, gain, own, g):
    return call(
        keep_grad_kernel,
        "keep_grads",
        [("vmem", a) for a in (sums, wq, u, gain, own, g)],
        [("vmem", ROWS, BF16), ("vmem", HALF_STATE, F32)],
        flops=10**9,
        moved=4 * 2**20,
        aliases={5: 0},
    )


def query_kernel(rates_ref, g_ref, k_ref, v_ref, own_ref, other_ref, out_hbm, state, wide, block, sems):
    states_of(own_ref, other_ref, state)
    done = rows_of((LENGTH, SIZE), 1)
    for h in range(HEADS):
        rate = rate_of(rates_ref, h)
        diag, off = masks(rate)
        g0, g1 = g_ref[h, :256], g_ref[h, 256:]
        k0, k1 = k_ref[h, :256], k_ref[h, 256:]
        v0, v1 = v_ref[h, :256], v_ref[h, 256:]
        b00 = (dot(g0, v0, NT) * diag).astype(BF16)
        b10 = (dot(g1, v0, NT) * off).astype(BF16)
        b11 = (dot(g1, v1, NT) * diag).astype(BF16)
        carried = jnp.exp(-rate * done) * dot(g_ref[h], state[h], NT)
        wide[pl.ds(h, 256, stride=HEADS), :] = dot(b00, k0, NN) + carried[:256]
        wide[pl.ds(h + 256 * HEADS, 256, stride=HEADS), :] = (
            dot(b10, k0, NN) + dot(b11, k1, NN) + carried[256:]
        )
    copies = []
    for p in range(PARTS):
        rows = pl.ds(p * CHUNK, CHUNK)
        block[rows] = wide[pl.ds(p * CHUNK * HEADS, CHUNK * HEADS), :].reshape(CHUNK, HEADS, SIZE).astype(BF16)
        copies.append(put(block, out_hbm, rows, sems.at[p]))
    wait_all(copies)


def grad_query(rates, g, k, v, own, other):
    (out,) = call(
        query_kernel,
        "grad_query",
        [("vmem", rates), ("vmem", g), ("vmem", k), ("vmem", v), ("vmem", own), ("vmem", other)],
        [("hbm", WHOLE, BF16)],
        [
            pltpu.VMEM((HEADS, SIZE, SIZE), BF16),
            pltpu.VMEM((LENGTH * HEADS, SIZE), F32),
            pltpu.VMEM(WHOLE, BF16),
            dma(PARTS),
        ],
        flops=3 * 10**9,
        moved=5 * 2**20,
    )
    return out


def back_kernel(rates_ref, a_ref, b_ref, c_ref, out_ref):
    for h in range(HEADS):
        diag, off = masks(rate_of(rates_ref, h), True)
        a0, a1 = a_ref[h, :256], a_ref[h, 256:]
        b0, b1 = b_ref[h, :256], b_ref[h, 256:]
        c0, c1 = c_ref[h, :256], c_ref[h, 256:]
        t00 = (dot(a0, b0, NT) * diag).astype(BF16)
        t01 = (dot(a0, b1, NT) * off).astype(BF16)
        t11 = (dot(a1, b1, NT) * diag).astype(BF16)
        out_ref[h, :256] = (dot(t00, c0, NN) + dot(t01, c1, NN)).astype(BF16)
        out_ref[h, 256:] = dot(t11, c1, NN).astype(BF16)


def back(rates, a, b, c, name):
    (out,) = call(
        back_kernel,
        name,
        [("vmem", rates), ("vmem", a), ("vmem", b), ("vmem", c)],
        [("vmem", ROWS, BF16)],
        flops=2 * 10**9,
        moved=5 * 2**20,
    )
    return out


def half_finish(rates_ref, k, v, kl_ref, vl_ref, state_ref, first_head, wk, wv):
    left = LENGTH - rows_of((LENGTH, SIZE))
    for x, add, wide, dims in ((v, kl_ref, wk, NT), (k, vl_ref, wv, NN)):
        for j in range(HALF):
            h = first_head + j
            moved = jnp.exp(-rate_of(rates_ref, h) * left) * dot(x[h], state_ref[j].astype(BF16), dims)
            wide[pl.ds(h, LENGTH, stride=HEADS), :] = add[h].astype(F32) + moved
        yield


def own_finish_kernel(rates_ref, k, v, kl_ref, vl_ref, state_ref, wk, wv):
    for _ in half_finish(rates_ref, k, v, kl_ref, vl_ref, state_ref, core_of() * HALF, wk, wv):
        pass


def other_finish_kernel(rates_ref, k, v, kl_ref, vl_ref, state_ref, wk_in, wv_in, gk_hbm, gv_hbm, wk, wv, gk, gv, sems):
    writes = []
    sides = ((wk, gk, gk_hbm), (wv, gv, gv_hbm))
    halves = half_finish(rates_ref, k, v, kl_ref, vl_ref, state_ref, (1 - core_of()) * HALF, wk, wv)
    for n, _ in enumerate(halves):
        wide, out, to = sides[n]
        for p in range(PARTS):
            rows = pl.ds(p * CHUNK, CHUNK)
            flat = pl.ds(p * CHUNK * HEADS, CHUNK * HEADS)
            out[rows] = wide[flat, :].reshape(CHUNK, HEADS, SIZE).astype(BF16)
            writes.append(put(out, to, rows, sems.at[PARTS * n + p]))
    wait_all(writes)


def own_finish(rates, k, v, kl, vl, state):
    return call(
        own_finish_kernel,
        "own_finish",
        [("vmem", a) for a in (rates, k, v, kl, vl, state)],
        [("vmem", WIDE, F32), ("vmem", WIDE, F32)],
        flops=10**9,
        moved=8 * 2**20,
    )


def other_finish(rates, k, v, kl, vl, state, wk, wv):
    block = pltpu.VMEM(WHOLE, BF16)
    return call(
        other_finish_kernel,
        "other_finish",
        [("vmem", a) for a in (rates, k, v, kl, vl, state, wk, wv)],
        [("hbm", WHOLE, BF16), ("hbm", WHOLE, BF16), ("vmem", WIDE, F32), ("vmem", WIDE, F32)],
        [block, block, dma(2 * PARTS)],
        aliases={6: 2, 7: 3},
    )[:2]


def permute(a, dy, dx, dc):
    pairs = []
    for y in range(RING):
        for x in range(RING):
            for c in range(2):
                to = ((y + dy) % RING * RING + (x + dx) % RING) * 2 + (c ^ dc)
                pairs.append(((y * RING + x) * 2 + c, to))
    return lax.ppermute(a, "ctx", pairs)


def exchange(a):
    return permute(a, 0, 0, 1)


def along_x(parts):
    return [permute(a, 0, d + 1, 0) for d, a in enumerate(parts)]


def along_y(a):
    return [permute(a, d, 0, 0) for d in (1, 2, 3)]


def beside(moved, work):
    out = lax.optimization_barrier((tuple(moved), tuple(work)))
    return list(out[0]), list(out[1])


def scan(rates, keep, send, reverse, first, second, third, last):
    recv = exchange(send)
    recv, (keep, *done0) = lax.optimization_barrier((recv, keep()))
    one = [ONE] * 4
    own, *parts = small(total_kernel, "chip_total", reverse, rates, [keep, recv], one, [HALF_STATE])
    moved = along_x(parts)
    moved, done1 = beside(moved, first(*done0))
    row, part = small(row_kernel, "row_sum", reverse, rates, [own, *moved], [ONE, HALF_STATE], [HALF_STATE])
    moved = along_y(row)
    moved, done2 = beside(moved, second(done1))
    own, *parts = small(
        column_kernel, "column_sum", reverse, rates, [row, *moved, part], one, [HALF_STATE, HALF_STATE]
    )
    moved = along_x(parts)
    moved, done3 = beside(moved, third(done1, done2))
    mine, give = small(
        after_kernel, "after", reverse, rates, [own, *moved, keep, recv], [HALF_STATE] * 2, [HALF_STATE]
    )
    (other,), done4 = beside([exchange(give)], last(mine, *done0, done1, done2, done3))
    return mine, other, done0, done1, done2, done3, done4


def on_device(queries, key_rows, value_rows, upstream, norm_gain, slope_index):
    send, kw, vw, rates = send_states(slope_index, key_rows, value_rows)
    e_own, e_other, _, (kh, qh), (vh, uh, wq), (loc,), (out_own, sq, dt) = scan(
        rates,
        lambda: [keep_states(rates, kw, vw)],
        send,
        False,
        lambda: turn(rates, kw, queries),
        lambda a: turn(rates, vw, upstream, a[1]),
        lambda a, b: [local_part(rates, a[1], a[0], b[0])],
        lambda e, a, b, c: own_outputs(rates, a[1], b[1], norm_gain, e, c[0]),
    )

    peers = lax.axis_size("head")
    out_other, sums = other_outputs(rates, qh, uh, norm_gain, e_other, loc, sq, dt, peers)
    sums = lax.all_to_all(sums, "head", 0, 0, tiled=True)
    g_part, send = send_grads(sums, wq, uh, norm_gain, out_other)

    def keep_part():
        g, keep = keep_grads(sums, wq, uh, norm_gain, out_own, g_part)
        return [keep, g]

    l_own, l_other, _, (gv_local, _), (gk_local,), (gq,), (wk, wv) = scan(
        rates,
        keep_part,
        send,
        True,
        lambda g: [back(rates, kh, qh, g, "gv_local"), g],
        lambda a: [back(rates, vh, a[1], qh, "gk_local")],
        lambda a, b: [grad_query(rates, a[1], kh, vh, e_own, e_other)],
        lambda l, g, a, b, c: own_finish(rates, kh, vh, b[0], a[0], l),
    )
    gk, gv = other_finish(rates, kh, vh, gk_local, gv_local, l_other, wk, wv)
    return gq, gk, gv


def solution(mesh):
    rows = P("ctx", "head", None)
    return jax.shard_map(
        on_device,
        mesh=mesh,
        in_specs=(rows, rows, rows, rows, P("head", None), P("head")),
        out_specs=(rows, rows, rows),
        check_vma=False,
    )
```

```python
import functools
import math

import jax
import jax.numpy as jnp
from jax import lax
from jax.experimental import pallas as pl
from jax.experimental.pallas import tpu as pltpu
from jax.sharding import PartitionSpec as P

F32 = jnp.float32
BF16 = jnp.bfloat16
LAYER_FACTOR = 1.0 - 78.0 / 79.0 + 1e-05
HEADS = 8
LENGTH = 512
SIZE = 128
HALF = 4
RING = 4
CHUNK = 128
PARTS = LENGTH // CHUNK
VMEM_LIMIT = 24 * 1024 * 1024

NN = ((1,), (0,))
NT = ((1,), (1,))
TN = ((0,), (0,))


def rate_of(rates_ref, head):
    return rates_ref[head][:1, :1]


def rows_of(shape, start=0):
    return (lax.broadcasted_iota(jnp.int32, shape, 0) + start).astype(F32)


def dot(a, b, dims):
    return lax.dot_general(a, b, (dims, ((), ())), preferred_element_type=F32)


def masks(rate, transposed=False):
    shape = (256, 256)
    gap = lax.broadcasted_iota(jnp.int32, shape, 0) - lax.broadcasted_iota(jnp.int32, shape, 1)
    if transposed:
        gap = -gap
    base = jnp.exp(-rate * gap.astype(F32))
    return jnp.where(gap >= 0, base, 0.0), base * jnp.exp(-256.0 * rate)


def hbm(x):
    return pltpu.with_memory_space_constraint(x, pltpu.HBM)


def near(x):
    return pltpu.with_memory_space_constraint(x, pltpu.VMEM)


def call(body, name, ins, outs, scratch=(), flops=0, moved=0, aliases=None):
    kinds = {"vmem": pltpu.VMEM, "hbm": pl.ANY}
    args, in_specs = [], []
    for kind, x in ins:
        in_specs.append(pl.BlockSpec(memory_space=kinds[kind]))
        args.append({"vmem": near, "hbm": hbm}[kind](x))
    out_shape, out_specs = [], []
    for kind, shape, dtype in outs:
        out_specs.append(pl.BlockSpec(memory_space=kinds[kind]))
        out_shape.append((pltpu.VMEM if kind == "vmem" else pltpu.HBM)(shape, dtype))
    return pl.pallas_call(
        body,
        in_specs=in_specs,
        out_specs=out_specs,
        out_shape=out_shape,
        scratch_shapes=list(scratch),
        input_output_aliases=aliases or {},
        compiler_params=pltpu.CompilerParams(vmem_limit_bytes=VMEM_LIMIT),
        cost_estimate=pl.CostEstimate(flops=flops, bytes_accessed=moved, transcendentals=0),
        name=name,
    )(*args)


STATE = (HEADS, SIZE, SIZE)
HALF_STATE = (HALF, SIZE, SIZE)
RATES = (HEADS, 8, SIZE)
WIDE = (LENGTH * HEADS, SIZE)
ONE = (SIZE, SIZE)
ROWS = (HEADS, LENGTH, SIZE)
WHOLE = (LENGTH, HEADS, SIZE)


def by_head(wide, part):
    return [wide[pl.ds(h + part * CHUNK * HEADS, CHUNK, stride=HEADS), :] for h in range(HEADS)]


def spread(wide, block, part):
    wide[pl.ds(part * CHUNK * HEADS, CHUNK * HEADS), :] = block.astype(F32).reshape(CHUNK * HEADS, SIZE)


def core_of():
    return lax.rem(lax.axis_index("ctx"), 2)


def x_of():
    return lax.rem(lax.axis_index("ctx") // 2, RING)


def y_of():
    return lax.axis_index("ctx") // (2 * RING)


def put(src, dst, part, sem):
    c = pltpu.make_async_copy(src.at[part], dst.at[part], sem)
    c.start()
    return c


def fetch_rows(src, dst, sems, base=0):
    return [put(src, dst, pl.ds(p * CHUNK, CHUNK), sems.at[base + p]) for p in range(PARTS)]


def wait_all(copies):
    for c in copies:
        c.wait()


def dma(count):
    return pltpu.SemaphoreType.DMA((count,))


def by_core(body):
    for core in range(2):
        pl.when(core_of() == core)(functools.partial(body, core))


def half_states(kw, vw, rates_ref, first_head, rows, left, s):
    start, count = rows
    for j in range(HALF):
        strided = pl.ds(first_head + j + start * HEADS, count, stride=HEADS)
        weight = jnp.exp(-rate_of(rates_ref, first_head + j) * left)
        part = dot((kw[strided, :] * weight).astype(BF16), vw[strided, :].astype(BF16), TN)
        s[j] = part if start == 0 else s[j] + part


def send_kernel(slope_hbm, k_hbm, v_hbm, send_ref, kw, vw, rates_ref, slope_ref, kin, vin, sems):
    first = pltpu.make_async_copy(slope_hbm, slope_ref, sems.at[2 * PARTS])
    first.start()
    copies = []
    for p in range(PARTS):
        rows = pl.ds(p * CHUNK, CHUNK)
        copies.append((put(k_hbm, kin, rows, sems.at[p]), put(v_hbm, vin, rows, sems.at[PARTS + p])))
    first.wait()
    for h in range(HEADS):
        slope = jnp.full((8, SIZE), slope_ref[h].astype(F32), F32)
        rates_ref[h] = jnp.exp((slope + 1.0) * (-8.0 / 64.0 * math.log(2.0))) * LAYER_FACTOR

    def form(core):
        for p in range(PARTS):
            rows = pl.ds(p * CHUNK, CHUNK)
            wait_all(copies[p])
            spread(kw, kin[rows], p)
            spread(vw, vin[rows], p)
            left = LENGTH - 1.0 - rows_of((CHUNK, SIZE), p * CHUNK)
            half_states(kw, vw, rates_ref, (1 - core) * HALF, (p * CHUNK, CHUNK), left, send_ref)

    by_core(form)


def send_states(slope, k, v):
    whole = pltpu.VMEM(WHOLE, BF16)
    return call(
        send_kernel,
        "send_states",
        [("hbm", slope), ("hbm", k), ("hbm", v)],
        [("vmem", HALF_STATE, F32), ("vmem", WIDE, F32), ("vmem", WIDE, F32), ("vmem", RATES, F32)],
        [pltpu.SMEM((HEADS,), jnp.int32), whole, whole, dma(2 * PARTS + 1)],
    )


def keep_kernel(rates_ref, kw, vw, keep_ref):
    left = LENGTH - 1.0 - rows_of((LENGTH, SIZE))
    by_core(lambda core: half_states(kw, vw, rates_ref, core * HALF, (0, LENGTH), left, keep_ref))


def keep_states(rates, kw, vw):
    (out,) = call(
        keep_kernel,
        "keep_states",
        [("vmem", rates), ("vmem", kw), ("vmem", vw)],
        [("vmem", HALF_STATE, F32)],
        flops=2 * 10**9,
        moved=4 * 2**20,
    )
    return out


def turn_kernel(weigh, rates_ref, a_wide, b_hbm, *refs):
    if weigh:
        q_ref, a_ref, b_ref, wq_ref, b_in, wide, sems = refs
    else:
        a_ref, b_ref, b_in, wide, sems = refs
    copies = fetch_rows(b_hbm, b_in, sems)
    if weigh:
        done = rows_of((LENGTH, SIZE))
        for h in range(HEADS):
            wq_ref[h] = (q_ref[h].astype(F32) * jnp.exp(-rate_of(rates_ref, h) * done)).T.astype(BF16)
    for p in range(PARTS):
        rows = pl.ds(p * CHUNK, CHUNK)
        for h, block in enumerate(by_head(a_wide, p)):
            a_ref[h, rows, :] = block.astype(BF16)
    for p in range(PARTS):
        rows = pl.ds(p * CHUNK, CHUNK)
        copies[p].wait()
        spread(wide, b_in[rows], p)
        for h, block in enumerate(by_head(wide, p)):
            b_ref[h, rows, :] = block.astype(BF16)


def turn(rates, a_wide, b, q=None):
    weigh = q is not None
    return call(
        functools.partial(turn_kernel, weigh),
        "turn",
        [("vmem", rates), ("vmem", a_wide), ("hbm", b)] + ([("vmem", q)] if weigh else []),
        [("vmem", ROWS, BF16)] * 2 + ([("vmem", (HEADS, SIZE, LENGTH), BF16)] if weigh else []),
        [pltpu.VMEM(WHOLE, BF16), pltpu.VMEM(WIDE, F32), dma(PARTS)],
        moved=8 * 2**20,
    )


def local_kernel(rates_ref, q_ref, k_ref, v_ref, loc_ref):
    for h in range(HEADS):
        diag, off = masks(rate_of(rates_ref, h))
        q0, q1 = q_ref[h, :256], q_ref[h, 256:]
        k0, k1 = k_ref[h, :256], k_ref[h, 256:]
        v0, v1 = v_ref[h, :256], v_ref[h, 256:]
        a00 = (dot(q0, k0, NT) * diag).astype(BF16)
        a10 = (dot(q1, k0, NT) * off).astype(BF16)
        a11 = (dot(q1, k1, NT) * diag).astype(BF16)
        loc_ref[h, :256] = dot(a00, v0, NN)
        loc_ref[h, 256:] = dot(a10, v0, NN) + dot(a11, v1, NN)


def local_part(rates, q, k, v):
    (out,) = call(
        local_kernel,
        "local_part",
        [("vmem", rates), ("vmem", q), ("vmem", k), ("vmem", v)],
        [("vmem", ROWS, F32)],
        flops=2 * 10**9,
        moved=5 * 2**20,
    )
    return out


def decay_of(rates_ref, head, length):
    return jnp.exp(-float(length) * rate_of(rates_ref, head))


def around(place, d):
    return lax.rem(place + d + RING, RING)


def total_kernel(reverse, rates_ref, keep_ref, recv_ref, own_ref, to1, to2, to3, total):
    core, x = core_of(), x_of()
    flag = (core == 0) != reverse
    for h in range(HALF):
        decay = decay_of(rates_ref, core * HALF + h, LENGTH)
        total[h] = jnp.where(flag, decay, 1.0) * keep_ref[h] + jnp.where(flag, 1.0, decay) * recv_ref[h]
    own_ref[...] = total[x]
    for d, ref in ((1, to1), (2, to2), (3, to3)):
        ref[...] = total[around(x, d)]


def row_kernel(reverse, rates_ref, own_ref, from1, from2, from3, sum_ref, part_ref, held):
    x = x_of()
    decay = decay_of(rates_ref, core_of() * HALF + x, 2 * LENGTH)
    held[x] = own_ref[...]
    for d, ref in ((1, from1), (2, from2), (3, from3)):
        held[around(x, -d)] = ref[...]
    state = jnp.zeros(ONE, F32)
    for n in range(RING):
        place = RING - 1 - n if reverse else n
        part_ref[place] = state
        state = decay * state + held[place]
    sum_ref[...] = state


def column_kernel(reverse, rates_ref, own_ref, from1, from2, from3, part_ref, mine_ref, to1, to2, to3, held, done):
    x, y = x_of(), y_of()
    head = core_of() * HALF + x
    decay = decay_of(rates_ref, head, 2 * RING * LENGTH)
    held[y] = own_ref[...]
    for d, ref in ((1, from1), (2, from2), (3, from3)):
        held[around(y, -d)] = ref[...]
    state = jnp.zeros(ONE, F32)
    for n in range(RING - 1):
        place = RING - 1 - n if reverse else n
        before = place > y if reverse else place < y
        state = jnp.where(before, decay * state + held[place], state)
    for place in range(RING):
        steps = RING - 1 - place if reverse else place
        done[place] = decay_of(rates_ref, head, 2 * LENGTH * steps) * state + part_ref[place]
    mine_ref[...] = done[x]
    for d, ref in ((1, to1), (2, to2), (3, to3)):
        ref[...] = done[around(x, d)]


def after_kernel(reverse, rates_ref, own_ref, from1, from2, from3, keep_ref, recv_ref, out_ref, give_ref, held):
    core, x = core_of(), x_of()
    flag = (core == 0) != reverse
    held[x] = own_ref[...]
    for d, ref in ((1, from1), (2, from2), (3, from3)):
        held[around(x, -d)] = ref[...]
    for h in range(HALF):
        decay = decay_of(rates_ref, core * HALF + h, LENGTH)
        state = held[h]
        beyond = decay * state + jnp.where(flag, keep_ref[h], recv_ref[h])
        out_ref[h] = jnp.where(flag, state, beyond)
        give_ref[h] = jnp.where(flag, beyond, state)


def small(kernel, name, reverse, rates, ins, outs, scratch):
    return call(
        functools.partial(kernel, reverse),
        name,
        [("vmem", rates)] + [("vmem", a) for a in ins],
        [("vmem", shape, F32) for shape in outs],
        [pltpu.VMEM(shape, F32) for shape in scratch],
    )


def states_of(own_ref, other_ref, state):
    core = core_of()
    state[pl.ds(core * HALF, HALF)] = own_ref[...].astype(BF16)
    state[pl.ds((1 - core) * HALF, HALF)] = other_ref[...].astype(BF16)


def half_outputs(rates_ref, q_ref, u_ref, gain_ref, state_ref, loc, first_head, o_ref, sq, dt, fresh):
    done = rows_of((LENGTH, SIZE), 1)
    for j in range(HALF):
        h = first_head + j
        decay_in = jnp.exp(-rate_of(rates_ref, h) * done)
        o_ref[j] = loc[h] + decay_in * dot(q_ref[h], state_ref[j].astype(BF16), NN)
    for r in range(0, LENGTH, 32):
        rows = pl.ds(r, 32)
        square, product = (None, None) if fresh else (sq[rows, :], dt[rows, :])
        for j in range(HALF):
            h = first_head + j
            out = o_ref[j, rows, :]
            scaled = gain_ref[pl.ds(h, 1), :] * u_ref[h, rows, :].astype(F32)
            square = out * out if square is None else square + out * out
            product = out * scaled if product is None else product + out * scaled
        sq[rows, :] = square
        dt[rows, :] = product


def own_output_kernel(rates_ref, q_ref, u_ref, gain_ref, state_ref, loc, o_ref, sq, dt):
    half_outputs(rates_ref, q_ref, u_ref, gain_ref, state_ref, loc, core_of() * HALF, o_ref, sq, dt, True)


def other_output_kernel(rates_ref, q_ref, u_ref, gain_ref, state_ref, loc, sq_ref, dt_ref, o_ref, sums_ref, sq, dt, sums):
    sq[...] = sq_ref[...]
    dt[...] = dt_ref[...]
    first_head = (1 - core_of()) * HALF
    half_outputs(rates_ref, q_ref, u_ref, gain_ref, state_ref, loc, first_head, o_ref, sq, dt, False)
    for b in range(4):
        rows = slice(b * 128, (b + 1) * 128)
        sums[b : b + 1, :] = jnp.sum(sq[rows, :].T, axis=0, keepdims=True)
        sums[4 + b : 5 + b, :] = jnp.sum(dt[rows, :].T, axis=0, keepdims=True)
    for i in range(sums_ref.shape[0]):
        sums_ref[i] = sums[...]


HALF_ROWS = (HALF, LENGTH, SIZE)


def own_outputs(rates, q, u, gain, state, loc):
    return call(
        own_output_kernel,
        "own_outputs",
        [("vmem", a) for a in (rates, q, u, gain, state, loc)],
        [("vmem", HALF_ROWS, F32), ("vmem", (LENGTH, SIZE), F32), ("vmem", (LENGTH, SIZE), F32)],
        flops=10**9,
        moved=4 * 2**20,
    )


def other_outputs(rates, q, u, gain, state, loc, sq, dt, peers):
    total = pltpu.VMEM((LENGTH, SIZE), F32)
    return call(
        other_output_kernel,
        "other_outputs",
        [("vmem", a) for a in (rates, q, u, gain, state, loc, sq, dt)],
        [("vmem", HALF_ROWS, F32), ("vmem", (peers, 8, SIZE), F32)],
        [total, total, pltpu.VMEM((8, SIZE), F32)],
    )


def half_grads(sums_ref, wq_ref, u_ref, gain_ref, o_ref, side, g, s):
    peers = sums_ref.shape[0]
    features = float(peers * HEADS * SIZE)
    sums = sums_ref[0]
    for i in range(1, peers):
        sums = sums + sums_ref[i]
    root = lax.rsqrt(sums[0:4, :] * (1.0 / features) + 1e-06)
    factor = root * root * root * sums[4:8, :] * (1.0 / features)
    for b in range(4):
        rows = pl.ds(b * 128, 128)
        inv = jnp.broadcast_to(root[b : b + 1, :], (128, 128)).T
        coef = jnp.broadcast_to(factor[b : b + 1, :], (128, 128)).T
        for j in range(HALF):
            h = side * HALF + j
            scaled = gain_ref[pl.ds(h, 1), :] * u_ref[h, rows, :].astype(F32)
            g[h, rows, :] = (inv * scaled - o_ref[j, rows, :] * coef).astype(BF16)
    for j in range(HALF):
        h = side * HALF + j
        s[j] = dot(wq_ref[h], g[h], NN)


def send_grad_kernel(sums_ref, wq_ref, u_ref, gain_ref, o_ref, g, s):
    half_grads(sums_ref, wq_ref, u_ref, gain_ref, o_ref, 1 - core_of(), g, s)


def keep_grad_kernel(sums_ref, wq_ref, u_ref, gain_ref, o_ref, g_in, g, s):
    half_grads(sums_ref, wq_ref, u_ref, gain_ref, o_ref, core_of(), g, s)


def send_grads(sums, wq, u, gain, other):
    return call(
        send_grad_kernel,
        "send_grads",
        [("vmem", a) for a in (sums, wq, u, gain, other)],
        [("vmem", ROWS, BF16), ("vmem", HALF_STATE, F32)],
    )


def keep_grads(sums, wq, u, gain, own, g):
    return call(
        keep_grad_kernel,
        "keep_grads",
        [("vmem", a) for a in (sums, wq, u, gain, own, g)],
        [("vmem", ROWS, BF16), ("vmem", HALF_STATE, F32)],
        flops=10**9,
        moved=4 * 2**20,
        aliases={5: 0},
    )


def query_kernel(rates_ref, g_ref, k_ref, v_ref, own_ref, other_ref, out_hbm, state, wide, block, sems):
    states_of(own_ref, other_ref, state)
    done = rows_of((LENGTH, SIZE), 1)
    for h in range(HEADS):
        rate = rate_of(rates_ref, h)
        diag, off = masks(rate)
        g0, g1 = g_ref[h, :256], g_ref[h, 256:]
        k0, k1 = k_ref[h, :256], k_ref[h, 256:]
        v0, v1 = v_ref[h, :256], v_ref[h, 256:]
        b00 = (dot(g0, v0, NT) * diag).astype(BF16)
        b10 = (dot(g1, v0, NT) * off).astype(BF16)
        b11 = (dot(g1, v1, NT) * diag).astype(BF16)
        carried = jnp.exp(-rate * done) * dot(g_ref[h], state[h], NT)
        wide[pl.ds(h, 256, stride=HEADS), :] = dot(b00, k0, NN) + carried[:256]
        wide[pl.ds(h + 256 * HEADS, 256, stride=HEADS), :] = (
            dot(b10, k0, NN) + dot(b11, k1, NN) + carried[256:]
        )
    copies = []
    for p in range(PARTS):
        rows = pl.ds(p * CHUNK, CHUNK)
        block[rows] = wide[pl.ds(p * CHUNK * HEADS, CHUNK * HEADS), :].reshape(CHUNK, HEADS, SIZE).astype(BF16)
        copies.append(put(block, out_hbm, rows, sems.at[p]))
    wait_all(copies)


def grad_query(rates, g, k, v, own, other):
    (out,) = call(
        query_kernel,
        "grad_query",
        [("vmem", rates), ("vmem", g), ("vmem", k), ("vmem", v), ("vmem", own), ("vmem", other)],
        [("hbm", WHOLE, BF16)],
        [
            pltpu.VMEM((HEADS, SIZE, SIZE), BF16),
            pltpu.VMEM((LENGTH * HEADS, SIZE), F32),
            pltpu.VMEM(WHOLE, BF16),
            dma(PARTS),
        ],
        flops=3 * 10**9,
        moved=5 * 2**20,
    )
    return out


def back_kernel(rates_ref, a_ref, b_ref, c_ref, out_ref):
    for h in range(HEADS):
        diag, off = masks(rate_of(rates_ref, h), True)
        a0, a1 = a_ref[h, :256], a_ref[h, 256:]
        b0, b1 = b_ref[h, :256], b_ref[h, 256:]
        c0, c1 = c_ref[h, :256], c_ref[h, 256:]
        t00 = (dot(a0, b0, NT) * diag).astype(BF16)
        t01 = (dot(a0, b1, NT) * off).astype(BF16)
        t11 = (dot(a1, b1, NT) * diag).astype(BF16)
        out_ref[h, :256] = (dot(t00, c0, NN) + dot(t01, c1, NN)).astype(BF16)
        out_ref[h, 256:] = dot(t11, c1, NN).astype(BF16)


def back(rates, a, b, c, name):
    (out,) = call(
        back_kernel,
        name,
        [("vmem", rates), ("vmem", a), ("vmem", b), ("vmem", c)],
        [("vmem", ROWS, BF16)],
        flops=2 * 10**9,
        moved=5 * 2**20,
    )
    return out


def half_finish(rates_ref, k, v, kl_ref, vl_ref, state_ref, first_head, wk, wv):
    left = LENGTH - rows_of((LENGTH, SIZE))
    for x, add, wide, dims in ((v, kl_ref, wk, NT), (k, vl_ref, wv, NN)):
        for j in range(HALF):
            h = first_head + j
            moved = jnp.exp(-rate_of(rates_ref, h) * left) * dot(x[h], state_ref[j].astype(BF16), dims)
            wide[pl.ds(h, LENGTH, stride=HEADS), :] = add[h].astype(F32) + moved
        yield


def own_finish_kernel(rates_ref, k, v, kl_ref, vl_ref, state_ref, wk, wv):
    def form(core):
        for _ in half_finish(rates_ref, k, v, kl_ref, vl_ref, state_ref, core * HALF, wk, wv):
            pass

    by_core(form)


def other_finish_kernel(rates_ref, k, v, kl_ref, vl_ref, state_ref, wk_in, wv_in, gk_hbm, gv_hbm, wk, wv, gk, gv, sems):
    sides = ((wk, gk, gk_hbm), (wv, gv, gv_hbm))

    def form(core):
        writes = []
        halves = half_finish(rates_ref, k, v, kl_ref, vl_ref, state_ref, (1 - core) * HALF, wk, wv)
        for n, _ in enumerate(halves):
            wide, out, to = sides[n]
            for p in range(PARTS):
                rows = pl.ds(p * CHUNK, CHUNK)
                flat = pl.ds(p * CHUNK * HEADS, CHUNK * HEADS)
                out[rows] = wide[flat, :].reshape(CHUNK, HEADS, SIZE).astype(BF16)
                writes.append(put(out, to, rows, sems.at[PARTS * n + p]))
        wait_all(writes)

    by_core(form)


def own_finish(rates, k, v, kl, vl, state):
    return call(
        own_finish_kernel,
        "own_finish",
        [("vmem", a) for a in (rates, k, v, kl, vl, state)],
        [("vmem", WIDE, F32), ("vmem", WIDE, F32)],
        flops=10**9,
        moved=8 * 2**20,
    )


def other_finish(rates, k, v, kl, vl, state, wk, wv):
    block = pltpu.VMEM(WHOLE, BF16)
    return call(
        other_finish_kernel,
        "other_finish",
        [("vmem", a) for a in (rates, k, v, kl, vl, state, wk, wv)],
        [("hbm", WHOLE, BF16), ("hbm", WHOLE, BF16), ("vmem", WIDE, F32), ("vmem", WIDE, F32)],
        [block, block, dma(2 * PARTS)],
        aliases={6: 2, 7: 3},
    )[:2]


def permute(a, dy, dx, dc):
    pairs = []
    for y in range(RING):
        for x in range(RING):
            for c in range(2):
                to = ((y + dy) % RING * RING + (x + dx) % RING) * 2 + (c ^ dc)
                pairs.append(((y * RING + x) * 2 + c, to))
    return lax.ppermute(a, "ctx", pairs)


def exchange(a):
    return permute(a, 0, 0, 1)


def along_x(parts):
    return [permute(a, 0, d + 1, 0) for d, a in enumerate(parts)]


def along_y(a):
    return [permute(a, d, 0, 0) for d in (1, 2, 3)]


def beside(moved, work):
    out = lax.optimization_barrier((tuple(moved), tuple(work)))
    return list(out[0]), list(out[1])


def scan(rates, keep, send, reverse, first, second, third, last):
    recv = exchange(send)
    recv, (keep, *done0) = lax.optimization_barrier((recv, keep()))
    one = [ONE] * 4
    own, *parts = small(total_kernel, "chip_total", reverse, rates, [keep, recv], one, [HALF_STATE])
    moved = along_x(parts)
    moved, done1 = beside(moved, first(*done0))
    row, part = small(row_kernel, "row_sum", reverse, rates, [own, *moved], [ONE, HALF_STATE], [HALF_STATE])
    moved = along_y(row)
    moved, done2 = beside(moved, second(done1))
    own, *parts = small(
        column_kernel, "column_sum", reverse, rates, [row, *moved, part], one, [HALF_STATE, HALF_STATE]
    )
    moved = along_x(parts)
    moved, done3 = beside(moved, third(done1, done2))
    mine, give = small(
        after_kernel, "after", reverse, rates, [own, *moved, keep, recv], [HALF_STATE] * 2, [HALF_STATE]
    )
    (other,), done4 = beside([exchange(give)], last(mine, *done0, done1, done2, done3))
    return mine, other, done0, done1, done2, done3, done4


def on_device(queries, key_rows, value_rows, upstream, norm_gain, slope_index):
    send, kw, vw, rates = send_states(slope_index, key_rows, value_rows)
    e_own, e_other, _, (kh, qh), (vh, uh, wq), (loc,), (out_own, sq, dt) = scan(
        rates,
        lambda: [keep_states(rates, kw, vw)],
        send,
        False,
        lambda: turn(rates, kw, queries),
        lambda a: turn(rates, vw, upstream, a[1]),
        lambda a, b: [local_part(rates, a[1], a[0], b[0])],
        lambda e, a, b, c: own_outputs(rates, a[1], b[1], norm_gain, e, c[0]),
    )

    peers = lax.axis_size("head")
    out_other, sums = other_outputs(rates, qh, uh, norm_gain, e_other, loc, sq, dt, peers)
    sums = lax.all_to_all(sums, "head", 0, 0, tiled=True)
    g_part, send = send_grads(sums, wq, uh, norm_gain, out_other)

    def keep_part():
        g, keep = keep_grads(sums, wq, uh, norm_gain, out_own, g_part)
        return [keep, g]

    l_own, l_other, _, (gv_local, _), (gk_local,), (gq,), (wk, wv) = scan(
        rates,
        keep_part,
        send,
        True,
        lambda g: [back(rates, kh, qh, g, "gv_local"), g],
        lambda a: [back(rates, vh, a[1], qh, "gk_local")],
        lambda a, b: [grad_query(rates, a[1], kh, vh, e_own, e_other)],
        lambda l, g, a, b, c: own_finish(rates, kh, vh, b[0], a[0], l),
    )
    gk, gv = other_finish(rates, kh, vh, gk_local, gv_local, l_other, wk, wv)
    return gq, gk, gv


def solution(mesh):
    rows = P("ctx", "head", None)
    return jax.shard_map(
        on_device,
        mesh=mesh,
        in_specs=(rows, rows, rows, rows, P("head", None), P("head")),
        out_specs=(rows, rows, rows),
        check_vma=False,
    )
```

```python
import functools
import math

import jax
import jax.numpy as jnp
from jax import lax
from jax.experimental import pallas as pl
from jax.experimental.pallas import tpu as pltpu
from jax.sharding import PartitionSpec as P

F32 = jnp.float32
BF16 = jnp.bfloat16
LAYER_FACTOR = 1.0 - 78.0 / 79.0 + 1e-05
HEADS = 8
LENGTH = 512
SIZE = 128
HALF = 4
RING = 4
CHUNK = 128
PARTS = LENGTH // CHUNK
VMEM_LIMIT = 24 * 1024 * 1024

NN = ((1,), (0,))
NT = ((1,), (1,))
TN = ((0,), (0,))


def rate_of(rates_ref, head):
    return rates_ref[head][:1, :1]


def rows_of(shape, start=0):
    return (lax.broadcasted_iota(jnp.int32, shape, 0) + start).astype(F32)


def dot(a, b, dims):
    return lax.dot_general(a, b, (dims, ((), ())), preferred_element_type=F32)


def masks(rate, transposed=False):
    shape = (256, 256)
    gap = lax.broadcasted_iota(jnp.int32, shape, 0) - lax.broadcasted_iota(jnp.int32, shape, 1)
    if transposed:
        gap = -gap
    base = jnp.exp(-rate * gap.astype(F32))
    return jnp.where(gap >= 0, base, 0.0), base * jnp.exp(-256.0 * rate)


def hbm(x):
    return pltpu.with_memory_space_constraint(x, pltpu.HBM)


def near(x):
    return pltpu.with_memory_space_constraint(x, pltpu.VMEM)


def call(body, name, ins, outs, scratch=(), flops=0, moved=0, aliases=None):
    kinds = {"vmem": pltpu.VMEM, "hbm": pl.ANY}
    args, in_specs = [], []
    for kind, x in ins:
        in_specs.append(pl.BlockSpec(memory_space=kinds[kind]))
        args.append({"vmem": near, "hbm": hbm}[kind](x))
    out_shape, out_specs = [], []
    for kind, shape, dtype in outs:
        out_specs.append(pl.BlockSpec(memory_space=kinds[kind]))
        out_shape.append((pltpu.VMEM if kind == "vmem" else pltpu.HBM)(shape, dtype))
    return pl.pallas_call(
        body,
        in_specs=in_specs,
        out_specs=out_specs,
        out_shape=out_shape,
        scratch_shapes=list(scratch),
        input_output_aliases=aliases or {},
        compiler_params=pltpu.CompilerParams(vmem_limit_bytes=VMEM_LIMIT),
        cost_estimate=pl.CostEstimate(flops=flops, bytes_accessed=moved, transcendentals=0),
        name=name,
    )(*args)


STATE = (HEADS, SIZE, SIZE)
HALF_STATE = (HALF, SIZE, SIZE)
RATES = (HEADS, 8, SIZE)
WIDE = (LENGTH * HEADS, SIZE)
ONE = (SIZE, SIZE)
ROWS = (HEADS, LENGTH, SIZE)
WHOLE = (LENGTH, HEADS, SIZE)


def by_head(wide, part):
    return [wide[pl.ds(h + part * CHUNK * HEADS, CHUNK, stride=HEADS), :] for h in range(HEADS)]


def spread(wide, block, part):
    wide[pl.ds(part * CHUNK * HEADS, CHUNK * HEADS), :] = block.astype(F32).reshape(CHUNK * HEADS, SIZE)


def core_of():
    return lax.rem(lax.axis_index("ctx"), 2)


def x_of():
    return lax.rem(lax.axis_index("ctx") // 2, RING)


def y_of():
    return lax.axis_index("ctx") // (2 * RING)


def put(src, dst, part, sem):
    c = pltpu.make_async_copy(src.at[part], dst.at[part], sem)
    c.start()
    return c


def fetch_rows(src, dst, sems, base=0):
    return [put(src, dst, pl.ds(p * CHUNK, CHUNK), sems.at[base + p]) for p in range(PARTS)]


def wait_all(copies):
    for c in copies:
        c.wait()


def dma(count):
    return pltpu.SemaphoreType.DMA((count,))


def by_core(body):
    for core in range(2):
        pl.when(core_of() == core)(functools.partial(body, core))


def half_states(kw, vw, rates_ref, first_head, rows, left, s):
    start, count = rows
    for j in range(HALF):
        strided = pl.ds(first_head + j + start * HEADS, count, stride=HEADS)
        weight = jnp.exp(-rate_of(rates_ref, first_head + j) * left)
        part = dot((kw[strided, :] * weight).astype(BF16), vw[strided, :].astype(BF16), TN)
        s[j] = part if start == 0 else s[j] + part


def send_kernel(slope_hbm, k_hbm, v_hbm, send_ref, kw, vw, rates_ref, slope_ref, kin, vin, sems):
    first = pltpu.make_async_copy(slope_hbm, slope_ref, sems.at[2 * PARTS])
    first.start()
    copies = []
    for p in range(PARTS):
        rows = pl.ds(p * CHUNK, CHUNK)
        copies.append((put(k_hbm, kin, rows, sems.at[p]), put(v_hbm, vin, rows, sems.at[PARTS + p])))
    first.wait()
    for h in range(HEADS):
        slope = jnp.full((8, SIZE), slope_ref[h].astype(F32), F32)
        rates_ref[h] = jnp.exp((slope + 1.0) * (-8.0 / 64.0 * math.log(2.0))) * LAYER_FACTOR

    def form(core):
        for p in range(PARTS):
            rows = pl.ds(p * CHUNK, CHUNK)
            wait_all(copies[p])
            spread(kw, kin[rows], p)
            spread(vw, vin[rows], p)
            left = LENGTH - 1.0 - rows_of((CHUNK, SIZE), p * CHUNK)
            half_states(kw, vw, rates_ref, (1 - core) * HALF, (p * CHUNK, CHUNK), left, send_ref)

    by_core(form)


def send_states(slope, k, v):
    whole = pltpu.VMEM(WHOLE, BF16)
    return call(
        send_kernel,
        "send_states",
        [("hbm", slope), ("hbm", k), ("hbm", v)],
        [("vmem", HALF_STATE, F32), ("vmem", WIDE, F32), ("vmem", WIDE, F32), ("vmem", RATES, F32)],
        [pltpu.SMEM((HEADS,), jnp.int32), whole, whole, dma(2 * PARTS + 1)],
    )


def keep_kernel(rates_ref, kw, vw, keep_ref):
    left = LENGTH - 1.0 - rows_of((LENGTH, SIZE))
    by_core(lambda core: half_states(kw, vw, rates_ref, core * HALF, (0, LENGTH), left, keep_ref))


def keep_states(rates, kw, vw):
    (out,) = call(
        keep_kernel,
        "keep_states",
        [("vmem", rates), ("vmem", kw), ("vmem", vw)],
        [("vmem", HALF_STATE, F32)],
        flops=2 * 10**9,
        moved=4 * 2**20,
    )
    return out


def turn_kernel(weigh, rates_ref, a_wide, b_hbm, *refs):
    if weigh:
        q_ref, a_ref, b_ref, wq_ref, b_in, wide, sems = refs
    else:
        a_ref, b_ref, b_in, wide, sems = refs
    copies = fetch_rows(b_hbm, b_in, sems)
    if weigh:
        done = rows_of((LENGTH, SIZE))
        for h in range(HEADS):
            wq_ref[h] = (q_ref[h].astype(F32) * jnp.exp(-rate_of(rates_ref, h) * done)).T.astype(BF16)
    for p in range(PARTS):
        rows = pl.ds(p * CHUNK, CHUNK)
        for h, block in enumerate(by_head(a_wide, p)):
            a_ref[h, rows, :] = block.astype(BF16)
    for p in range(PARTS):
        rows = pl.ds(p * CHUNK, CHUNK)
        copies[p].wait()
        spread(wide, b_in[rows], p)
        for h, block in enumerate(by_head(wide, p)):
            b_ref[h, rows, :] = block.astype(BF16)


def turn(rates, a_wide, b, q=None):
    weigh = q is not None
    return call(
        functools.partial(turn_kernel, weigh),
        "turn",
        [("vmem", rates), ("vmem", a_wide), ("hbm", b)] + ([("vmem", q)] if weigh else []),
        [("vmem", ROWS, BF16)] * 2 + ([("vmem", (HEADS, SIZE, LENGTH), BF16)] if weigh else []),
        [pltpu.VMEM(WHOLE, BF16), pltpu.VMEM(WIDE, F32), dma(PARTS)],
        moved=8 * 2**20,
    )


def local_kernel(rates_ref, q_ref, k_ref, v_ref, loc_ref):
    for h in range(HEADS):
        diag, off = masks(rate_of(rates_ref, h))
        q0, q1 = q_ref[h, :256], q_ref[h, 256:]
        k0, k1 = k_ref[h, :256], k_ref[h, 256:]
        v0, v1 = v_ref[h, :256], v_ref[h, 256:]
        a00 = (dot(q0, k0, NT) * diag).astype(BF16)
        a10 = (dot(q1, k0, NT) * off).astype(BF16)
        a11 = (dot(q1, k1, NT) * diag).astype(BF16)
        loc_ref[h, :256] = dot(a00, v0, NN)
        loc_ref[h, 256:] = dot(a10, v0, NN) + dot(a11, v1, NN)


def local_part(rates, q, k, v):
    (out,) = call(
        local_kernel,
        "local_part",
        [("vmem", rates), ("vmem", q), ("vmem", k), ("vmem", v)],
        [("vmem", ROWS, F32)],
        flops=2 * 10**9,
        moved=5 * 2**20,
    )
    return out


def decay_of(rates_ref, head, length):
    return jnp.exp(-float(length) * rate_of(rates_ref, head))


def around(place, d):
    return lax.rem(place + d + RING, RING)


def total_kernel(reverse, rates_ref, keep_ref, recv_ref, own_ref, to1, to2, to3, total):
    core, x = core_of(), x_of()
    flag = (core == 0) != reverse
    for h in range(HALF):
        decay = decay_of(rates_ref, core * HALF + h, LENGTH)
        total[h] = jnp.where(flag, decay, 1.0) * keep_ref[h] + jnp.where(flag, 1.0, decay) * recv_ref[h]
    own_ref[...] = total[x]
    for d, ref in ((1, to1), (2, to2), (3, to3)):
        ref[...] = total[around(x, d)]


def row_kernel(reverse, rates_ref, own_ref, from1, from2, from3, sum_ref, part_ref, held):
    x = x_of()
    decay = decay_of(rates_ref, core_of() * HALF + x, 2 * LENGTH)
    held[x] = own_ref[...]
    for d, ref in ((1, from1), (2, from2), (3, from3)):
        held[around(x, -d)] = ref[...]
    state = jnp.zeros(ONE, F32)
    for n in range(RING):
        place = RING - 1 - n if reverse else n
        part_ref[place] = state
        state = decay * state + held[place]
    sum_ref[...] = state


def column_kernel(reverse, rates_ref, own_ref, from1, from2, from3, part_ref, mine_ref, to1, to2, to3, held, done):
    x, y = x_of(), y_of()
    head = core_of() * HALF + x
    decay = decay_of(rates_ref, head, 2 * RING * LENGTH)
    held[y] = own_ref[...]
    for d, ref in ((1, from1), (2, from2), (3, from3)):
        held[around(y, -d)] = ref[...]
    state = jnp.zeros(ONE, F32)
    for n in range(RING - 1):
        place = RING - 1 - n if reverse else n
        before = place > y if reverse else place < y
        state = jnp.where(before, decay * state + held[place], state)
    for place in range(RING):
        steps = RING - 1 - place if reverse else place
        done[place] = decay_of(rates_ref, head, 2 * LENGTH * steps) * state + part_ref[place]
    mine_ref[...] = done[x]
    for d, ref in ((1, to1), (2, to2), (3, to3)):
        ref[...] = done[around(x, d)]


def after_kernel(reverse, rates_ref, own_ref, from1, from2, from3, keep_ref, recv_ref, out_ref, give_ref, held):
    core, x = core_of(), x_of()
    flag = (core == 0) != reverse
    held[x] = own_ref[...]
    for d, ref in ((1, from1), (2, from2), (3, from3)):
        held[around(x, -d)] = ref[...]
    for h in range(HALF):
        decay = decay_of(rates_ref, core * HALF + h, LENGTH)
        state = held[h]
        beyond = decay * state + jnp.where(flag, keep_ref[h], recv_ref[h])
        out_ref[h] = jnp.where(flag, state, beyond)
        give_ref[h] = jnp.where(flag, beyond, state)


def small(kernel, name, reverse, rates, ins, outs, scratch):
    return call(
        functools.partial(kernel, reverse),
        name,
        [("vmem", rates)] + [("vmem", a) for a in ins],
        [("vmem", shape, F32) for shape in outs],
        [pltpu.VMEM(shape, F32) for shape in scratch],
    )


def states_of(own_ref, other_ref, state):
    core = core_of()
    state[pl.ds(core * HALF, HALF)] = own_ref[...].astype(BF16)
    state[pl.ds((1 - core) * HALF, HALF)] = other_ref[...].astype(BF16)


def half_outputs(rates_ref, q_ref, u_ref, gain_ref, state_ref, loc, first_head, o_ref, sq, dt, fresh):
    done = rows_of((LENGTH, SIZE), 1)
    for j in range(HALF):
        h = first_head + j
        decay_in = jnp.exp(-rate_of(rates_ref, h) * done)
        o_ref[j] = loc[h] + decay_in * dot(q_ref[h], state_ref[j].astype(BF16), NN)
    for r in range(0, LENGTH, 32):
        rows = pl.ds(r, 32)
        square, product = (None, None) if fresh else (sq[rows, :], dt[rows, :])
        for j in range(HALF):
            h = first_head + j
            out = o_ref[j, rows, :]
            scaled = gain_ref[pl.ds(h, 1), :] * u_ref[h, rows, :].astype(F32)
            square = out * out if square is None else square + out * out
            product = out * scaled if product is None else product + out * scaled
        sq[rows, :] = square
        dt[rows, :] = product


def own_output_kernel(rates_ref, q_ref, u_ref, gain_ref, state_ref, loc, o_ref, sq, dt):
    half_outputs(rates_ref, q_ref, u_ref, gain_ref, state_ref, loc, core_of() * HALF, o_ref, sq, dt, True)


def other_output_kernel(rates_ref, q_ref, u_ref, gain_ref, state_ref, loc, sq_ref, dt_ref, o_ref, sums_ref, sq, dt, sums):
    sq[...] = sq_ref[...]
    dt[...] = dt_ref[...]
    first_head = (1 - core_of()) * HALF
    half_outputs(rates_ref, q_ref, u_ref, gain_ref, state_ref, loc, first_head, o_ref, sq, dt, False)
    for b in range(4):
        rows = slice(b * 128, (b + 1) * 128)
        sums[b : b + 1, :] = jnp.sum(sq[rows, :].T, axis=0, keepdims=True)
        sums[4 + b : 5 + b, :] = jnp.sum(dt[rows, :].T, axis=0, keepdims=True)
    for i in range(sums_ref.shape[0]):
        sums_ref[i] = sums[...]


HALF_ROWS = (HALF, LENGTH, SIZE)


def own_outputs(rates, q, u, gain, state, loc):
    return call(
        own_output_kernel,
        "own_outputs",
        [("vmem", a) for a in (rates, q, u, gain, state, loc)],
        [("vmem", HALF_ROWS, F32), ("vmem", (LENGTH, SIZE), F32), ("vmem", (LENGTH, SIZE), F32)],
        flops=10**9,
        moved=4 * 2**20,
    )


def other_outputs(rates, q, u, gain, state, loc, sq, dt, peers):
    total = pltpu.VMEM((LENGTH, SIZE), F32)
    return call(
        other_output_kernel,
        "other_outputs",
        [("vmem", a) for a in (rates, q, u, gain, state, loc, sq, dt)],
        [("vmem", HALF_ROWS, F32), ("vmem", (peers, 8, SIZE), F32)],
        [total, total, pltpu.VMEM((8, SIZE), F32)],
    )


def half_grads(sums_ref, wq_ref, u_ref, gain_ref, o_ref, side, g, s):
    peers = sums_ref.shape[0]
    features = float(peers * HEADS * SIZE)
    sums = sums_ref[0]
    for i in range(1, peers):
        sums = sums + sums_ref[i]
    root = lax.rsqrt(sums[0:4, :] * (1.0 / features) + 1e-06)
    factor = root * root * root * sums[4:8, :] * (1.0 / features)
    for b in range(4):
        rows = pl.ds(b * 128, 128)
        inv = jnp.broadcast_to(root[b : b + 1, :], (128, 128)).T
        coef = jnp.broadcast_to(factor[b : b + 1, :], (128, 128)).T
        for j in range(HALF):
            h = side * HALF + j
            scaled = gain_ref[pl.ds(h, 1), :] * u_ref[h, rows, :].astype(F32)
            g[h, rows, :] = (inv * scaled - o_ref[j, rows, :] * coef).astype(BF16)
    for j in range(HALF):
        h = side * HALF + j
        s[j] = dot(wq_ref[h], g[h], NN)


def send_grad_kernel(sums_ref, wq_ref, u_ref, gain_ref, o_ref, g, s):
    half_grads(sums_ref, wq_ref, u_ref, gain_ref, o_ref, 1 - core_of(), g, s)


def keep_grad_kernel(sums_ref, wq_ref, u_ref, gain_ref, o_ref, g_in, g, s):
    half_grads(sums_ref, wq_ref, u_ref, gain_ref, o_ref, core_of(), g, s)


def send_grads(sums, wq, u, gain, other):
    return call(
        send_grad_kernel,
        "send_grads",
        [("vmem", a) for a in (sums, wq, u, gain, other)],
        [("vmem", ROWS, BF16), ("vmem", HALF_STATE, F32)],
    )


def keep_grads(sums, wq, u, gain, own, g):
    return call(
        keep_grad_kernel,
        "keep_grads",
        [("vmem", a) for a in (sums, wq, u, gain, own, g)],
        [("vmem", ROWS, BF16), ("vmem", HALF_STATE, F32)],
        flops=10**9,
        moved=4 * 2**20,
        aliases={5: 0},
    )


def query_kernel(rates_ref, g_ref, k_ref, v_ref, own_ref, other_ref, out_hbm, state, wide, block, sems):
    states_of(own_ref, other_ref, state)
    done = rows_of((LENGTH, SIZE), 1)
    for h in range(HEADS):
        rate = rate_of(rates_ref, h)
        diag, off = masks(rate)
        g0, g1 = g_ref[h, :256], g_ref[h, 256:]
        k0, k1 = k_ref[h, :256], k_ref[h, 256:]
        v0, v1 = v_ref[h, :256], v_ref[h, 256:]
        b00 = (dot(g0, v0, NT) * diag).astype(BF16)
        b10 = (dot(g1, v0, NT) * off).astype(BF16)
        b11 = (dot(g1, v1, NT) * diag).astype(BF16)
        carried = jnp.exp(-rate * done) * dot(g_ref[h], state[h], NT)
        wide[pl.ds(h, 256, stride=HEADS), :] = dot(b00, k0, NN) + carried[:256]
        wide[pl.ds(h + 256 * HEADS, 256, stride=HEADS), :] = (
            dot(b10, k0, NN) + dot(b11, k1, NN) + carried[256:]
        )
    copies = []
    for p in range(PARTS):
        rows = pl.ds(p * CHUNK, CHUNK)
        block[rows] = wide[pl.ds(p * CHUNK * HEADS, CHUNK * HEADS), :].reshape(CHUNK, HEADS, SIZE).astype(BF16)
        copies.append(put(block, out_hbm, rows, sems.at[p]))
    wait_all(copies)


def grad_query(rates, g, k, v, own, other):
    (out,) = call(
        query_kernel,
        "grad_query",
        [("vmem", rates), ("vmem", g), ("vmem", k), ("vmem", v), ("vmem", own), ("vmem", other)],
        [("hbm", WHOLE, BF16)],
        [
            pltpu.VMEM((HEADS, SIZE, SIZE), BF16),
            pltpu.VMEM((LENGTH * HEADS, SIZE), F32),
            pltpu.VMEM(WHOLE, BF16),
            dma(PARTS),
        ],
        flops=3 * 10**9,
        moved=5 * 2**20,
    )
    return out


def back_kernel(rates_ref, a_ref, b_ref, c_ref, out_ref):
    for h in range(HEADS):
        diag, off = masks(rate_of(rates_ref, h), True)
        a0, a1 = a_ref[h, :256], a_ref[h, 256:]
        b0, b1 = b_ref[h, :256], b_ref[h, 256:]
        c0, c1 = c_ref[h, :256], c_ref[h, 256:]
        t00 = (dot(a0, b0, NT) * diag).astype(BF16)
        t01 = (dot(a0, b1, NT) * off).astype(BF16)
        t11 = (dot(a1, b1, NT) * diag).astype(BF16)
        out_ref[h, :256] = (dot(t00, c0, NN) + dot(t01, c1, NN)).astype(BF16)
        out_ref[h, 256:] = dot(t11, c1, NN).astype(BF16)


def back(rates, a, b, c, name):
    (out,) = call(
        back_kernel,
        name,
        [("vmem", rates), ("vmem", a), ("vmem", b), ("vmem", c)],
        [("vmem", ROWS, BF16)],
        flops=2 * 10**9,
        moved=5 * 2**20,
    )
    return out


def half_finish(rates_ref, k, v, kl_ref, vl_ref, state_ref, first_head, wk, wv):
    left = LENGTH - rows_of((LENGTH, SIZE))
    for x, add, wide, dims in ((v, kl_ref, wk, NT), (k, vl_ref, wv, NN)):
        for j in range(HALF):
            h = first_head + j
            moved = jnp.exp(-rate_of(rates_ref, h) * left) * dot(x[h], state_ref[j].astype(BF16), dims)
            wide[pl.ds(h, LENGTH, stride=HEADS), :] = add[h].astype(F32) + moved
        yield


def own_finish_kernel(rates_ref, k, v, kl_ref, vl_ref, state_ref, wk, wv):
    def form(core):
        for _ in half_finish(rates_ref, k, v, kl_ref, vl_ref, state_ref, core * HALF, wk, wv):
            pass

    by_core(form)


def other_finish_kernel(rates_ref, k, v, kl_ref, vl_ref, state_ref, wk_in, wv_in, gk_hbm, gv_hbm, wk, wv, gk, gv, sems):
    sides = ((wk, gk, gk_hbm), (wv, gv, gv_hbm))

    def form(core):
        writes = []
        halves = half_finish(rates_ref, k, v, kl_ref, vl_ref, state_ref, (1 - core) * HALF, wk, wv)
        for _ in halves:
            pass
        for p in range(PARTS):
            rows = pl.ds(p * CHUNK, CHUNK)
            flat = pl.ds(p * CHUNK * HEADS, CHUNK * HEADS)
            for n, (wide, out, to) in enumerate(sides):
                out[rows] = wide[flat, :].reshape(CHUNK, HEADS, SIZE).astype(BF16)
                writes.append(put(out, to, rows, sems.at[PARTS * n + p]))
        wait_all(writes)

    by_core(form)


def own_finish(rates, k, v, kl, vl, state):
    return call(
        own_finish_kernel,
        "own_finish",
        [("vmem", a) for a in (rates, k, v, kl, vl, state)],
        [("vmem", WIDE, F32), ("vmem", WIDE, F32)],
        flops=10**9,
        moved=8 * 2**20,
    )


def other_finish(rates, k, v, kl, vl, state, wk, wv):
    block = pltpu.VMEM(WHOLE, BF16)
    return call(
        other_finish_kernel,
        "other_finish",
        [("vmem", a) for a in (rates, k, v, kl, vl, state, wk, wv)],
        [("hbm", WHOLE, BF16), ("hbm", WHOLE, BF16), ("vmem", WIDE, F32), ("vmem", WIDE, F32)],
        [block, block, dma(2 * PARTS)],
        aliases={6: 2, 7: 3},
    )[:2]


def permute(a, dy, dx, dc):
    pairs = []
    for y in range(RING):
        for x in range(RING):
            for c in range(2):
                to = ((y + dy) % RING * RING + (x + dx) % RING) * 2 + (c ^ dc)
                pairs.append(((y * RING + x) * 2 + c, to))
    return lax.ppermute(a, "ctx", pairs)


def exchange(a):
    return permute(a, 0, 0, 1)


def along_x(parts):
    return [permute(a, 0, d + 1, 0) for d, a in enumerate(parts)]


def along_y(a):
    return [permute(a, d, 0, 0) for d in (1, 2, 3)]


def beside(moved, work):
    out = lax.optimization_barrier((tuple(moved), tuple(work)))
    return list(out[0]), list(out[1])


def scan(rates, keep, send, reverse, first, second, third, last):
    recv = exchange(send)
    recv, (keep, *done0) = lax.optimization_barrier((recv, keep()))
    one = [ONE] * 4
    own, *parts = small(total_kernel, "chip_total", reverse, rates, [keep, recv], one, [HALF_STATE])
    moved = along_x(parts)
    moved, done1 = beside(moved, first(*done0))
    row, part = small(row_kernel, "row_sum", reverse, rates, [own, *moved], [ONE, HALF_STATE], [HALF_STATE])
    moved = along_y(row)
    moved, done2 = beside(moved, second(done1))
    own, *parts = small(
        column_kernel, "column_sum", reverse, rates, [row, *moved, part], one, [HALF_STATE, HALF_STATE]
    )
    moved = along_x(parts)
    moved, done3 = beside(moved, third(done1, done2))
    mine, give = small(
        after_kernel, "after", reverse, rates, [own, *moved, keep, recv], [HALF_STATE] * 2, [HALF_STATE]
    )
    (other,), done4 = beside([exchange(give)], last(mine, *done0, done1, done2, done3))
    return mine, other, done0, done1, done2, done3, done4


def on_device(queries, key_rows, value_rows, upstream, norm_gain, slope_index):
    send, kw, vw, rates = send_states(slope_index, key_rows, value_rows)
    e_own, e_other, _, (kh, qh), (vh, uh, wq), (loc,), (out_own, sq, dt) = scan(
        rates,
        lambda: [keep_states(rates, kw, vw)],
        send,
        False,
        lambda: turn(rates, kw, queries),
        lambda a: turn(rates, vw, upstream, a[1]),
        lambda a, b: [local_part(rates, a[1], a[0], b[0])],
        lambda e, a, b, c: own_outputs(rates, a[1], b[1], norm_gain, e, c[0]),
    )

    peers = lax.axis_size("head")
    out_other, sums = other_outputs(rates, qh, uh, norm_gain, e_other, loc, sq, dt, peers)
    sums = lax.all_to_all(sums, "head", 0, 0, tiled=True)
    g_part, send = send_grads(sums, wq, uh, norm_gain, out_other)

    def keep_part():
        g, keep = keep_grads(sums, wq, uh, norm_gain, out_own, g_part)
        return [keep, g]

    l_own, l_other, _, (gv_local, _), (gk_local,), (gq,), (wk, wv) = scan(
        rates,
        keep_part,
        send,
        True,
        lambda g: [back(rates, kh, qh, g, "gv_local"), g],
        lambda a: [back(rates, vh, a[1], qh, "gk_local")],
        lambda a, b: [grad_query(rates, a[1], kh, vh, e_own, e_other)],
        lambda l, g, a, b, c: own_finish(rates, kh, vh, b[0], a[0], l),
    )
    gk, gv = other_finish(rates, kh, vh, gk_local, gv_local, l_other, wk, wv)
    return gq, gk, gv


def solution(mesh):
    rows = P("ctx", "head", None)
    return jax.shard_map(
        on_device,
        mesh=mesh,
        in_specs=(rows, rows, rows, rows, P("head", None), P("head")),
        out_specs=(rows, rows, rows),
        check_vma=False,
    )
```
